32 devices in a mesh: dp: 8 (over z, x), ctx: 4 (over y, core).
Axes of the slice: x: 2, y: 2, z: 4, core: 2. Of those that a mesh axis runs over, the one named last changes fastest.
Arguments:
- patches: bfloat16 [1024, 5120], P('dp'), may hold values from -6 to 6
- vit_gain: float32 [1280], replicated, may hold values from 0.1 to 1.9
- merge_up: bfloat16 [5120, 3072], P(None, 'ctx'), may hold values from -0.078125 to 0.078125
- merge_down: bfloat16 [3072, 8192], P('ctx'), may hold values from -0.109375 to 0.109375
- dest: int32 [1024], P(('dp', 'ctx')), may hold values from 0 to 4095, as said below
- text: bfloat16 [8, 512, 8192], P('dp', 'ctx'), may hold values from -6 to 6
- norm_gain: float32 [8192], replicated, may hold values from 0.5 to 1.5
- kv_weight: bfloat16 [8192, 1024], P(('dp', 'ctx')), may hold values from -0.0625 to 0.0625
- queries: bfloat16 [8, 512, 4096], P('dp', 'ctx'), may hold values from -256 to 256
- out_grad: bfloat16 [8, 512, 4096], P('dp', 'ctx'), may hold values from -6 to 6
- assign: int32 [8], replicated, may hold values from 0 to 7, each once
- docs: int32 [8, 512], P('dp'), may hold values from 0 to 3, never falling along the last dimension, each value on 1 to 256 neighbouring positions
Outputs:
- attn_out: bfloat16 [8, 512, 4096], P('dp', 'ctx')
- q_grad: bfloat16 [8, 512, 4096], P('dp', 'ctx')
- hidden_grad: bfloat16 [8, 512, 8192], P('dp', 'ctx')
- visual_grad: bfloat16 [1024, 8192], P(('dp', 'ctx'))
The draws below stay inside these ranges and needn't reach their ends.
Inputs may be any that keep to these rules, and one draw needn't show every extreme that they name: `dest`: all entries are distinct. The 32 entries held by one device name rows of 32 devices' blocks of 128 rows per device (row // 128 names the device), each such device named by exactly one entry of the holding device. Every device's block receives exactly 32 entries, which fill one run of consecutive rows, in the order of the entries' index within their holding device.
All inputs are finite; a program needn't handle non-finite values.
Results may differ from the reference program's by a relative error of at most 0.035.
Values may be sent and summed in bfloat16 or wider, within the bound.
No kernel may reach another device: no remote copies, remote signals or barrier semaphores. Data moves between devices by JAX's collectives and lax.ppermute only.
A program may use at most 192 MiB of HBM per device.

```python
import math
import jax
import jax.numpy as jnp
import numpy as np
from jax import lax

D = 8192
VW = 1280
MH = 3072
HEADS = 32
KVH = 4
HD = 128
DOCS = 4
TOK_DEV = 128
VTOK_DEV = 32
SEQS = 8
LEN = 512
VIS = 1024
CAP = 1
N_DP = 8
N_CTX = 4


def draw_dest(key, part):
    splits = jax.random.split(jax.random.fold_in(key, 11), 4)
    device_total = N_DP * N_CTX
    group_total = VTOK_DEV // CAP
    relabel = jax.random.permutation(splits[0], device_total)
    shuffle = jax.random.permutation(splits[1], device_total)
    offsets = jax.random.permutation(splits[2], device_total)[:group_total]
    starts = jax.random.randint(splits[3], (device_total,), 0, TOK_DEV - VTOK_DEV + 1)
    source = jnp.arange(device_total, dtype=jnp.int32)[:, None]
    token_index = jnp.arange(VTOK_DEV, dtype=jnp.int32)[None, :]
    target = relabel[(shuffle[source] + offsets[token_index // CAP]) % device_total]
    row_index = starts[target] + token_index
    return (target * TOK_DEV + row_index).reshape(VIS).astype(jnp.int32)


def draw_queries(key, part):
    base_key = jax.random.fold_in(jax.random.fold_in(key, 23), 0)
    values = jax.random.normal(base_key, (SEQS, LEN, HEADS * HD), jnp.float32)
    return jnp.clip(values, -256.0, 256.0).astype(jnp.bfloat16)


def steps_of(key, dims, cuts, smallest, largest):
    factor_of = 1.0
    for axis_at, parts in cuts:
        heights = jax.random.uniform(jax.random.fold_in(jax.random.fold_in(key, 6), axis_at), (parts,), jnp.float32, smallest / len(cuts), largest / len(cuts))
        factor_of = factor_of * jnp.repeat(jnp.exp(heights), dims[axis_at] // parts).reshape((-1,) + (1,) * (len(dims) - 1 - axis_at))
    return factor_of


def length_profile(amount, total, bound, skew):
    portions = [(1 << 20) // math.isqrt(rank ** skew) + 1 for rank in range(2, amount + 1)]
    surplus, given = total - bound - (amount - 1), [1] * (amount - 1)
    while surplus > 0:
        movable = [i for i in range(amount - 1) if given[i] < bound]
        whole, remaining = sum([portions[i] for i in movable]), surplus
        for i in movable:
            more = min(bound - given[i], max(1, remaining * portions[i] // whole), surplus)
            given[i] = given[i] + more
            surplus = surplus - more
    return np.array([bound] + given)


def ragged(rng, amount, total, bound, slope):
    if amount == 2:
        one = jax.random.randint(rng, (), max(1, total - bound), min(bound, total - 1) + 1)
        return jnp.stack([one, total - one])
    lengths = jnp.asarray(length_profile(amount, total, bound, slope), jnp.int32)
    pairs = (amount - 1) // 2
    source_of, sink = lengths[1:1 + 2 * pairs:2], lengths[2:2 + 2 * pairs:2]
    slack = jnp.minimum(source_of - 1, bound - sink)
    shifted = jax.random.randint(jax.random.fold_in(rng, 1), (pairs,), 0, 1 << 20) % (slack + 1)
    lengths = lengths.at[1:1 + 2 * pairs:2].set(source_of - shifted).at[2:2 + 2 * pairs:2].set(sink + shifted)
    return lengths[jax.random.permutation(jax.random.fold_in(rng, 2), amount)]


def normal_values(rng, shape, deviation, most, shards=(), held_as=jnp.bfloat16):
    array = jax.random.normal(rng, shape, jnp.float32) * deviation
    if len(shards) > 0:
        array = steps_of(rng, shape, shards, -0.22, 0.18) * array
    return jnp.clip(array, min=-most, max=most).astype(held_as)


def setup_inputs(seed: int = 0) -> dict:
    keys = jax.random.split(jax.random.key(seed), 13)
    patches = normal_values(keys[0], (VIS, 4 * VW), 1.0, 6.0, ((0, 8),))
    vit_gain = jnp.clip(1.0 + 0.18 * jax.random.normal(keys[1], (VW,), jnp.float32), 0.1, 1.9)
    merge_up = normal_values(keys[2], (4 * VW, MH), (4 * VW) ** -0.5, 0.078125, ((1, 4),))
    merge_down = normal_values(keys[3], (MH, D), MH ** -0.5, 0.109375, ((0, 4),))
    dest = draw_dest(jax.random.fold_in(keys[12], 71), 0)
    text = normal_values(keys[5], (SEQS, LEN, D), 1.0, 6.0, ((0, 8), (1, 4)))
    norm_gain = jnp.clip(1.0 + 0.1 * jax.random.normal(keys[6], (D,), jnp.float32), 0.5, 1.5)
    kv_weight = normal_values(keys[7], (D, 2 * KVH * HD), D ** -0.5, 0.0625, ((0, 32),))
    queries = draw_queries(jax.random.fold_in(keys[12], 71), 0)
    out_grad = normal_values(keys[9], (SEQS, LEN, HEADS * HD), 1.0, 6.0, ((0, 8), (1, 4)))
    assign = jax.random.permutation(keys[10], 2 * N_CTX).astype(jnp.int32)
    docs = jax.vmap(lambda own: jnp.searchsorted(jnp.cumsum(ragged(own, DOCS, LEN, LEN // 2, 2)), jnp.arange(LEN), side="right"))(jax.random.split(keys[11], SEQS)).reshape((SEQS, LEN)).astype(jnp.int32)
    return {"patches": patches, "vit_gain": vit_gain, "merge_up": merge_up, "merge_down": merge_down, "dest": dest, "text": text, "norm_gain": norm_gain, "kv_weight": kv_weight, "queries": queries, "out_grad": out_grad, "assign": assign, "docs": docs}


epsilon = 1e-06

def rounded(values):
    return lax.optimization_barrier(values.astype(jnp.bfloat16)).astype(jnp.float32)

def merger_norm(patches, vit_gain):
    pieces = patches.astype(jnp.float32).reshape(patches.shape[0], 4, vit_gain.shape[0])
    center = pieces - lax.optimization_barrier(jnp.mean(pieces, axis=-1, keepdims=True))
    spread = lax.optimization_barrier(jnp.mean(center * center, axis=-1, keepdims=True))
    scaled = center * lax.rsqrt(spread + epsilon) * vit_gain.astype(jnp.float32)
    return scaled.reshape(patches.shape[0], -1).astype(jnp.bfloat16)

def rms_scale(hidden32, norm_gain):
    square = lax.optimization_barrier(jnp.mean(hidden32 * hidden32, axis=-1, keepdims=True))
    return hidden32 * lax.rsqrt(square + epsilon) * norm_gain.astype(jnp.float32)

def attend_exact(query_rows, pair_rows, upstream_rows, query_pos, query_doc, key_pos, key_doc):
    row_count = query_rows.shape[0]
    key_count = pair_rows.shape[0]
    group_size = HEADS // KVH
    score_scale = HD ** (-0.5)
    query_heads = query_rows.astype(jnp.float32).reshape(row_count, KVH, group_size, HD)
    key_heads = pair_rows[:, :KVH * HD].astype(jnp.float32).reshape(key_count, KVH, HD)
    value_heads = pair_rows[:, KVH * HD:].astype(jnp.float32).reshape(key_count, KVH, HD)
    scores = jnp.einsum('qhgd,khd->hgqk', query_heads, key_heads) * score_scale
    allowed = (key_pos[None, :] <= query_pos[:, None]) & (key_doc[None, :] == query_doc[:, None])
    scores = jnp.where(allowed, scores, -jnp.inf)
    weights = jnp.exp(scores - lax.optimization_barrier(jnp.max(scores, axis=-1, keepdims=True)))
    weights = weights / lax.optimization_barrier(jnp.sum(weights, axis=-1, keepdims=True))
    light_weights = rounded(weights)
    output = jnp.einsum('hgqk,khd->qhgd', light_weights, value_heads).reshape(row_count, HEADS * HD)
    upstream = upstream_rows.astype(jnp.float32).reshape(row_count, KVH, group_size, HD)
    value_grad = jnp.einsum('hgqk,qhgd->khd', light_weights, upstream).reshape(key_count, KVH * HD)
    weight_grad = jnp.einsum('qhgd,khd->hgqk', upstream, value_heads)
    inner_sum = lax.optimization_barrier(jnp.sum(weights * weight_grad, axis=-1, keepdims=True))
    score_grad = rounded(weights * (weight_grad - inner_sum) * score_scale)
    query_grad = jnp.einsum('hgqk,khd->qhgd', score_grad, key_heads).reshape(row_count, HEADS * HD)
    key_grad = jnp.einsum('hgqk,qhgd->khd', score_grad, query_heads).reshape(key_count, KVH * HD)
    return (output.astype(jnp.bfloat16), query_grad.astype(jnp.bfloat16), key_grad, value_grad)

def reference(patches, vit_gain, merge_up, merge_down, dest, text, norm_gain, kv_weight, queries, out_grad, assign, docs):
    normed = merger_norm(patches, vit_gain)
    inner_hidden = jax.nn.gelu(jnp.dot(normed, merge_up, preferred_element_type=jnp.float32), approximate=False).astype(jnp.bfloat16)
    slice_width = MH // N_CTX
    running = jnp.zeros((VIS, D), jnp.float32)
    for group_number in range(N_CTX):
        offset = group_number * slice_width
        partial_sum = jnp.dot(inner_hidden[:, offset:offset + slice_width], merge_down[offset:offset + slice_width], preferred_element_type=jnp.float32)
        running = running + rounded(partial_sum)
    visual = running.astype(jnp.bfloat16)
    flattened = text.reshape(SEQS * LEN, D).at[dest].set(visual)
    marked = jnp.zeros((SEQS * LEN,), jnp.bool_).at[dest].set(True)
    hidden32 = flattened.astype(jnp.float32)
    normed_hidden = rms_scale(hidden32, norm_gain).astype(jnp.bfloat16)
    pairs = jnp.dot(normed_hidden, kv_weight, preferred_element_type=jnp.float32).astype(jnp.bfloat16)
    pairs = pairs.reshape(SEQS, LEN, 2 * KVH * HD)
    halves = TOK_DEV // 2
    positions = (assign[:, None] * halves + jnp.arange(halves, dtype=jnp.int32)[None, :]).reshape(LEN).astype(jnp.int32)

    def one_sequence(operands):
        query_rows, pair_rows, upstream_rows, doc_row = operands
        labels = doc_row.reshape(-1, halves)[assign].reshape(LEN)
        return attend_exact(query_rows, pair_rows, upstream_rows, positions, labels, positions, labels)
    attn_out, q_grad, key_grad, value_grad = lax.map(one_sequence, (queries, pairs, out_grad, docs))
    pair_grad = jnp.concatenate([key_grad, value_grad], axis=-1).reshape(SEQS * LEN, 2 * KVH * HD).astype(jnp.bfloat16)
    normed_grad = jnp.dot(pair_grad, kv_weight.T, preferred_element_type=jnp.float32)
    forward_value, pullback = jax.vjp(lambda values: rms_scale(values, norm_gain), hidden32)
    full_grad = pullback(normed_grad)[0]
    hidden_grad = jnp.where(marked[:, None], jnp.float32(0.0), full_grad).astype(jnp.bfloat16).reshape(SEQS, LEN, D)
    visual_grad = full_grad[dest].astype(jnp.bfloat16)
    return (attn_out, q_grad, hidden_grad, visual_grad)
```

```python
import jax
import jax.numpy as jnp
from jax import lax
from jax.experimental import pallas as pl
from jax.experimental.pallas import tpu as pltpu
from jax.sharding import Mesh
from jax.sharding import PartitionSpec as P

HEADS = 32
KVH = 4
HD = 128


epsilon = 1e-06


def merger_norm(patches, vit_gain):
    pieces = patches.astype(jnp.float32).reshape(patches.shape[0], 4, vit_gain.shape[0])
    center = pieces - jnp.mean(pieces, axis=-1, keepdims=True)
    spread = jnp.mean(center * center, axis=-1, keepdims=True)
    scaled = center * lax.rsqrt(spread + epsilon) * vit_gain
    return scaled.reshape(patches.shape[0], -1).astype(jnp.bfloat16)


def rms_scale(hidden32, norm_gain):
    square = jnp.mean(hidden32 * hidden32, axis=-1, keepdims=True)
    return hidden32 * lax.rsqrt(square + epsilon) * norm_gain


def attend(query_rows, pair_rows, upstream_rows, query_pos, query_doc, key_pos, key_doc):
    row_count = query_rows.shape[0]
    key_count = pair_rows.shape[0]
    group_size = HEADS // KVH
    score_scale = HD ** (-0.5)
    query_heads = query_rows.reshape(row_count, KVH, group_size, HD)
    key_heads = pair_rows[:, : KVH * HD].reshape(key_count, KVH, HD)
    value_heads = pair_rows[:, KVH * HD :].reshape(key_count, KVH, HD)
    scores = (
        jnp.einsum("qhgd,khd->hgqk", query_heads, key_heads, preferred_element_type=jnp.float32)
        * score_scale
    )
    allowed = (key_pos[None, :] <= query_pos[:, None]) & (key_doc[None, :] == query_doc[:, None])
    scores = jnp.where(allowed, scores, -jnp.inf)
    weights = jnp.exp(scores - jnp.max(scores, axis=-1, keepdims=True))
    weights = weights / jnp.sum(weights, axis=-1, keepdims=True)
    light_weights = weights.astype(jnp.bfloat16)
    output = jnp.einsum(
        "hgqk,khd->qhgd", light_weights, value_heads, preferred_element_type=jnp.float32
    )
    upstream = upstream_rows.reshape(row_count, KVH, group_size, HD)
    value_grad = jnp.einsum(
        "hgqk,qhgd->khd", light_weights, upstream, preferred_element_type=jnp.float32
    )
    weight_grad = jnp.einsum(
        "qhgd,khd->hgqk", upstream, value_heads, preferred_element_type=jnp.float32
    )
    inner_sum = jnp.sum(weights * weight_grad, axis=-1, keepdims=True)
    score_grad = (weights * (weight_grad - inner_sum) * score_scale).astype(jnp.bfloat16)
    query_grad = jnp.einsum(
        "hgqk,khd->qhgd", score_grad, key_heads, preferred_element_type=jnp.float32
    )
    key_grad = jnp.einsum(
        "hgqk,qhgd->khd", score_grad, query_heads, preferred_element_type=jnp.float32
    )
    output = output.reshape(row_count, HEADS * HD).astype(jnp.bfloat16)
    query_grad = query_grad.reshape(row_count, HEADS * HD).astype(jnp.bfloat16)
    return (
        output,
        query_grad,
        key_grad.reshape(key_count, KVH * HD),
        value_grad.reshape(key_count, KVH * HD),
    )


def local(
    patches,
    vit_gain,
    merge_up,
    merge_down,
    dest,
    text,
    norm_gain,
    kv_weight,
    queries,
    out_grad,
    assign,
    docs,
):
    ctx_count = lax.axis_size("ctx")
    data_count = lax.axis_size("dp")
    device_count = ctx_count * data_count
    token_rows = text.shape[1]
    visual_rows = dest.shape[0]
    capacity = max(1, visual_rows // device_count)
    slot_total = device_count * capacity
    normed = merger_norm(patches, vit_gain)
    inner_hidden = jax.nn.gelu(
        jnp.dot(normed, merge_up, preferred_element_type=jnp.float32), approximate=False
    ).astype(jnp.bfloat16)
    visual = lax.psum_scatter(
        jnp.dot(inner_hidden, merge_down, preferred_element_type=jnp.float32).astype(jnp.bfloat16),
        "ctx",
        scatter_dimension=0,
        tiled=True,
    )
    target = dest // token_rows
    local_row = dest % token_rows
    token_order = jnp.arange(visual_rows, dtype=jnp.int32)
    before = (target[:, None] == target[None, :]) & (token_order[None, :] < token_order[:, None])
    slot_index = target * capacity + jnp.sum(before.astype(jnp.int32), axis=1)
    picking = jnp.arange(slot_total, dtype=jnp.int32)[:, None] == slot_index[None, :]
    outgoing = jnp.dot(
        picking.astype(jnp.bfloat16), visual, preferred_element_type=jnp.float32
    ).astype(jnp.bfloat16)
    outgoing_rows = jnp.sum(jnp.where(picking, local_row[None, :] + 1, 0), axis=1) - 1
    arrived, arrived_rows = (
        lax.all_to_all(outgoing, ("dp", "ctx"), split_axis=0, concat_axis=0, tiled=True),
        lax.all_to_all(outgoing_rows, ("dp", "ctx"), split_axis=0, concat_axis=0, tiled=True),
    )
    placing = jnp.arange(token_rows, dtype=jnp.int32)[:, None] == arrived_rows[None, :]
    placed = jnp.dot(
        placing.astype(jnp.bfloat16), arrived, preferred_element_type=jnp.float32
    ).astype(jnp.bfloat16)
    marked = jnp.any(placing, axis=1)
    hidden = jnp.where(marked[:, None], placed, text[0])
    hidden32 = hidden.astype(jnp.float32)
    normed_hidden = rms_scale(hidden32, norm_gain).astype(jnp.bfloat16)
    projected = jnp.dot(
        normed_hidden,
        lax.all_gather(kv_weight, ("dp", "ctx"), axis=0, tiled=True),
        preferred_element_type=jnp.float32,
    )
    pairs_local = projected.astype(jnp.bfloat16)
    pairs_all = lax.all_gather(pairs_local, "ctx", axis=0, tiled=True)
    halves = token_rows // 2
    length = token_rows * ctx_count
    positions = (assign[:, None] * halves + jnp.arange(halves, dtype=jnp.int32)[None, :]).reshape(
        length
    )
    labels = docs[0].reshape(-1, halves)[assign].reshape(length)
    own_start = lax.axis_index("ctx") * token_rows
    query_pos = lax.dynamic_slice_in_dim(positions, own_start, token_rows, 0)
    query_doc = lax.dynamic_slice_in_dim(labels, own_start, token_rows, 0)
    attention, query_grad, key_grad, value_grad = attend(
        queries[0], pairs_all, out_grad[0], query_pos, query_doc, positions, labels
    )
    key_grad, value_grad = (
        lax.psum_scatter(
            key_grad.astype(jnp.bfloat16), "ctx", scatter_dimension=0, tiled=True
        ).astype(jnp.float32),
        lax.psum_scatter(
            value_grad.astype(jnp.bfloat16), "ctx", scatter_dimension=0, tiled=True
        ).astype(jnp.float32),
    )
    pair_grad = jnp.concatenate([key_grad, value_grad], axis=1).astype(jnp.bfloat16)
    contract = (((1,), (1,)), ((), ()))
    normed_grad = lax.dot_general(
        pair_grad,
        lax.all_gather(kv_weight, ("dp", "ctx"), axis=0, tiled=True),
        contract,
        preferred_element_type=jnp.float32,
    )
    forward_value, pullback = jax.vjp(lambda values: rms_scale(values, norm_gain), hidden32)
    full_grad = pullback(normed_grad)[0]
    hidden_grad = jnp.where(marked[:, None], jnp.float32(0.0), full_grad).astype(jnp.bfloat16)
    returning = jnp.dot(
        placing.T.astype(jnp.bfloat16),
        full_grad.astype(jnp.bfloat16),
        preferred_element_type=jnp.float32,
    ).astype(jnp.bfloat16)
    returned = lax.all_to_all(returning, ("dp", "ctx"), split_axis=0, concat_axis=0, tiled=True)
    visual_grad = jnp.dot(
        picking.T.astype(jnp.bfloat16), returned, preferred_element_type=jnp.float32
    ).astype(jnp.bfloat16)
    return (attention[None], query_grad[None], hidden_grad[None], visual_grad)


def neighbor(values, axis, offset):
    count = lax.axis_size(axis)
    return lax.ppermute(values, axis, [(d, d ^ offset) for d in range(count)])


def swap(values):
    return neighbor(values, "core", 1)


def vmem_params():
    return pltpu.CompilerParams(vmem_limit_bytes=56 * 1024 * 1024)


def smem():
    return pl.BlockSpec(memory_space=pltpu.SMEM)


def store_halves(core, values, own_ref, other_ref, block):
    def put(own_parity):
        for j in range(values.shape[1] // (2 * block)):
            even = values[:, 2 * j * block : (2 * j + 1) * block]
            odd = values[:, (2 * j + 1) * block : (2 * j + 2) * block]
            own_ref[:, j * block : (j + 1) * block] = odd if own_parity else even
            other_ref[:, j * block : (j + 1) * block] = even if own_parity else odd

    @pl.when(core == 0)
    def _():
        put(0)

    @pl.when(core != 0)
    def _():
        put(1)


def split_halves(values, core, block):
    rows, width = values.shape
    step = 8 * block

    def kernel(core_ref, value_ref, own_ref, other_ref):
        store_halves(core_ref[0], value_ref[...], own_ref, other_ref, block)

    half = jax.ShapeDtypeStruct((rows, width // 2), values.dtype)
    out = pl.BlockSpec((rows, step // 2), lambda j: (0, j))
    return pl.pallas_call(
        kernel,
        grid=(width // step,),
        in_specs=[smem(), pl.BlockSpec((rows, step), lambda j: (0, j))],
        out_specs=[out, out],
        out_shape=[half, half],
        compiler_params=vmem_params(),
        name="split_halves",
    )(core, values)


def down_halves(inner_hidden, merge_down, core, block):
    rows, depth = inner_hidden.shape
    width = merge_down.shape[1]
    step = 4 * block

    def kernel(core_ref, hidden_ref, weight_ref, own_ref, other_ref):
        product = jnp.dot(hidden_ref[...], weight_ref[...], preferred_element_type=jnp.float32)
        store_halves(core_ref[0], product.astype(jnp.bfloat16), own_ref, other_ref, block)

    half = jax.ShapeDtypeStruct((rows, width // 2), jnp.bfloat16)
    out = pl.BlockSpec((rows, step // 2), lambda j: (0, j))
    return pl.pallas_call(
        kernel,
        grid=(width // step,),
        in_specs=[
            smem(),
            pl.BlockSpec((rows, depth), lambda j: (0, 0)),
            pl.BlockSpec((depth, step), lambda j: (0, j)),
        ],
        out_specs=[out, out],
        out_shape=[half, half],
        compiler_params=vmem_params(),
        cost_estimate=pl.CostEstimate(
            flops=2 * rows * depth * width, bytes_accessed=2 * depth * width, transcendentals=0
        ),
        name="merge_down",
    )(core, inner_hidden, merge_down)


def project(table, own_rows, sibling_rows, visual, gain, blocks):
    rows = own_rows.shape[0]
    total = 2 * rows + visual.shape[0]
    block, width = blocks[0].shape
    quarter = width // 4
    count = len(blocks)

    def kernel(table_ref, own_ref, sibling_ref, visual_ref, gain_ref, *rest):
        block_refs = rest[:count]
        mine_ref, theirs_ref, buffers, total_ref, sems = rest[count:]
        copies = [
            pltpu.make_async_copy(block_refs[r], buffers.at[r], sems.at[r]) for r in range(count)
        ]
        for copy in copies:
            copy.start()
        for r in range(count):
            columns = pl.ds(pl.multiple_of(table_ref[r] * block, block), block)
            gains = gain_ref[:, columns]
            part = jnp.concatenate(
                [
                    (ref[:, columns].astype(jnp.float32) * gains).astype(jnp.bfloat16)
                    for ref in (own_ref, sibling_ref, visual_ref)
                ],
                axis=0,
            )
            copies[r].wait()
            product = jnp.dot(part, buffers[r], preferred_element_type=jnp.float32)
            if r == 0:
                total_ref[...] = product
            else:
                total_ref[...] += product

        def put(parity):
            for piece in range(2):
                start = 2 * piece * quarter
                mine = slice(start + parity * quarter, start + (parity + 1) * quarter)
                theirs = slice(start + (1 - parity) * quarter, start + (2 - parity) * quarter)
                place = slice(piece * quarter, (piece + 1) * quarter)
                mine_ref[:, place] = total_ref[:, mine]
                theirs_ref[:rows, place] = total_ref[rows : 2 * rows, theirs].astype(jnp.bfloat16)
                theirs_ref[rows : 2 * rows, place] = total_ref[:rows, theirs].astype(jnp.bfloat16)
                theirs_ref[2 * rows :, place] = total_ref[2 * rows :, theirs].astype(jnp.bfloat16)

        @pl.when(table_ref[count] == 0)
        def _():
            put(0)

        @pl.when(table_ref[count] != 0)
        def _():
            put(1)

    vmem = pl.BlockSpec(memory_space=pltpu.VMEM)
    return pl.pallas_call(
        kernel,
        in_specs=[smem()] + [vmem] * 4 + [pl.BlockSpec(memory_space=pl.ANY)] * count,
        out_specs=[vmem, vmem],
        out_shape=[
            jax.ShapeDtypeStruct((total, width // 2), jnp.float32),
            jax.ShapeDtypeStruct((total, width // 2), jnp.bfloat16),
        ],
        scratch_shapes=[
            pltpu.VMEM((count, block, width), jnp.bfloat16),
            pltpu.VMEM((total, width), jnp.float32),
            pltpu.SemaphoreType.DMA((count,)),
        ],
        compiler_params=vmem_params(),
        cost_estimate=pl.CostEstimate(
            flops=2 * total * count * block * width,
            bytes_accessed=2 * count * block * (width + total),
            transcendentals=0,
        ),
        name="project_pairs",
    )(table, own_rows, sibling_rows, visual, gain, *blocks)


def project_back(table, grads, sibling_grads, own_rows, sibling_rows, visual, gain, scale, back, keep, blocks):
    rows = own_rows.shape[0]
    tokens = visual.shape[0] // 2
    total = 2 * rows + 2 * tokens
    block, width = blocks[0].shape
    quarter = width // 4
    count = len(blocks)

    def kernel(
        table_ref, grad_ref, other_ref, own_ref, sibling_ref, visual_ref, gain_ref, scale_ref, back_ref, keep_ref, *rest
    ):
        block_refs = rest[:count]
        held_ref, sent_ref, buffers, pair_ref, sems = rest[count:]
        copies = [
            pltpu.make_async_copy(block_refs[r], buffers.at[r], sems.at[r]) for r in range(count)
        ]
        for copy in copies:
            copy.start()

        def gather(parity):
            for piece in range(2):
                place = slice(piece * quarter, (piece + 1) * quarter)
                start = (2 * piece + parity) * quarter
                pair_ref[:, start : start + quarter] = grad_ref[:, place]
                start = (2 * piece + 1 - parity) * quarter
                pair_ref[:, start : start + quarter] = other_ref[:, place]

        @pl.when(table_ref[count] == 0)
        def _():
            gather(0)

        @pl.when(table_ref[count] != 0)
        def _():
            gather(1)

        for r in range(count):
            columns = pl.ds(pl.multiple_of(table_ref[r] * block, block), block)
            copies[r].wait()
            normed_grad = lax.dot_general(
                pair_ref[...], buffers[r], (((1,), (1,)), ((), ())), preferred_element_type=jnp.float32
            )
            value = jnp.concatenate(
                [ref[:, columns].astype(jnp.float32) for ref in (own_ref, sibling_ref, visual_ref)],
                axis=0,
            )
            full = normed_grad * (scale_ref[...] * gain_ref[:, columns]) - value * back_ref[...]
            full = jnp.where(keep_ref[...] > 0, full, 0.0).astype(jnp.bfloat16)
            held_ref[:rows, columns] = full[:rows]
            sent_ref[:rows, columns] = full[rows : 2 * rows]
            first, second = full[2 * rows : 2 * rows + tokens], full[2 * rows + tokens :]

            @pl.when(table_ref[count] == 0)
            def _():
                held_ref[rows:, columns] = first
                sent_ref[rows:, columns] = second

            @pl.when(table_ref[count] != 0)
            def _():
                held_ref[rows:, columns] = second
                sent_ref[rows:, columns] = first

    vmem = pl.BlockSpec(memory_space=pltpu.VMEM)
    half = jax.ShapeDtypeStruct((rows + tokens, count * block), jnp.bfloat16)
    return pl.pallas_call(
        kernel,
        in_specs=[smem()] + [vmem] * 9 + [pl.BlockSpec(memory_space=pl.ANY)] * count,
        out_specs=[vmem, vmem],
        out_shape=[half, half],
        scratch_shapes=[
            pltpu.VMEM((count, block, width), jnp.bfloat16),
            pltpu.VMEM((total, width), jnp.bfloat16),
            pltpu.SemaphoreType.DMA((count,)),
        ],
        compiler_params=vmem_params(),
        cost_estimate=pl.CostEstimate(
            flops=2 * total * count * block * width,
            bytes_accessed=2 * count * block * (width + 2 * total),
            transcendentals=0,
        ),
        name="project_back",
    )(table, grads, sibling_grads, own_rows, sibling_rows, visual, gain, scale, back, keep, *blocks)


def join_halves(core, held, received, rows, block):
    total, half = held.shape
    step = 4 * block

    def kernel(core_ref, held_ref, received_ref, hidden_ref, visual_ref):
        def put(parity):
            for j in range(step // block):
                source = slice(j * block, (j + 1) * block)
                for ref, side in ((held_ref, parity), (received_ref, 1 - parity)):
                    place = slice((2 * j + side) * block, (2 * j + side + 1) * block)
                    hidden_ref[:, place] = ref[:rows, source]
                    visual_ref[:, place] = ref[rows:, source]

        @pl.when(core_ref[0] == 0)
        def _():
            put(0)

        @pl.when(core_ref[0] != 0)
        def _():
            put(1)

    part = pl.BlockSpec((total, step), lambda j: (0, j))
    return pl.pallas_call(
        kernel,
        grid=(half // step,),
        in_specs=[smem(), part, part],
        out_specs=[
            pl.BlockSpec((rows, 2 * step), lambda j: (0, j)),
            pl.BlockSpec((total - rows, 2 * step), lambda j: (0, j)),
        ],
        out_shape=[
            jax.ShapeDtypeStruct((rows, 2 * half), jnp.bfloat16),
            jax.ShapeDtypeStruct((total - rows, 2 * half), jnp.bfloat16),
        ],
        compiler_params=vmem_params(),
        name="join_halves",
    )(core, held, received)


def attend_pair(queries, upstream, pair_text, pair_visual, key_row, key_pos, key_doc, visual_row, query_pos, query_doc):
    rows, width = queries[0].shape
    length, pair_width = pair_text.shape
    slots = pair_visual.shape[0]
    own_kv = pair_width // (2 * HD)
    heads = width // HD
    group = heads // own_kv
    step_heads = max(1, group // 2)
    steps = heads // step_heads
    score_scale = HD ** (-0.5)
    f32, bf16 = jnp.float32, jnp.bfloat16

    def kernel(
        qa, qb, ua, ub, text_ref, visual_ref, row_s, row_l, pos_ref, doc_ref, slot_s, slot_l, qpos_ref, qdoc_ref,
        oa, ob, ga, gb, grad_ref, grad_visual_ref, keep_ref, heads_ref, turned_ref, bias_ref, total_ref,
    ):
        step = pl.program_id(0)

        @pl.when(step == 0)
        def _():
            hit = row_s[...] == slot_l[...]
            placing = jnp.where(hit, 1.0, 0.0).astype(f32)
            placed = jnp.dot(placing.astype(bf16), visual_ref[...], preferred_element_type=f32)
            marked = jnp.max(placing, axis=1, keepdims=True)
            keep_ref[...] = 1.0 - marked
            pairs = jnp.where(marked > 0, placed, text_ref[...].astype(f32))
            for j in range(2 * own_kv):
                piece = pairs[:, j * HD : (j + 1) * HD]
                heads_ref[j] = piece.astype(bf16)
                turned_ref[j] = piece.T.astype(bf16)
            allowed = (pos_ref[...] <= qpos_ref[...]) & (doc_ref[...] == qdoc_ref[...])
            bias_ref[...] = jnp.where(allowed, 0.0, -jnp.inf).astype(f32)
            total_ref[...] = jnp.zeros_like(total_ref)

        head = (step * step_heads) // group
        keys, values = heads_ref[head], heads_ref[own_kv + head]
        keys_turned, values_turned = turned_ref[head], turned_ref[own_kv + head]
        contract = (((1,), (1,)), ((), ()))
        for h in range(step_heads):
            lanes = slice(h * HD, (h + 1) * HD)
            query = jnp.concatenate([qa[:, lanes], qb[:, lanes]], axis=0)
            up = jnp.concatenate([ua[:, lanes], ub[:, lanes]], axis=0)
            scores = lax.dot_general(keys, query, contract, preferred_element_type=f32)
            scores = scores * score_scale + bias_ref[...]
            weights = jnp.exp(scores - jnp.max(scores, axis=0, keepdims=True))
            weights = weights * (1.0 / jnp.sum(weights, axis=0, keepdims=True))
            light = weights.astype(bf16)
            output = jnp.dot(values_turned, light, preferred_element_type=f32).T.astype(bf16)
            oa[:, lanes] = output[:rows]
            ob[:, lanes] = output[rows:]
            total_ref[own_kv + head] += jnp.dot(light, up, preferred_element_type=f32)
            weight_grad = lax.dot_general(values, up, contract, preferred_element_type=f32)
            inner = jnp.sum(weights * weight_grad, axis=0, keepdims=True)
            score_grad = (weights * (weight_grad - inner) * score_scale).astype(bf16)
            query_grad = jnp.dot(keys_turned, score_grad, preferred_element_type=f32).T.astype(bf16)
            ga[:, lanes] = query_grad[:rows]
            gb[:, lanes] = query_grad[rows:]
            total_ref[head] += jnp.dot(score_grad, query, preferred_element_type=f32)

        @pl.when(step == steps - 1)
        def _():
            lifting = jnp.where(slot_s[...] == row_l[...], 1.0, 0.0).astype(bf16)
            for j in range(2 * own_kv):
                piece = total_ref[j].astype(bf16)
                place = slice(j * HD, (j + 1) * HD)
                grad_ref[:, place] = piece
                grad_visual_ref[:, place] = jnp.dot(lifting, piece, preferred_element_type=f32).astype(bf16)

    part = pl.BlockSpec((rows, step_heads * HD), lambda j: (0, j))
    vmem = pl.BlockSpec(memory_space=pltpu.VMEM)
    shape = jax.ShapeDtypeStruct
    return pl.pallas_call(
        kernel,
        grid=(steps,),
        in_specs=[part] * 4 + [vmem] * 10,
        out_specs=[part] * 4 + [vmem] * 3,
        out_shape=[shape((rows, width), bf16)] * 4
        + [shape((length, pair_width), bf16), shape((slots, pair_width), bf16), shape((length, 1), f32)],
        scratch_shapes=[
            pltpu.VMEM((2 * own_kv, length, HD), bf16),
            pltpu.VMEM((2 * own_kv, HD, length), bf16),
            pltpu.VMEM((length, 2 * rows), f32),
            pltpu.VMEM((2 * own_kv, length, HD), f32),
        ],
        compiler_params=vmem_params(),
        cost_estimate=pl.CostEstimate(
            flops=20 * rows * length * width,
            bytes_accessed=16 * rows * width,
            transcendentals=2 * heads * rows * length,
        ),
        name="attend",
    )(
        *queries,
        *upstream,
        pair_text,
        pair_visual,
        key_row[:, None],
        key_row[None, :],
        key_pos[:, None],
        key_doc[:, None],
        visual_row[:, None],
        visual_row[None, :],
        query_pos[None, :],
        query_doc[None, :],
    )


def local_fast(
    patches, vit_gain, merge_up, merge_down, dest, text, norm_gain, kv_weight, queries, out_grad, assign, docs
):
    f32, bf16 = jnp.float32, jnp.bfloat16
    data_count, column_count = lax.axis_size("dp"), lax.axis_size("y")
    ctx_count = 2 * column_count
    data, column, core = lax.axis_index("dp"), lax.axis_index("y"), lax.axis_index("core")
    rows, width = text.shape[1], text.shape[2]
    tokens = dest.shape[0]
    block = kv_weight.shape[0]
    length = rows * ctx_count
    core_word = core[None].astype(jnp.int32)

    far = [kv_weight] + [neighbor(kv_weight, "dp", 2 * i) for i in range(1, data_count // 2)]
    blocks, owners = [], []
    for i, held in enumerate(far):
        beside = neighbor(held, "dp", 1)
        below = neighbor(held, "y", 1)
        corner = neighbor(beside, "y", 1) if i % 2 == 0 else neighbor(below, "dp", 1)
        for piece, along, down in ((held, 0, 0), (beside, 1, 0), (below, 0, 1), (corner, 1, 1)):
            blocks.append(piece)
            owners.append((data ^ (2 * i + along)) * column_count + (column ^ down))
    table = jnp.stack(owners + [core]).astype(jnp.int32)

    own_rows, other_part = split_halves(text[0], core_word, block)
    sibling_rows = swap(other_part)
    query_width = queries.shape[2] // 2

    def heads_of(values):
        mine = lax.dynamic_slice_in_dim(values, core * query_width, query_width, 1)
        theirs = lax.dynamic_slice_in_dim(values, (1 - core) * query_width, query_width, 1)
        return mine, swap(theirs)

    query_parts, upstream_parts = heads_of(queries[0]), heads_of(out_grad[0])

    normed = merger_norm(patches, vit_gain)
    inner_hidden = jax.nn.gelu(
        jnp.dot(normed, merge_up, preferred_element_type=f32), approximate=False
    ).astype(bf16)
    merged, merged_other = down_halves(inner_hidden, merge_down, core_word, block)
    merged = (merged.astype(f32) + swap(merged_other).astype(f32)).astype(bf16)
    chip_tokens = 2 * tokens
    visual32 = lax.dynamic_slice_in_dim(merged, column * chip_tokens, chip_tokens, 0).astype(f32)
    for offset in range(1, column_count):
        leaving = lax.dynamic_slice_in_dim(merged, (column ^ offset) * chip_tokens, chip_tokens, 0)
        visual32 = visual32 + neighbor(leaving, "y", offset).astype(f32)
    visual = visual32.astype(bf16)

    dest_other = swap(dest)
    chip_dest = jnp.where(
        core == 0, jnp.concatenate([dest, dest_other]), jnp.concatenate([dest_other, dest])
    )
    token_core = jnp.arange(chip_tokens, dtype=jnp.int32) // tokens
    sequence, row_of = chip_dest // length, chip_dest % length
    slot = sequence * (2 * ctx_count) + token_core * ctx_count + row_of // rows
    slot_total = data_count * 2 * ctx_count
    picking = jnp.arange(slot_total, dtype=jnp.int32)[:, None] == slot[None, :]
    leaving_rows = jnp.sum(jnp.where(picking, row_of[None, :] + 1, 0), axis=1) - 1

    def to_sequences(values):
        shaped = values.reshape((data_count, 1, 2 * ctx_count) + values.shape[1:])
        shaped = jnp.broadcast_to(shaped, (data_count, column_count) + shaped.shape[2:])
        shaped = shaped.reshape((data_count * column_count,) + shaped.shape[2:])
        return lax.all_to_all(shaped, ("dp", "y"), split_axis=0, concat_axis=0, tiled=True)

    visual_row = to_sequences(leaving_rows).reshape(-1)

    halves = rows // 2
    positions = (assign[:, None] * halves + jnp.arange(halves, dtype=jnp.int32)[None, :]).reshape(length)
    labels = docs[0].reshape(-1, halves)[assign].reshape(length)
    order = jnp.stack(
        [2 * (column ^ down) + (core ^ side) for down in range(column_count) for side in range(2)]
    )
    key_row = (order[:, None] * rows + jnp.arange(rows, dtype=jnp.int32)[None, :]).reshape(length)
    key_pos = positions.reshape(ctx_count, rows)[order].reshape(length)
    key_doc = labels.reshape(ctx_count, rows)[order].reshape(length)

    def squares(values):
        values = values.astype(f32)
        return jnp.sum(values * values, axis=1)

    own_squares, sibling_squares, visual_squares = squares(own_rows), squares(sibling_rows), squares(visual)
    arrived = swap(jnp.concatenate([sibling_squares, own_squares, visual_squares]))
    square = jnp.concatenate([own_squares, sibling_squares, visual_squares]) + arrived
    scale = lax.rsqrt(square / width + epsilon)[:, None]
    gain = lax.dynamic_index_in_dim(
        norm_gain.reshape(-1, 2, block), core, axis=1, keepdims=False
    ).reshape(1, width // 2)

    mine, theirs = project(table, own_rows, sibling_rows, visual, gain, blocks)
    pairs = ((mine + swap(theirs).astype(f32)) * scale).astype(bf16)
    pair_chip, pair_tokens = pairs[: 2 * rows], pairs[2 * rows :]
    pair_text = jnp.concatenate(
        [pair_chip] + [neighbor(pair_chip, "y", down) for down in range(1, column_count)], axis=0
    )
    leaving = jnp.dot(picking.astype(bf16), pair_tokens, preferred_element_type=f32).astype(bf16)
    pair_visual = to_sequences(leaving).reshape(-1, pairs.shape[1])
    out_a, out_b, grad_a, grad_b, pair_grad, visual_pair_grad, keep = attend_pair(
        query_parts, upstream_parts, pair_text, pair_visual, key_row, key_pos, key_doc, visual_row,
        key_pos[: 2 * rows], key_doc[: 2 * rows],
    )

    def heads_back(held, leaving):
        arrived = swap(leaving)
        return jnp.where(
            core == 0, jnp.concatenate([held, arrived], axis=1), jnp.concatenate([arrived, held], axis=1)
        )

    attention, query_grad = heads_back(out_a, out_b), heads_back(grad_a, grad_b)
    text_grad = pair_grad[: 2 * rows].astype(f32)
    for down in range(1, column_count):
        part = pair_grad[2 * rows * down : 2 * rows * (down + 1)]
        text_grad = text_grad + neighbor(part, "y", down).astype(f32)
    returned = lax.all_to_all(
        visual_pair_grad.reshape(data_count * column_count, 2 * ctx_count, -1),
        ("dp", "y"), split_axis=0, concat_axis=0, tiled=True,
    )
    returned = jnp.sum(returned.reshape(data_count, column_count, 2 * ctx_count, -1).astype(f32), axis=1)
    token_grad = jnp.dot(
        picking.T.astype(bf16), returned.reshape(slot_total, -1).astype(bf16), preferred_element_type=f32
    )
    grads = jnp.concatenate([text_grad, token_grad], axis=0).astype(bf16)

    def turned(values):
        return jnp.concatenate([values[rows : 2 * rows], values[:rows], values[2 * rows :]], axis=0)

    inner = jnp.sum(grads.astype(f32) * pairs.astype(f32), axis=1)
    inner = inner + swap(turned(inner))
    back = inner[:, None] * scale * scale / width
    sibling_grads = swap(turned(grads))
    keep_rows = jnp.concatenate([keep[: 2 * rows], jnp.ones((chip_tokens, 1), f32)], axis=0)
    held, leaving = project_back(
        table, grads, sibling_grads, own_rows, sibling_rows, visual, gain, scale, back, keep_rows, blocks
    )
    hidden_grad, visual_grad = join_halves(core_word, held, swap(leaving), rows, block)
    return (attention[None], query_grad[None], hidden_grad[None], visual_grad)


def solution(mesh):
    data_count, ctx_count = mesh.shape["dp"], mesh.shape["ctx"]
    split = Mesh(mesh.devices.reshape(data_count, -1, 2), ("dp", "y", "core"))

    def call(*arrays):
        text, kv_weight, dest = arrays[5], arrays[7], arrays[4]
        devices = data_count * ctx_count
        rows = text.shape[1] // ctx_count
        fits = (
            ctx_count == 4
            and data_count % 4 == 0
            and data_count & (data_count - 1) == 0
            and (kv_weight.shape[0] // devices) % 128 == 0
            and dest.shape[0] // devices <= devices
            and rows % 128 == 0
        )
        if fits:
            whole, ctx, body, used = ("dp", "y", "core"), ("y", "core"), local_fast, split
        else:
            whole, ctx, body, used = ("dp", "ctx"), "ctx", local, mesh
        placed = (
            P("dp", None),
            P(),
            P(None, ctx),
            P(ctx, None),
            P(whole),
            P("dp", ctx, None),
            P(),
            P(whole, None),
            P("dp", ctx, None),
            P("dp", ctx, None),
            P(),
            P("dp", None),
        )
        return jax.shard_map(
            body,
            mesh=used,
            in_specs=placed,
            out_specs=(P("dp", ctx, None), P("dp", ctx, None), P("dp", ctx, None), P(whole, None)),
            check_vma=False,
        )(*arrays)

    return call
```

```python
import jax
import jax.numpy as jnp
from jax import lax
from jax.experimental import pallas as pl
from jax.experimental.pallas import tpu as pltpu
from jax.sharding import Mesh
from jax.sharding import PartitionSpec as P

HEADS = 32
KVH = 4
HD = 128


epsilon = 1e-06


def merger_norm(patches, vit_gain):
    pieces = patches.astype(jnp.float32).reshape(patches.shape[0], 4, vit_gain.shape[0])
    center = pieces - jnp.mean(pieces, axis=-1, keepdims=True)
    spread = jnp.mean(center * center, axis=-1, keepdims=True)
    scaled = center * lax.rsqrt(spread + epsilon) * vit_gain
    return scaled.reshape(patches.shape[0], -1).astype(jnp.bfloat16)


def rms_scale(hidden32, norm_gain):
    square = jnp.mean(hidden32 * hidden32, axis=-1, keepdims=True)
    return hidden32 * lax.rsqrt(square + epsilon) * norm_gain


def attend(query_rows, pair_rows, upstream_rows, query_pos, query_doc, key_pos, key_doc):
    row_count = query_rows.shape[0]
    key_count = pair_rows.shape[0]
    group_size = HEADS // KVH
    score_scale = HD ** (-0.5)
    query_heads = query_rows.reshape(row_count, KVH, group_size, HD)
    key_heads = pair_rows[:, : KVH * HD].reshape(key_count, KVH, HD)
    value_heads = pair_rows[:, KVH * HD :].reshape(key_count, KVH, HD)
    scores = (
        jnp.einsum("qhgd,khd->hgqk", query_heads, key_heads, preferred_element_type=jnp.float32)
        * score_scale
    )
    allowed = (key_pos[None, :] <= query_pos[:, None]) & (key_doc[None, :] == query_doc[:, None])
    scores = jnp.where(allowed, scores, -jnp.inf)
    weights = jnp.exp(scores - jnp.max(scores, axis=-1, keepdims=True))
    weights = weights / jnp.sum(weights, axis=-1, keepdims=True)
    light_weights = weights.astype(jnp.bfloat16)
    output = jnp.einsum(
        "hgqk,khd->qhgd", light_weights, value_heads, preferred_element_type=jnp.float32
    )
    upstream = upstream_rows.reshape(row_count, KVH, group_size, HD)
    value_grad = jnp.einsum(
        "hgqk,qhgd->khd", light_weights, upstream, preferred_element_type=jnp.float32
    )
    weight_grad = jnp.einsum(
        "qhgd,khd->hgqk", upstream, value_heads, preferred_element_type=jnp.float32
    )
    inner_sum = jnp.sum(weights * weight_grad, axis=-1, keepdims=True)
    score_grad = (weights * (weight_grad - inner_sum) * score_scale).astype(jnp.bfloat16)
    query_grad = jnp.einsum(
        "hgqk,khd->qhgd", score_grad, key_heads, preferred_element_type=jnp.float32
    )
    key_grad = jnp.einsum(
        "hgqk,qhgd->khd", score_grad, query_heads, preferred_element_type=jnp.float32
    )
    output = output.reshape(row_count, HEADS * HD).astype(jnp.bfloat16)
    query_grad = query_grad.reshape(row_count, HEADS * HD).astype(jnp.bfloat16)
    return (
        output,
        query_grad,
        key_grad.reshape(key_count, KVH * HD),
        value_grad.reshape(key_count, KVH * HD),
    )


def local(
    patches,
    vit_gain,
    merge_up,
    merge_down,
    dest,
    text,
    norm_gain,
    kv_weight,
    queries,
    out_grad,
    assign,
    docs,
):
    ctx_count = lax.axis_size("ctx")
    data_count = lax.axis_size("dp")
    device_count = ctx_count * data_count
    token_rows = text.shape[1]
    visual_rows = dest.shape[0]
    capacity = max(1, visual_rows // device_count)
    slot_total = device_count * capacity
    normed = merger_norm(patches, vit_gain)
    inner_hidden = jax.nn.gelu(
        jnp.dot(normed, merge_up, preferred_element_type=jnp.float32), approximate=False
    ).astype(jnp.bfloat16)
    visual = lax.psum_scatter(
        jnp.dot(inner_hidden, merge_down, preferred_element_type=jnp.float32).astype(jnp.bfloat16),
        "ctx",
        scatter_dimension=0,
        tiled=True,
    )
    target = dest // token_rows
    local_row = dest % token_rows
    token_order = jnp.arange(visual_rows, dtype=jnp.int32)
    before = (target[:, None] == target[None, :]) & (token_order[None, :] < token_order[:, None])
    slot_index = target * capacity + jnp.sum(before.astype(jnp.int32), axis=1)
    picking = jnp.arange(slot_total, dtype=jnp.int32)[:, None] == slot_index[None, :]
    outgoing = jnp.dot(
        picking.astype(jnp.bfloat16), visual, preferred_element_type=jnp.float32
    ).astype(jnp.bfloat16)
    outgoing_rows = jnp.sum(jnp.where(picking, local_row[None, :] + 1, 0), axis=1) - 1
    arrived, arrived_rows = (
        lax.all_to_all(outgoing, ("dp", "ctx"), split_axis=0, concat_axis=0, tiled=True),
        lax.all_to_all(outgoing_rows, ("dp", "ctx"), split_axis=0, concat_axis=0, tiled=True),
    )
    placing = jnp.arange(token_rows, dtype=jnp.int32)[:, None] == arrived_rows[None, :]
    placed = jnp.dot(
        placing.astype(jnp.bfloat16), arrived, preferred_element_type=jnp.float32
    ).astype(jnp.bfloat16)
    marked = jnp.any(placing, axis=1)
    hidden = jnp.where(marked[:, None], placed, text[0])
    hidden32 = hidden.astype(jnp.float32)
    normed_hidden = rms_scale(hidden32, norm_gain).astype(jnp.bfloat16)
    projected = jnp.dot(
        normed_hidden,
        lax.all_gather(kv_weight, ("dp", "ctx"), axis=0, tiled=True),
        preferred_element_type=jnp.float32,
    )
    pairs_local = projected.astype(jnp.bfloat16)
    pairs_all = lax.all_gather(pairs_local, "ctx", axis=0, tiled=True)
    halves = token_rows // 2
    length = token_rows * ctx_count
    positions = (assign[:, None] * halves + jnp.arange(halves, dtype=jnp.int32)[None, :]).reshape(
        length
    )
    labels = docs[0].reshape(-1, halves)[assign].reshape(length)
    own_start = lax.axis_index("ctx") * token_rows
    query_pos = lax.dynamic_slice_in_dim(positions, own_start, token_rows, 0)
    query_doc = lax.dynamic_slice_in_dim(labels, own_start, token_rows, 0)
    attention, query_grad, key_grad, value_grad = attend(
        queries[0], pairs_all, out_grad[0], query_pos, query_doc, positions, labels
    )
    key_grad, value_grad = (
        lax.psum_scatter(
            key_grad.astype(jnp.bfloat16), "ctx", scatter_dimension=0, tiled=True
        ).astype(jnp.float32),
        lax.psum_scatter(
            value_grad.astype(jnp.bfloat16), "ctx", scatter_dimension=0, tiled=True
        ).astype(jnp.float32),
    )
    pair_grad = jnp.concatenate([key_grad, value_grad], axis=1).astype(jnp.bfloat16)
    contract = (((1,), (1,)), ((), ()))
    normed_grad = lax.dot_general(
        pair_grad,
        lax.all_gather(kv_weight, ("dp", "ctx"), axis=0, tiled=True),
        contract,
        preferred_element_type=jnp.float32,
    )
    forward_value, pullback = jax.vjp(lambda values: rms_scale(values, norm_gain), hidden32)
    full_grad = pullback(normed_grad)[0]
    hidden_grad = jnp.where(marked[:, None], jnp.float32(0.0), full_grad).astype(jnp.bfloat16)
    returning = jnp.dot(
        placing.T.astype(jnp.bfloat16),
        full_grad.astype(jnp.bfloat16),
        preferred_element_type=jnp.float32,
    ).astype(jnp.bfloat16)
    returned = lax.all_to_all(returning, ("dp", "ctx"), split_axis=0, concat_axis=0, tiled=True)
    visual_grad = jnp.dot(
        picking.T.astype(jnp.bfloat16), returned, preferred_element_type=jnp.float32
    ).astype(jnp.bfloat16)
    return (attention[None], query_grad[None], hidden_grad[None], visual_grad)


def neighbor(values, axis, offset):
    count = lax.axis_size(axis)
    return lax.ppermute(values, axis, [(d, d ^ offset) for d in range(count)])


def after(values, earlier):
    return lax.optimization_barrier((values, *earlier))[0]


def swap(values):
    return neighbor(values, "core", 1)


def vmem_params(size=16):
    return pltpu.CompilerParams(vmem_limit_bytes=size * 1024 * 1024)


def brief():
    return pl.CostEstimate(flops=1, bytes_accessed=1, transcendentals=0)


def smem():
    return pl.BlockSpec(memory_space=pltpu.SMEM)


def store_halves(core, values, own_ref, other_ref, block):
    def put(own_parity):
        for j in range(values.shape[1] // (2 * block)):
            even = values[:, 2 * j * block : (2 * j + 1) * block]
            odd = values[:, (2 * j + 1) * block : (2 * j + 2) * block]
            own_ref[:, j * block : (j + 1) * block] = odd if own_parity else even
            other_ref[:, j * block : (j + 1) * block] = even if own_parity else odd

    @pl.when(core == 0)
    def _():
        put(0)

    @pl.when(core != 0)
    def _():
        put(1)


def split_halves(values, core, block):
    rows, width = values.shape
    step = 8 * block

    def kernel(core_ref, value_ref, own_ref, other_ref):
        store_halves(core_ref[0], value_ref[...], own_ref, other_ref, block)

    half = jax.ShapeDtypeStruct((rows, width // 2), values.dtype)
    out = pl.BlockSpec((rows, step // 2), lambda j: (0, j))
    return pl.pallas_call(
        kernel,
        grid=(width // step,),
        in_specs=[smem(), pl.BlockSpec((rows, step), lambda j: (0, j))],
        out_specs=[out, out],
        out_shape=[half, half],
        compiler_params=vmem_params(56),
        cost_estimate=brief(),
        name="split_halves",
    )(core, values)


def down_halves(inner_hidden, merge_down, core, block):
    rows, depth = inner_hidden.shape
    width = merge_down.shape[1]
    step = 4 * block
    count = width // step

    def kernel(core_ref, hidden_ref, weight_ref, own_ref, other_ref, buffers, sems):
        copies = [
            pltpu.make_async_copy(weight_ref.at[:, j * step : (j + 1) * step], buffers.at[j], sems.at[j])
            for j in range(count)
        ]
        for copy in copies:
            copy.start()
        for j in range(count):
            copies[j].wait()
            product = jnp.dot(hidden_ref[...], buffers[j], preferred_element_type=jnp.float32)
            place = slice(j * step // 2, (j + 1) * step // 2)
            store_halves(
                core_ref[0], product.astype(jnp.bfloat16), own_ref.at[:, place], other_ref.at[:, place], block
            )

    vmem = pl.BlockSpec(memory_space=pltpu.VMEM)
    half = jax.ShapeDtypeStruct((rows, width // 2), jnp.bfloat16)
    return pl.pallas_call(
        kernel,
        in_specs=[smem(), vmem, pl.BlockSpec(memory_space=pl.ANY)],
        out_specs=[vmem, vmem],
        out_shape=[half, half],
        scratch_shapes=[
            pltpu.VMEM((count, depth, step), jnp.bfloat16),
            pltpu.SemaphoreType.DMA((count,)),
        ],
        compiler_params=vmem_params(56),
        cost_estimate=brief(),
        name="merge_down",
    )(core, inner_hidden, merge_down)


def project(table, own_rows, sibling_rows, visual, gain, blocks, first, count, earlier):
    rows = own_rows.shape[0]
    total = 2 * rows + visual.shape[0]
    block, width = blocks[0].shape
    quarter = width // 4
    size = len(blocks)
    last = first + size == count
    flag = table.shape[0] - 1

    def kernel(table_ref, own_ref, sibling_ref, visual_ref, gain_ref, *rest):
        block_refs = rest[:size]
        before_refs = rest[size : size + len(earlier)]
        turned_ref, *outs, turning, sems = rest[size + len(earlier) :]
        total_ref = outs[-1]
        turns = []
        for r in range(size):
            columns = pl.ds(pl.multiple_of(table_ref[first + r] * block, block), block)
            gains = gain_ref[:, columns]
            part = jnp.concatenate(
                [
                    (ref[:, columns].astype(jnp.float32) * gains).astype(jnp.bfloat16)
                    for ref in (own_ref, sibling_ref, visual_ref)
                ],
                axis=0,
            )
            values = block_refs[r][...]
            product = jnp.dot(part, values, preferred_element_type=jnp.float32)
            if r > 0:
                total_ref[...] += product
            elif earlier:
                total_ref[...] = before_refs[0][...] + product
            else:
                total_ref[...] = product
            turning[r] = values.T
            turn = pltpu.make_async_copy(turning.at[r], turned_ref.at[r], sems.at[r])
            turn.start()
            turns.append(turn)
        if last:
            mine_ref, theirs_ref = outs[:2]

            def put(parity):
                for piece in range(2):
                    start = 2 * piece * quarter
                    mine = slice(start + parity * quarter, start + (parity + 1) * quarter)
                    theirs = slice(start + (1 - parity) * quarter, start + (2 - parity) * quarter)
                    place = slice(piece * quarter, (piece + 1) * quarter)
                    mine_ref[:, place] = total_ref[:, mine]
                    theirs_ref[:rows, place] = total_ref[rows : 2 * rows, theirs].astype(jnp.bfloat16)
                    theirs_ref[rows : 2 * rows, place] = total_ref[:rows, theirs].astype(jnp.bfloat16)
                    theirs_ref[2 * rows :, place] = total_ref[2 * rows :, theirs].astype(jnp.bfloat16)

            @pl.when(table_ref[flag] == 0)
            def _():
                put(0)

            @pl.when(table_ref[flag] != 0)
            def _():
                put(1)

        for turn in turns:
            turn.wait()

    vmem = pl.BlockSpec(memory_space=pltpu.VMEM)
    shape = jax.ShapeDtypeStruct
    sums, scratch = [shape((total, width), jnp.float32)], []
    if last:
        sums = [shape((total, width // 2), jnp.float32), shape((total, width // 2), jnp.bfloat16)]
        scratch = [pltpu.VMEM((total, width), jnp.float32)]
    return pl.pallas_call(
        kernel,
        in_specs=[smem()] + [vmem] * (4 + size + len(earlier)),
        out_specs=[pl.BlockSpec(memory_space=pl.ANY)] + [vmem] * len(sums),
        out_shape=[shape((size, width, block), jnp.bfloat16)] + sums,
        scratch_shapes=scratch + [pltpu.VMEM((size, width, block), jnp.bfloat16), pltpu.SemaphoreType.DMA((size,))],
        compiler_params=vmem_params(24 if last else 56),
        cost_estimate=brief(),
        name="project_pairs",
    )(table, own_rows, sibling_rows, visual, gain, *blocks, *earlier)


def finish_pairs(mine, received, scale, codes, picking, rows):
    total, width = mine.shape
    slots, tokens = picking.shape

    def kernel(mine_ref, received_ref, scale_ref, codes_ref, picking_ref, chip_ref, token_ref, slot_ref):
        pairs = (mine_ref[...] + received_ref[...].astype(jnp.float32)) * scale_ref[...]
        pairs = pairs.astype(jnp.bfloat16)
        chip_ref[...] = pairs[: 2 * rows]
        token_ref[...] = pairs[2 * rows :]
        placing = picking_ref[...]
        slot_ref[:, :width] = jnp.dot(
            placing, pairs[2 * rows :], preferred_element_type=jnp.float32
        ).astype(jnp.bfloat16)
        slot_ref[:, width:] = jnp.dot(
            placing, codes_ref[...], preferred_element_type=jnp.float32
        ).astype(jnp.bfloat16)

    shape = jax.ShapeDtypeStruct
    return pl.pallas_call(
        kernel,
        out_shape=[
            shape((2 * rows, width), jnp.bfloat16),
            shape((tokens, width), jnp.bfloat16),
            shape((slots, width + codes.shape[1]), jnp.bfloat16),
        ],
        compiler_params=vmem_params(56),
        cost_estimate=brief(),
        name="finish_pairs",
    )(mine, received, scale, codes, picking)


def sum_grads(core, pair_grad, received, returned, picking, rows):
    width = pair_grad.shape[1]
    tokens = picking.shape[1] // 2

    def kernel(core_ref, grad_ref, returned_ref, picking_ref, *rest):
        held_ref, sent_ref = rest[-2:]
        text = grad_ref[...].astype(jnp.float32)
        for ref in rest[:-2]:
            text = text + ref[...].astype(jnp.float32)
        text = text.astype(jnp.bfloat16)
        held_ref[:rows] = text[:rows]
        sent_ref[:rows] = text[rows:]
        token = lax.dot_general(
            picking_ref[...], returned_ref[...], (((0,), (0,)), ((), ())), preferred_element_type=jnp.float32
        ).astype(jnp.bfloat16)

        @pl.when(core_ref[0] == 0)
        def _():
            held_ref[rows:] = token[:tokens]
            sent_ref[rows:] = token[tokens:]

        @pl.when(core_ref[0] != 0)
        def _():
            held_ref[rows:] = token[tokens:]
            sent_ref[rows:] = token[:tokens]

    def whole(values):
        return pl.BlockSpec(values.shape, lambda j: (0, 0))

    half = jax.ShapeDtypeStruct((rows + tokens, width), jnp.bfloat16)
    return pl.pallas_call(
        kernel,
        grid=(1,),
        in_specs=[smem(), pl.BlockSpec((2 * rows, width), lambda j: (0, 0)), whole(returned), whole(picking)]
        + [whole(part) for part in received],
        out_specs=[whole(jax.ShapeDtypeStruct((rows + tokens, width), jnp.bfloat16))] * 2,
        out_shape=[half, half],
        compiler_params=vmem_params(56),
        cost_estimate=brief(),
        name="sum_grads",
    )(core, pair_grad, returned, picking, *received)


def project_back(table, grads, pairs, turned, text, visual, gain, scale, keep):
    rows, width = text.shape
    tokens = visual[0].shape[0]
    total = rows + tokens
    pair_width, block = turned[0][0].shape[1:]
    quarter = pair_width // 4
    flag = table.shape[0] - 1
    pieces = len(turned[0])
    count = sum(part.shape[0] for part in turned[0])
    groups, first = [], 0
    for piece in range(pieces):
        size = turned[0][piece].shape[0]
        for low in range(0, size, 4):
            high = min(size, low + 4)
            groups.append((piece, low, high, first + low))
        first += size

    def kernel(
        table_ref, grad_ref, grad_other_ref, pair_ref, pair_other_ref, text_ref, visual_ref, visual_other_ref,
        gain_ref, scale_ref, keep_ref, *rest,
    ):
        turned_refs, (hidden_ref, token_ref, joined, buffers, sems) = rest[: 2 * pieces], rest[2 * pieces :]
        core = table_ref[flag]
        copies = []
        for at, (piece, low, high, place) in enumerate(groups):
            copies.append(
                [
                    pltpu.make_async_copy(
                        turned_refs[side * pieces + piece].at[low:high],
                        buffers.at[side, place : place + high - low],
                        sems.at[at, side],
                    )
                    for side in range(2)
                ]
            )
        for pair in copies[:2]:
            for copy in pair:
                copy.start()

        def join(parity):
            for piece in range(2):
                place = slice(piece * quarter, (piece + 1) * quarter)
                start = (2 * piece + parity) * quarter
                joined[:, start : start + quarter] = grad_ref[:, place]
                start = (2 * piece + 1 - parity) * quarter
                joined[:, start : start + quarter] = grad_other_ref[:, place]

        @pl.when(core == 0)
        def _():
            join(0)

        @pl.when(core != 0)
        def _():
            join(1)

        inner = jnp.zeros((total, 1), jnp.float32)
        for left, right in ((grad_ref, pair_ref), (grad_other_ref, pair_other_ref)):
            inner = inner + jnp.sum(
                left[...].astype(jnp.float32) * right[...].astype(jnp.float32), axis=1, keepdims=True
            )
        scales = scale_ref[...]
        backs = inner * scales * scales * (1.0 / width)
        keeps = keep_ref[:rows] > 0
        for at, (piece, low, high, first) in enumerate(groups):
            for copy in copies[at]:
                copy.wait()
            if at + 2 < len(groups):
                for copy in copies[at + 2]:
                    copy.start()
            for r in range(first, first + high - low):
                spot = table_ref[r]
                inside = pl.ds(pl.multiple_of(spot * block, block), block)
                for half, (side, token_in) in enumerate(((core, visual_ref), (1 - core, visual_other_ref))):
                    place = pl.ds(pl.multiple_of((2 * spot + side) * block, block), block)
                    normed_grad = jnp.dot(joined[...], buffers[half, r], preferred_element_type=jnp.float32)
                    full = normed_grad * scales * gain_ref[:, place]
                    hidden = full[:rows] - text_ref[:, place].astype(jnp.float32) * backs[:rows]
                    hidden_ref[:, place] = jnp.where(keeps, hidden, 0.0).astype(jnp.bfloat16)
                    token = full[rows:] - token_in[:, inside].astype(jnp.float32) * backs[rows:]
                    token_ref[:, place] = token.astype(jnp.bfloat16)

    vmem = pl.BlockSpec(memory_space=pltpu.VMEM)
    shape = jax.ShapeDtypeStruct
    return pl.pallas_call(
        kernel,
        in_specs=[smem()] + [vmem] * 10 + [pl.BlockSpec(memory_space=pl.ANY)] * (2 * pieces),
        out_specs=[vmem, vmem],
        out_shape=[shape((rows, width), jnp.bfloat16), shape((tokens, width), jnp.bfloat16)],
        scratch_shapes=[
            pltpu.VMEM((total, pair_width), jnp.bfloat16),
            pltpu.VMEM((2, count, pair_width, block), jnp.bfloat16),
            pltpu.SemaphoreType.DMA((len(groups), 2)),
        ],
        compiler_params=vmem_params(56),
        cost_estimate=brief(),
        name="project_back",
    )(table, *grads, *pairs, text, *visual, gain, scale, keep, *turned[0], *turned[1])


def attend_pair(queries, upstream, pair_text, pair_visual, keyed):
    rows, width = queries[0].shape
    length, pair_width = pair_text[0].shape[0] * len(pair_text), pair_text[0].shape[1]
    slots = pair_visual.shape[0]
    own_kv = pair_width // (2 * HD)
    heads = width // HD
    group = heads // own_kv
    step_heads = max(1, group // 2)
    steps = heads // step_heads
    score_scale = HD ** (-0.5)
    f32, bf16 = jnp.float32, jnp.bfloat16

    def kernel(
        qa, qb, ua, ub, visual_ref, row_s, row_l, pos_ref, doc_ref, qpos_ref, qdoc_ref, *rest,
    ):
        text_refs = rest[: len(pair_text)]
        oa, ob, ga, gb, *grad_refs, grad_visual_ref, keep_ref, heads_ref, turned_ref, bias_ref, total_ref = rest[
            len(pair_text) :
        ]
        step = pl.program_id(0)

        @pl.when(step == 0)
        def _():
            codes = visual_ref[:, pair_width:].astype(f32).T
            placing = jnp.where(row_s[...] == codes[0:1] * 16.0 + codes[1:2], 1.0, 0.0).astype(f32)
            placed = jnp.dot(placing.astype(bf16), visual_ref[:, :pair_width], preferred_element_type=f32)
            marked = jnp.max(placing, axis=1, keepdims=True)
            keep_ref[...] = 1.0 - marked
            texts = jnp.concatenate([ref[...].astype(f32) for ref in text_refs], axis=0)
            pairs = jnp.where(marked > 0, placed, texts)
            for j in range(2 * own_kv):
                piece = pairs[:, j * HD : (j + 1) * HD]
                heads_ref[j] = piece.astype(bf16)
                turned_ref[j] = piece.T.astype(bf16)
            allowed = (pos_ref[...] <= qpos_ref[...]) & (doc_ref[...] == qdoc_ref[...])
            bias_ref[...] = jnp.where(allowed, 0.0, -jnp.inf).astype(f32)
            total_ref[...] = jnp.zeros_like(total_ref)

        head = (step * step_heads) // group
        keys, values = heads_ref[head], heads_ref[own_kv + head]
        keys_turned, values_turned = turned_ref[head], turned_ref[own_kv + head]
        contract = (((1,), (1,)), ((), ()))
        for h in range(step_heads):
            lanes = slice(h * HD, (h + 1) * HD)
            query = jnp.concatenate([qa[:, lanes], qb[:, lanes]], axis=0)
            up = jnp.concatenate([ua[:, lanes], ub[:, lanes]], axis=0)
            scores = lax.dot_general(keys, query, contract, preferred_element_type=f32)
            scores = scores * score_scale + bias_ref[...]
            weights = jnp.exp(scores - jnp.max(scores, axis=0, keepdims=True))
            weights = weights * (1.0 / jnp.sum(weights, axis=0, keepdims=True))
            light = weights.astype(bf16)
            output = jnp.dot(values_turned, light, preferred_element_type=f32).T.astype(bf16)
            oa[:, lanes] = output[:rows]
            ob[:, lanes] = output[rows:]
            total_ref[own_kv + head] += jnp.dot(light, up, preferred_element_type=f32)
            weight_grad = lax.dot_general(values, up, contract, preferred_element_type=f32)
            inner = jnp.sum(weights * weight_grad, axis=0, keepdims=True)
            score_grad = (weights * (weight_grad - inner) * score_scale).astype(bf16)
            query_grad = jnp.dot(keys_turned, score_grad, preferred_element_type=f32).T.astype(bf16)
            ga[:, lanes] = query_grad[:rows]
            gb[:, lanes] = query_grad[rows:]
            total_ref[head] += jnp.dot(score_grad, query, preferred_element_type=f32)

        @pl.when(step == steps - 1)
        def _():
            codes = visual_ref[:, pair_width : pair_width + 2].astype(f32)
            lifting = jnp.where(codes[:, 0:1] * 16.0 + codes[:, 1:2] == row_l[...], 1.0, 0.0).astype(bf16)
            for j in range(2 * own_kv):
                piece = total_ref[j].astype(bf16)
                place = slice(j * HD, (j + 1) * HD)
                for i, ref in enumerate(grad_refs):
                    ref[:, place] = piece[i * ref.shape[0] : (i + 1) * ref.shape[0]]
                grad_visual_ref[:, place] = jnp.dot(lifting, piece, preferred_element_type=f32).astype(bf16)

    part = pl.BlockSpec((rows, step_heads * HD), lambda j: (0, j))
    vmem = pl.BlockSpec(memory_space=pltpu.VMEM)
    shape = jax.ShapeDtypeStruct
    return pl.pallas_call(
        kernel,
        grid=(steps,),
        in_specs=[part] * 4 + [vmem] * (7 + len(pair_text)),
        out_specs=[part] * 4 + [vmem] * (2 + len(pair_text)),
        out_shape=[shape((rows, width), bf16)] * 4
        + [shape(x.shape, bf16) for x in pair_text]
        + [shape((slots, pair_width), bf16), shape((length, 1), f32)],
        scratch_shapes=[
            pltpu.VMEM((2 * own_kv, length, HD), bf16),
            pltpu.VMEM((2 * own_kv, HD, length), bf16),
            pltpu.VMEM((length, 2 * rows), f32),
            pltpu.VMEM((2 * own_kv, length, HD), f32),
        ],
        compiler_params=vmem_params(56),
        cost_estimate=brief(),
        name="attend",
    )(
        *queries,
        *upstream,
        pair_visual,
        *keyed,
        *pair_text,
    )


def local_fast(
    patches, vit_gain, merge_up, merge_down, dest, text, norm_gain, kv_weight, queries, out_grad, assign, docs
):
    f32, bf16 = jnp.float32, jnp.bfloat16
    data_count, column_count = lax.axis_size("dp"), lax.axis_size("y")
    ctx_count = 2 * column_count
    data, column, core = lax.axis_index("dp"), lax.axis_index("y"), lax.axis_index("core")
    rows, width = text.shape[1], text.shape[2]
    tokens = dest.shape[0]
    block = kv_weight.shape[0]
    length = rows * ctx_count
    core_word = core[None].astype(jnp.int32)

    def line(values, pairs):
        return lax.ppermute(values, "dp", [(2 * p + low, 2 * q + low) for p, q in pairs for low in range(2)])

    def both(values):
        return neighbor(values, "dp", 1), neighbor(values, "y", 1)

    close = lax.optimization_barrier
    swapped = [(0, 1), (1, 0), (2, 3), (3, 2)]
    middle, outward = [(1, 2), (2, 1)], [(1, 0), (2, 3)]
    far_index = data // 2
    is_middle = (far_index == 1) | (far_index == 2)
    hops = [0, 1, jnp.where(is_middle, 3, 2), jnp.where(is_middle, 2, 3)]
    owners = [
        ((far_index ^ hops[i + j]) * 2 + ((data % 2) ^ along)) * column_count + (column ^ down)
        for i in (0, 2)
        for along, down in ((0, 0), (1, 0), (0, 1), (1, 1))
        for j in range(2)
    ]
    table = jnp.stack(owners + [core]).astype(jnp.int32)
    gain = lax.dynamic_index_in_dim(
        norm_gain.reshape(-1, 2, block), core, axis=1, keepdims=False
    ).reshape(1, width // 2)
    query_width = queries.shape[2] // 2
    chip_tokens = 2 * tokens

    beside0, below0 = both(kv_weight)
    far1, across = line(kv_weight, swapped), line(kv_weight, middle)
    vectors = []
    for j in range(patches.shape[1] // vit_gain.shape[0]):
        piece = lax.slice_in_dim(patches, j * vit_gain.shape[0], (j + 1) * vit_gain.shape[0], axis=1)
        center = piece.astype(f32)
        center = center - jnp.mean(center, axis=-1, keepdims=True)
        spread = jnp.mean(center * center, axis=-1, keepdims=True)
        vectors.append((center * lax.rsqrt(spread + epsilon) * vit_gain).astype(bf16))
    normed = jnp.concatenate(vectors, axis=1)
    inner_hidden = jax.nn.gelu(
        jnp.dot(normed, merge_up, preferred_element_type=f32), approximate=False
    ).astype(bf16)
    rows_in = text[0]
    beside0, below0, far1, across, inner_hidden, rows_in, core_word, table, gain = close(
        (beside0, below0, far1, across, inner_hidden, rows_in, core_word, table, gain)
    )

    beside1, below1 = both(far1)
    across2, ends1 = line(far1, middle), line(across, outward)
    merged, merged_other = down_halves(inner_hidden, merge_down, core_word, block)
    beside1, below1, across2, ends1, merged, merged_other, rows_in, core_word = close(
        (beside1, below1, across2, ends1, merged, merged_other, rows_in, core_word)
    )

    corner0, corner1 = neighbor(beside0, "y", 1), neighbor(below1, "dp", 1)
    ends2 = line(across2, outward)
    arriving = swap(merged_other)
    own_rows, other_part = split_halves(rows_in, core_word, block)
    sibling_rows = swap(other_part)
    far2 = jnp.where(is_middle, across, ends1)
    merged = (merged.astype(f32) + arriving.astype(f32)).astype(bf16)
    visual32 = lax.dynamic_slice_in_dim(merged, column * chip_tokens, chip_tokens, 0)
    leaving = lax.dynamic_slice_in_dim(merged, (column ^ 1) * chip_tokens, chip_tokens, 0)
    summing = neighbor(leaving, "y", 1)
    query_in, upstream_in = queries[0], out_grad[0]
    corner0, corner1, ends2, own_rows, sibling_rows, far2, visual32, summing = close(
        (corner0, corner1, ends2, own_rows, sibling_rows, far2, visual32, summing)
    )
    query_in, upstream_in, dest, assign, docs, ends2 = close((query_in, upstream_in, dest, assign, docs, ends2))

    def heads_of(values):
        mine = lax.dynamic_slice_in_dim(values, core * query_width, query_width, 1)
        theirs = lax.dynamic_slice_in_dim(values, (1 - core) * query_width, query_width, 1)
        return mine, theirs

    beside2, below2 = both(far2)
    far3 = jnp.where(is_middle, across2, ends2)
    query_parts, upstream_parts = heads_of(query_in), heads_of(upstream_in)
    query_parts = (query_parts[0], swap(query_parts[1]))
    upstream_parts = (upstream_parts[0], swap(upstream_parts[1]))

    def squares(values):
        values = values.astype(f32)
        return jnp.sum(values * values, axis=1)

    own_squares, sibling_squares = squares(own_rows), squares(sibling_rows)

    dest_other = swap(dest)
    chip_dest = jnp.where(
        core == 0, jnp.concatenate([dest, dest_other]), jnp.concatenate([dest_other, dest])
    )
    token_core = jnp.arange(chip_tokens, dtype=jnp.int32) // tokens
    sequence, row_of = chip_dest // length, chip_dest % length
    slot = token_core * ctx_count + row_of // rows
    slot_total = data_count * column_count * 2 * ctx_count
    slot_index = jnp.arange(slot_total, dtype=jnp.int32)[:, None]
    picking = (slot_index // (column_count * 2 * ctx_count) == sequence[None, :]) & (
        slot_index % (2 * ctx_count) == slot[None, :]
    )
    picking = picking.astype(bf16)
    lane = jnp.arange(128, dtype=jnp.int32)[None, :]
    code = row_of[:, None] + 1
    codes = jnp.where(lane == 0, code // 16, jnp.where(lane == 1, code % 16, 0)).astype(bf16)

    def between_chips(values):
        shaped = values.reshape(data_count * column_count, 2 * ctx_count, -1)
        moved = lax.all_to_all(shaped, ("dp", "y"), split_axis=0, concat_axis=0, tiled=True)
        return moved.reshape(values.shape)

    halves = rows // 2
    positions = (assign[:, None] * halves + jnp.arange(halves, dtype=jnp.int32)[None, :]).reshape(length)
    labels = docs[0].reshape(-1, halves)[assign].reshape(length)
    order = jnp.stack(
        [2 * (column ^ down) + (core ^ side) for down in range(column_count) for side in range(2)]
    )
    key_row = (order[:, None] * rows + jnp.arange(rows, dtype=jnp.int32)[None, :]).reshape(length)
    key_pos = positions.reshape(ctx_count, rows)[order].reshape(length)
    key_doc = labels.reshape(ctx_count, rows)[order].reshape(length)
    key_row = key_row.astype(f32) + 1.0
    keyed = (key_row[:, None], key_row[None, :], key_pos[:, None], key_doc[:, None])
    keyed += (key_pos[None, : 2 * rows], key_doc[None, : 2 * rows])

    def of_core(values, which):
        return lax.dynamic_slice_in_dim(values, which * tokens, tokens, 0)

    beside2, below2, far3, summing, query_parts, upstream_parts, keyed, picking, codes, own_squares, sibling_squares = close(
        (beside2, below2, far3, summing, query_parts, upstream_parts, keyed, picking, codes, own_squares, sibling_squares)
    )

    beside3, below3 = both(far3)
    visual = (visual32.astype(f32) + summing.astype(f32)).astype(bf16)
    blocks = [kv_weight, far1, beside0, beside1, below0, below1, corner0, corner1]
    part0, sums = project(table, own_rows, sibling_rows, visual, gain, blocks, 0, 16, ())
    beside3, below3, part0, sums, visual = close((beside3, below3, part0, sums, visual))

    corner2, corner3 = neighbor(beside2, "y", 1), neighbor(below3, "dp", 1)
    other0 = swap(part0)
    blocks = [far2, far3, beside2, beside3, below2, below3]
    part1, sums = project(table, own_rows, sibling_rows, visual, gain, blocks, 8, 16, (sums,))
    visual_squares = squares(visual)
    arrived = swap(jnp.concatenate([sibling_squares, own_squares, visual_squares]))
    square = jnp.concatenate([own_squares, sibling_squares, visual_squares]) + arrived
    scale = lax.rsqrt(square / width + epsilon)[:, None]
    own_visual, other_visual = of_core(visual, core), swap(of_core(visual, 1 - core))
    own_scale = jnp.concatenate([scale[:rows], of_core(scale[2 * rows :], core)], axis=0)
    corner2, corner3, part1, sums, other0, scale, own_visual, other_visual, own_scale = close(
        (corner2, corner3, part1, sums, other0, scale, own_visual, other_visual, own_scale)
    )
    part2, *sums = project(table, own_rows, sibling_rows, visual, gain, [corner2, corner3], 14, 16, (sums,))
    turned, turned_other = [part0, part1, part2], [other0]
    mine, theirs = sums
    received = swap(theirs)
    pair_chip, pair_tokens, leaving = finish_pairs(mine, received, scale, codes, picking, rows)
    pair_text = [pair_chip] + [neighbor(pair_chip, "y", down) for down in range(1, column_count)]
    pair_visual = between_chips(leaving)
    turned_other += [swap(after(part, (received,))) for part in turned[1:]]

    own_pairs = jnp.concatenate([pair_chip[:rows], of_core(pair_tokens, core)], axis=0)
    other_pairs = swap(jnp.concatenate([pair_chip[rows:], of_core(pair_tokens, 1 - core)], axis=0))

    out_a, out_b, grad_a, grad_b, pair_grad, *far_grads, visual_pair_grad, keep = attend_pair(
        query_parts, upstream_parts, pair_text, pair_visual, keyed
    )

    def heads_back(held, leaving):
        arrived = swap(leaving)
        return jnp.where(
            core == 0, jnp.concatenate([held, arrived], axis=1), jnp.concatenate([arrived, held], axis=1)
        )

    received = [neighbor(part, "y", down) for down, part in enumerate(far_grads, 1)]
    returned = between_chips(after(visual_pair_grad, turned_other))
    attention, query_grad = heads_back(out_a, out_b), heads_back(grad_a, grad_b)
    pair_grad, attention, query_grad = close((pair_grad, attention, query_grad))
    held, leaving = sum_grads(core_word, pair_grad, received, returned, picking, rows)
    hidden_grad, visual_grad = project_back(
        table, (held, swap(leaving)), (own_pairs, other_pairs), (turned, turned_other), text[0],
        (own_visual, other_visual), norm_gain[None, :], own_scale, keep,
    )
    return (attention[None], query_grad[None], hidden_grad[None], visual_grad)


def solution(mesh):
    data_count, ctx_count = mesh.shape["dp"], mesh.shape["ctx"]
    split = Mesh(mesh.devices.reshape(data_count, -1, 2), ("dp", "y", "core"))

    def call(*arrays):
        text, kv_weight, dest = arrays[5], arrays[7], arrays[4]
        devices = data_count * ctx_count
        rows = text.shape[1] // ctx_count
        fits = (
            ctx_count == 4
            and data_count == 8
            and (kv_weight.shape[0] // devices) % 128 == 0
            and dest.shape[0] // devices <= devices
            and rows % 128 == 0
        )
        if fits:
            whole, ctx, body, used = ("dp", "y", "core"), ("y", "core"), local_fast, split
        else:
            whole, ctx, body, used = ("dp", "ctx"), "ctx", local, mesh
        placed = (
            P("dp", None),
            P(),
            P(None, ctx),
            P(ctx, None),
            P(whole),
            P("dp", ctx, None),
            P(),
            P(whole, None),
            P("dp", ctx, None),
            P("dp", ctx, None),
            P(),
            P("dp", None),
        )
        return jax.shard_map(
            body,
            mesh=used,
            in_specs=placed,
            out_specs=(P("dp", ctx, None), P("dp", ctx, None), P("dp", ctx, None), P(whole, None)),
            check_vma=False,
        )(*arrays)

    return call
```

```python
import math

import jax
import jax.numpy as jnp
from jax import lax
from jax.experimental import pallas as pl
from jax.experimental.pallas import tpu as pltpu
from jax.sharding import Mesh
from jax.sharding import PartitionSpec as P

HEADS = 32
KVH = 4
HD = 128


epsilon = 1e-06


def merger_norm(patches, vit_gain):
    pieces = patches.astype(jnp.float32).reshape(patches.shape[0], 4, vit_gain.shape[0])
    center = pieces - jnp.mean(pieces, axis=-1, keepdims=True)
    spread = jnp.mean(center * center, axis=-1, keepdims=True)
    scaled = center * lax.rsqrt(spread + epsilon) * vit_gain
    return scaled.reshape(patches.shape[0], -1).astype(jnp.bfloat16)


def rms_scale(hidden32, norm_gain):
    square = jnp.mean(hidden32 * hidden32, axis=-1, keepdims=True)
    return hidden32 * lax.rsqrt(square + epsilon) * norm_gain


def attend(query_rows, pair_rows, upstream_rows, query_pos, query_doc, key_pos, key_doc):
    row_count = query_rows.shape[0]
    key_count = pair_rows.shape[0]
    group_size = HEADS // KVH
    score_scale = HD ** (-0.5)
    query_heads = query_rows.reshape(row_count, KVH, group_size, HD)
    key_heads = pair_rows[:, : KVH * HD].reshape(key_count, KVH, HD)
    value_heads = pair_rows[:, KVH * HD :].reshape(key_count, KVH, HD)
    scores = (
        jnp.einsum("qhgd,khd->hgqk", query_heads, key_heads, preferred_element_type=jnp.float32)
        * score_scale
    )
    allowed = (key_pos[None, :] <= query_pos[:, None]) & (key_doc[None, :] == query_doc[:, None])
    scores = jnp.where(allowed, scores, -jnp.inf)
    weights = jnp.exp(scores - jnp.max(scores, axis=-1, keepdims=True))
    weights = weights / jnp.sum(weights, axis=-1, keepdims=True)
    light_weights = weights.astype(jnp.bfloat16)
    output = jnp.einsum(
        "hgqk,khd->qhgd", light_weights, value_heads, preferred_element_type=jnp.float32
    )
    upstream = upstream_rows.reshape(row_count, KVH, group_size, HD)
    value_grad = jnp.einsum(
        "hgqk,qhgd->khd", light_weights, upstream, preferred_element_type=jnp.float32
    )
    weight_grad = jnp.einsum(
        "qhgd,khd->hgqk", upstream, value_heads, preferred_element_type=jnp.float32
    )
    inner_sum = jnp.sum(weights * weight_grad, axis=-1, keepdims=True)
    score_grad = (weights * (weight_grad - inner_sum) * score_scale).astype(jnp.bfloat16)
    query_grad = jnp.einsum(
        "hgqk,khd->qhgd", score_grad, key_heads, preferred_element_type=jnp.float32
    )
    key_grad = jnp.einsum(
        "hgqk,qhgd->khd", score_grad, query_heads, preferred_element_type=jnp.float32
    )
    output = output.reshape(row_count, HEADS * HD).astype(jnp.bfloat16)
    query_grad = query_grad.reshape(row_count, HEADS * HD).astype(jnp.bfloat16)
    return (
        output,
        query_grad,
        key_grad.reshape(key_count, KVH * HD),
        value_grad.reshape(key_count, KVH * HD),
    )


def local(
    patches,
    vit_gain,
    merge_up,
    merge_down,
    dest,
    text,
    norm_gain,
    kv_weight,
    queries,
    out_grad,
    assign,
    docs,
):
    ctx_count = lax.axis_size("ctx")
    data_count = lax.axis_size("dp")
    device_count = ctx_count * data_count
    token_rows = text.shape[1]
    visual_rows = dest.shape[0]
    capacity = max(1, visual_rows // device_count)
    slot_total = device_count * capacity
    normed = merger_norm(patches, vit_gain)
    inner_hidden = jax.nn.gelu(
        jnp.dot(normed, merge_up, preferred_element_type=jnp.float32), approximate=False
    ).astype(jnp.bfloat16)
    visual = lax.psum_scatter(
        jnp.dot(inner_hidden, merge_down, preferred_element_type=jnp.float32).astype(jnp.bfloat16),
        "ctx",
        scatter_dimension=0,
        tiled=True,
    )
    target = dest // token_rows
    local_row = dest % token_rows
    token_order = jnp.arange(visual_rows, dtype=jnp.int32)
    before = (target[:, None] == target[None, :]) & (token_order[None, :] < token_order[:, None])
    slot_index = target * capacity + jnp.sum(before.astype(jnp.int32), axis=1)
    picking = jnp.arange(slot_total, dtype=jnp.int32)[:, None] == slot_index[None, :]
    outgoing = jnp.dot(
        picking.astype(jnp.bfloat16), visual, preferred_element_type=jnp.float32
    ).astype(jnp.bfloat16)
    outgoing_rows = jnp.sum(jnp.where(picking, local_row[None, :] + 1, 0), axis=1) - 1
    arrived, arrived_rows = (
        lax.all_to_all(outgoing, ("dp", "ctx"), split_axis=0, concat_axis=0, tiled=True),
        lax.all_to_all(outgoing_rows, ("dp", "ctx"), split_axis=0, concat_axis=0, tiled=True),
    )
    placing = jnp.arange(token_rows, dtype=jnp.int32)[:, None] == arrived_rows[None, :]
    placed = jnp.dot(
        placing.astype(jnp.bfloat16), arrived, preferred_element_type=jnp.float32
    ).astype(jnp.bfloat16)
    marked = jnp.any(placing, axis=1)
    hidden = jnp.where(marked[:, None], placed, text[0])
    hidden32 = hidden.astype(jnp.float32)
    normed_hidden = rms_scale(hidden32, norm_gain).astype(jnp.bfloat16)
    projected = jnp.dot(
        normed_hidden,
        lax.all_gather(kv_weight, ("dp", "ctx"), axis=0, tiled=True),
        preferred_element_type=jnp.float32,
    )
    pairs_local = projected.astype(jnp.bfloat16)
    pairs_all = lax.all_gather(pairs_local, "ctx", axis=0, tiled=True)
    halves = token_rows // 2
    length = token_rows * ctx_count
    positions = (assign[:, None] * halves + jnp.arange(halves, dtype=jnp.int32)[None, :]).reshape(
        length
    )
    labels = docs[0].reshape(-1, halves)[assign].reshape(length)
    own_start = lax.axis_index("ctx") * token_rows
    query_pos = lax.dynamic_slice_in_dim(positions, own_start, token_rows, 0)
    query_doc = lax.dynamic_slice_in_dim(labels, own_start, token_rows, 0)
    attention, query_grad, key_grad, value_grad = attend(
        queries[0], pairs_all, out_grad[0], query_pos, query_doc, positions, labels
    )
    key_grad, value_grad = (
        lax.psum_scatter(
            key_grad.astype(jnp.bfloat16), "ctx", scatter_dimension=0, tiled=True
        ).astype(jnp.float32),
        lax.psum_scatter(
            value_grad.astype(jnp.bfloat16), "ctx", scatter_dimension=0, tiled=True
        ).astype(jnp.float32),
    )
    pair_grad = jnp.concatenate([key_grad, value_grad], axis=1).astype(jnp.bfloat16)
    contract = (((1,), (1,)), ((), ()))
    normed_grad = lax.dot_general(
        pair_grad,
        lax.all_gather(kv_weight, ("dp", "ctx"), axis=0, tiled=True),
        contract,
        preferred_element_type=jnp.float32,
    )
    forward_value, pullback = jax.vjp(lambda values: rms_scale(values, norm_gain), hidden32)
    full_grad = pullback(normed_grad)[0]
    hidden_grad = jnp.where(marked[:, None], jnp.float32(0.0), full_grad).astype(jnp.bfloat16)
    returning = jnp.dot(
        placing.T.astype(jnp.bfloat16),
        full_grad.astype(jnp.bfloat16),
        preferred_element_type=jnp.float32,
    ).astype(jnp.bfloat16)
    returned = lax.all_to_all(returning, ("dp", "ctx"), split_axis=0, concat_axis=0, tiled=True)
    visual_grad = jnp.dot(
        picking.T.astype(jnp.bfloat16), returned, preferred_element_type=jnp.float32
    ).astype(jnp.bfloat16)
    return (attention[None], query_grad[None], hidden_grad[None], visual_grad)


def neighbor(values, axis, offset):
    count = lax.axis_size(axis)
    return lax.ppermute(values, axis, [(d, d ^ offset) for d in range(count)])


def after(values, earlier):
    return lax.optimization_barrier((values, *earlier))[0]


def swap(values):
    return neighbor(values, "core", 1)


def vmem_params(size=16):
    return pltpu.CompilerParams(vmem_limit_bytes=size * 1024 * 1024)


def brief():
    return pl.CostEstimate(flops=1, bytes_accessed=1, transcendentals=0)


def smem():
    return pl.BlockSpec(memory_space=pltpu.SMEM)


def store_halves(core, values, own_ref, other_ref, block):
    def put(own_parity):
        for j in range(values.shape[1] // (2 * block)):
            even = values[:, 2 * j * block : (2 * j + 1) * block]
            odd = values[:, (2 * j + 1) * block : (2 * j + 2) * block]
            own_ref[:, j * block : (j + 1) * block] = odd if own_parity else even
            other_ref[:, j * block : (j + 1) * block] = even if own_parity else odd

    @pl.when(core == 0)
    def _():
        put(0)

    @pl.when(core != 0)
    def _():
        put(1)


def split_halves(values, core, block):
    rows, width = values.shape
    step = 8 * block

    def kernel(core_ref, value_ref, own_ref, other_ref):
        store_halves(core_ref[0], value_ref[...], own_ref, other_ref, block)

    half = jax.ShapeDtypeStruct((rows, width // 2), values.dtype)
    out = pl.BlockSpec((rows, step // 2), lambda j: (0, j))
    return pl.pallas_call(
        kernel,
        grid=(width // step,),
        in_specs=[smem(), pl.BlockSpec((rows, step), lambda j: (0, j))],
        out_specs=[out, out],
        out_shape=[half, half],
        compiler_params=vmem_params(56),
        cost_estimate=brief(),
        name="split_halves",
    )(core, values)


def down_halves(inner_hidden, merge_down, core, block):
    rows, depth = inner_hidden.shape
    width = merge_down.shape[1]
    step = 4 * block
    count = width // step

    def kernel(core_ref, hidden_ref, weight_ref, own_ref, other_ref, buffers, sems):
        copies = [
            pltpu.make_async_copy(weight_ref.at[:, j * step : (j + 1) * step], buffers.at[j], sems.at[j])
            for j in range(count)
        ]
        for copy in copies:
            copy.start()
        for j in range(count):
            copies[j].wait()
            product = jnp.dot(hidden_ref[...], buffers[j], preferred_element_type=jnp.float32)
            place = slice(j * step // 2, (j + 1) * step // 2)
            store_halves(
                core_ref[0], product.astype(jnp.bfloat16), own_ref.at[:, place], other_ref.at[:, place], block
            )

    vmem = pl.BlockSpec(memory_space=pltpu.VMEM)
    half = jax.ShapeDtypeStruct((rows, width // 2), jnp.bfloat16)
    return pl.pallas_call(
        kernel,
        in_specs=[smem(), vmem, pl.BlockSpec(memory_space=pl.ANY)],
        out_specs=[vmem, vmem],
        out_shape=[half, half],
        scratch_shapes=[
            pltpu.VMEM((count, depth, step), jnp.bfloat16),
            pltpu.SemaphoreType.DMA((count,)),
        ],
        compiler_params=vmem_params(56),
        cost_estimate=brief(),
        name="merge_down",
    )(core, inner_hidden, merge_down)


def project(table, own_rows, sibling_rows, visual, gain, blocks, first, count, earlier):
    rows = own_rows.shape[0]
    total = 2 * rows + visual.shape[0]
    block, width = blocks[0].shape
    quarter = width // 4
    size = len(blocks)
    last = first + size == count
    flag = table.shape[0] - 1

    def kernel(table_ref, own_ref, sibling_ref, visual_ref, gain_ref, *rest):
        block_refs = rest[:size]
        before_refs = rest[size : size + len(earlier)]
        turned_ref, *outs, turning, sems = rest[size + len(earlier) :]
        total_ref = outs[-1]
        turns = []
        for r in range(size):
            columns = pl.ds(pl.multiple_of(table_ref[first + r] * block, block), block)
            gains = gain_ref[:, columns]
            part = jnp.concatenate(
                [
                    (ref[:, columns].astype(jnp.float32) * gains).astype(jnp.bfloat16)
                    for ref in (own_ref, sibling_ref, visual_ref)
                ],
                axis=0,
            )
            values = block_refs[r][...]
            product = jnp.dot(part, values, preferred_element_type=jnp.float32)
            if r > 0:
                total_ref[...] += product
            elif earlier:
                total_ref[...] = before_refs[0][...] + product
            else:
                total_ref[...] = product
            turning[r] = values.T
            turn = pltpu.make_async_copy(turning.at[r], turned_ref.at[r], sems.at[r])
            turn.start()
            turns.append(turn)
        if last:
            mine_ref, theirs_ref = outs[:2]

            def put(parity):
                for piece in range(2):
                    start = 2 * piece * quarter
                    mine = slice(start + parity * quarter, start + (parity + 1) * quarter)
                    theirs = slice(start + (1 - parity) * quarter, start + (2 - parity) * quarter)
                    place = slice(piece * quarter, (piece + 1) * quarter)
                    mine_ref[:, place] = total_ref[:, mine]
                    theirs_ref[:rows, place] = total_ref[rows : 2 * rows, theirs].astype(jnp.bfloat16)
                    theirs_ref[rows : 2 * rows, place] = total_ref[:rows, theirs].astype(jnp.bfloat16)
                    theirs_ref[2 * rows :, place] = total_ref[2 * rows :, theirs].astype(jnp.bfloat16)

            @pl.when(table_ref[flag] == 0)
            def _():
                put(0)

            @pl.when(table_ref[flag] != 0)
            def _():
                put(1)

        for turn in turns:
            turn.wait()

    vmem = pl.BlockSpec(memory_space=pltpu.VMEM)
    shape = jax.ShapeDtypeStruct
    sums, scratch = [shape((total, width), jnp.float32)], []
    if last:
        sums = [shape((total, width // 2), jnp.float32), shape((total, width // 2), jnp.bfloat16)]
        scratch = [pltpu.VMEM((total, width), jnp.float32)]
    return pl.pallas_call(
        kernel,
        in_specs=[smem()] + [vmem] * (4 + size + len(earlier)),
        out_specs=[pl.BlockSpec(memory_space=pl.ANY)] + [vmem] * len(sums),
        out_shape=[shape((size, width, block), jnp.bfloat16)] + sums,
        scratch_shapes=scratch + [pltpu.VMEM((size, width, block), jnp.bfloat16), pltpu.SemaphoreType.DMA((size,))],
        compiler_params=vmem_params(24 if last else 56),
        cost_estimate=brief(),
        name="project_pairs",
    )(table, own_rows, sibling_rows, visual, gain, *blocks, *earlier)


def finish_pairs(mine, received, scale, codes, picking, rows):
    total, width = mine.shape
    slots, tokens = picking.shape

    def kernel(mine_ref, received_ref, scale_ref, codes_ref, picking_ref, chip_ref, token_ref, slot_ref):
        pairs = (mine_ref[...] + received_ref[...].astype(jnp.float32)) * scale_ref[:, :1]
        pairs = pairs.astype(jnp.bfloat16)
        chip_ref[...] = pairs[: 2 * rows]
        token_ref[...] = pairs[2 * rows :]
        placing = picking_ref[...]
        slot_ref[:, :width] = jnp.dot(
            placing, pairs[2 * rows :], preferred_element_type=jnp.float32
        ).astype(jnp.bfloat16)
        slot_ref[:, width:] = jnp.dot(
            placing, codes_ref[...], preferred_element_type=jnp.float32
        ).astype(jnp.bfloat16)

    shape = jax.ShapeDtypeStruct
    return pl.pallas_call(
        kernel,
        out_shape=[
            shape((2 * rows, width), jnp.bfloat16),
            shape((tokens, width), jnp.bfloat16),
            shape((slots, width + codes.shape[1]), jnp.bfloat16),
        ],
        compiler_params=vmem_params(56),
        cost_estimate=brief(),
        name="finish_pairs",
    )(mine, received, scale, codes, picking)


def sum_grads(core, pair_grad, received, returned, picking, rows):
    width = pair_grad.shape[1]
    tokens = picking.shape[1] // 2

    def kernel(core_ref, grad_ref, returned_ref, picking_ref, *rest):
        held_ref, sent_ref = rest[-2:]
        text = grad_ref[...].astype(jnp.float32)
        for ref in rest[:-2]:
            text = text + ref[...].astype(jnp.float32)
        text = text.astype(jnp.bfloat16)
        held_ref[:rows] = text[:rows]
        sent_ref[:rows] = text[rows:]
        token = lax.dot_general(
            picking_ref[...], returned_ref[...], (((0,), (0,)), ((), ())), preferred_element_type=jnp.float32
        ).astype(jnp.bfloat16)

        @pl.when(core_ref[0] == 0)
        def _():
            held_ref[rows:] = token[:tokens]
            sent_ref[rows:] = token[tokens:]

        @pl.when(core_ref[0] != 0)
        def _():
            held_ref[rows:] = token[tokens:]
            sent_ref[rows:] = token[:tokens]

    def whole(values):
        return pl.BlockSpec(values.shape, lambda j: (0, 0))

    half = jax.ShapeDtypeStruct((rows + tokens, width), jnp.bfloat16)
    return pl.pallas_call(
        kernel,
        grid=(1,),
        in_specs=[smem(), pl.BlockSpec((2 * rows, width), lambda j: (0, 0)), whole(returned), whole(picking)]
        + [whole(part) for part in received],
        out_specs=[whole(jax.ShapeDtypeStruct((rows + tokens, width), jnp.bfloat16))] * 2,
        out_shape=[half, half],
        compiler_params=vmem_params(56),
        cost_estimate=brief(),
        name="sum_grads",
    )(core, pair_grad, returned, picking, *received)


def project_back(table, grads, pairs, turned, text, visual, gain, scale, keep):
    rows, width = text.shape
    tokens = visual[0].shape[0]
    total = rows + tokens
    pair_width, block = turned[0][0].shape[1:]
    quarter = pair_width // 4
    flag = table.shape[0] - 1
    pieces = len(turned[0])
    count = sum(part.shape[0] for part in turned[0])
    groups, first = [], 0
    for piece in range(pieces):
        size = turned[0][piece].shape[0]
        for low in range(0, size, 4):
            high = min(size, low + 4)
            groups.append((piece, low, high, first + low))
        first += size

    def kernel(
        table_ref, grad_ref, grad_other_ref, pair_ref, pair_other_ref, text_ref, visual_ref, visual_other_ref,
        gain_ref, scale_ref, keep_ref, *rest,
    ):
        turned_refs, (hidden_ref, token_ref, joined, buffers, sems) = rest[: 2 * pieces], rest[2 * pieces :]
        core = table_ref[flag]
        copies = []
        for at, (piece, low, high, place) in enumerate(groups):
            copies.append(
                [
                    pltpu.make_async_copy(
                        turned_refs[side * pieces + piece].at[low:high],
                        buffers.at[side, place : place + high - low],
                        sems.at[at, side],
                    )
                    for side in range(2)
                ]
            )
        for pair in copies[:2]:
            for copy in pair:
                copy.start()

        def join(parity):
            for piece in range(2):
                place = slice(piece * quarter, (piece + 1) * quarter)
                start = (2 * piece + parity) * quarter
                joined[:, start : start + quarter] = grad_ref[:, place]
                start = (2 * piece + 1 - parity) * quarter
                joined[:, start : start + quarter] = grad_other_ref[:, place]

        @pl.when(core == 0)
        def _():
            join(0)

        @pl.when(core != 0)
        def _():
            join(1)

        inner = jnp.zeros((total, 1), jnp.float32)
        for left, right in ((grad_ref, pair_ref), (grad_other_ref, pair_other_ref)):
            inner = inner + jnp.sum(
                left[...].astype(jnp.float32) * right[...].astype(jnp.float32), axis=1, keepdims=True
            )
        scales = scale_ref[...]
        backs = inner * scales * scales * (1.0 / width)
        keeps = keep_ref[:rows] > 0
        for at, (piece, low, high, first) in enumerate(groups):
            for copy in copies[at]:
                copy.wait()
            if at + 2 < len(groups):
                for copy in copies[at + 2]:
                    copy.start()
            for r in range(first, first + high - low):
                spot = table_ref[r]
                inside = pl.ds(pl.multiple_of(spot * block, block), block)
                for half, (side, token_in) in enumerate(((core, visual_ref), (1 - core, visual_other_ref))):
                    place = pl.ds(pl.multiple_of((2 * spot + side) * block, block), block)
                    normed_grad = jnp.dot(joined[...], buffers[half, r], preferred_element_type=jnp.float32)
                    full = normed_grad * scales * gain_ref[:, place]
                    hidden = full[:rows] - text_ref[:, place].astype(jnp.float32) * backs[:rows]
                    hidden_ref[:, place] = jnp.where(keeps, hidden, 0.0).astype(jnp.bfloat16)
                    token = full[rows:] - token_in[:, inside].astype(jnp.float32) * backs[rows:]
                    token_ref[:, place] = token.astype(jnp.bfloat16)

    vmem = pl.BlockSpec(memory_space=pltpu.VMEM)
    shape = jax.ShapeDtypeStruct
    return pl.pallas_call(
        kernel,
        in_specs=[smem()] + [vmem] * 10 + [pl.BlockSpec(memory_space=pl.ANY)] * (2 * pieces),
        out_specs=[vmem, vmem],
        out_shape=[shape((rows, width), jnp.bfloat16), shape((tokens, width), jnp.bfloat16)],
        scratch_shapes=[
            pltpu.VMEM((total, pair_width), jnp.bfloat16),
            pltpu.VMEM((2, count, pair_width, block), jnp.bfloat16),
            pltpu.SemaphoreType.DMA((len(groups), 2)),
        ],
        compiler_params=vmem_params(56),
        cost_estimate=brief(),
        name="project_back",
    )(table, *grads, *pairs, text, *visual, gain, scale, keep, *turned[0], *turned[1])


def attend_pair(queries, upstream, pair_text, pair_visual, keyed):
    rows, width = queries[0].shape
    length, pair_width = pair_text[0].shape[0] * len(pair_text), pair_text[0].shape[1]
    slots = pair_visual.shape[0]
    own_kv = pair_width // (2 * HD)
    heads = width // HD
    group = heads // own_kv
    step_heads = group
    steps = heads // step_heads
    score_scale = HD ** (-0.5)
    f32, bf16 = jnp.float32, jnp.bfloat16

    def kernel(
        qa, qb, ua, ub, visual_ref, row_s, row_l, pos_ref, doc_ref, qpos_ref, qdoc_ref, *rest,
    ):
        text_refs = rest[: len(pair_text)]
        oa, ob, ga, gb, *grad_refs, grad_visual_ref, keep_ref, heads_ref, turned_ref, bias_ref, total_ref = rest[
            len(pair_text) :
        ]
        step = pl.program_id(0)

        @pl.when(step == 0)
        def _():
            codes = visual_ref[:, pair_width:].astype(f32).T
            placing = jnp.where(row_s[...] == codes[0:1] * 16.0 + codes[1:2], 1.0, 0.0).astype(f32)
            placed = jnp.dot(placing.astype(bf16), visual_ref[:, :pair_width], preferred_element_type=f32)
            marked = jnp.max(placing, axis=1, keepdims=True)
            keep_ref[...] = 1.0 - marked
            texts = jnp.concatenate([ref[...].astype(f32) for ref in text_refs], axis=0)
            pairs = jnp.where(marked > 0, placed, texts)
            for j in range(2 * own_kv):
                piece = pairs[:, j * HD : (j + 1) * HD]
                heads_ref[j] = piece.astype(bf16)
                turned_ref[j] = piece.T.astype(bf16)
            allowed = (pos_ref[...] <= qpos_ref[...]) & (doc_ref[...] == qdoc_ref[...])
            bias_ref[...] = jnp.where(allowed, 0.0, -jnp.inf).astype(f32).T
            total_ref[...] = jnp.zeros_like(total_ref)

        head = (step * step_heads) // group
        keys, values = heads_ref[head], heads_ref[own_kv + head]
        keys_turned, values_turned = turned_ref[head], turned_ref[own_kv + head]
        lights, score_grads, query_list, ups = [], [], [], []
        for h in range(step_heads):
            lanes = slice(h * HD, (h + 1) * HD)
            query = jnp.concatenate([qa[:, lanes], qb[:, lanes]], axis=0)
            up = jnp.concatenate([ua[:, lanes], ub[:, lanes]], axis=0)
            scores = jnp.dot(query, keys_turned, preferred_element_type=f32)
            weight_grad = jnp.dot(up, values_turned, preferred_element_type=f32)
            scores = scores * (score_scale * math.log2(math.e)) + bias_ref[...]
            weights = jnp.exp2(scores - jnp.max(scores, axis=1, keepdims=True))
            weights = weights * (1.0 / jnp.sum(weights, axis=1, keepdims=True))
            light = weights.astype(bf16)
            inner = jnp.sum(weights * weight_grad, axis=1, keepdims=True)
            score_grad = (weights * (weight_grad - inner)).astype(bf16)
            output = jnp.dot(light, values, preferred_element_type=f32).astype(bf16)
            oa[:, lanes] = output[:rows]
            ob[:, lanes] = output[rows:]
            query_grad = (jnp.dot(score_grad, keys, preferred_element_type=f32) * score_scale).astype(bf16)
            ga[:, lanes] = query_grad[:rows]
            gb[:, lanes] = query_grad[rows:]
            lights.append(light)
            score_grads.append(score_grad)
            query_list.append(query)
            ups.append(up)
        up, light = jnp.concatenate(ups, axis=0).T, jnp.concatenate(lights, axis=0)
        total_ref[own_kv + head] += jnp.dot(up, light, preferred_element_type=f32)
        query, score_grad = jnp.concatenate(query_list, axis=0).T, jnp.concatenate(score_grads, axis=0)
        total_ref[head] += jnp.dot(query, score_grad, preferred_element_type=f32) * score_scale

        @pl.when(step == steps - 1)
        def _():
            codes = visual_ref[:, pair_width : pair_width + 2].astype(f32)
            lifting = jnp.where(codes[:, 0:1] * 16.0 + codes[:, 1:2] == row_l[...], 1.0, 0.0).astype(bf16)
            for j in range(2 * own_kv):
                piece = total_ref[j].T.astype(bf16)
                place = slice(j * HD, (j + 1) * HD)
                for i, ref in enumerate(grad_refs):
                    ref[:, place] = piece[i * ref.shape[0] : (i + 1) * ref.shape[0]]
                grad_visual_ref[:, place] = jnp.dot(lifting, piece, preferred_element_type=f32).astype(bf16)

    part = pl.BlockSpec((rows, step_heads * HD), lambda j: (0, j))
    vmem = pl.BlockSpec(memory_space=pltpu.VMEM)
    shape = jax.ShapeDtypeStruct
    return pl.pallas_call(
        kernel,
        grid=(steps,),
        in_specs=[part] * 4 + [vmem] * (7 + len(pair_text)),
        out_specs=[part] * 4 + [vmem] * (2 + len(pair_text)),
        out_shape=[shape((rows, width), bf16)] * 4
        + [shape(x.shape, bf16) for x in pair_text]
        + [shape((slots, pair_width), bf16), shape((length, 1), f32)],
        scratch_shapes=[
            pltpu.VMEM((2 * own_kv, length, HD), bf16),
            pltpu.VMEM((2 * own_kv, HD, length), bf16),
            pltpu.VMEM((2 * rows, length), f32),
            pltpu.VMEM((2 * own_kv, HD, length), f32),
        ],
        compiler_params=vmem_params(56),
        cost_estimate=brief(),
        name="attend",
    )(
        *queries,
        *upstream,
        pair_visual,
        *keyed,
        *pair_text,
    )


def local_fast(
    patches, vit_gain, merge_up, merge_down, dest, text, norm_gain, kv_weight, queries, out_grad, assign, docs
):
    f32, bf16 = jnp.float32, jnp.bfloat16
    data_count, column_count = lax.axis_size("dp"), lax.axis_size("y")
    ctx_count = 2 * column_count
    data, column, core = lax.axis_index("dp"), lax.axis_index("y"), lax.axis_index("core")
    rows, width = text.shape[1], text.shape[2]
    tokens = dest.shape[0]
    block = kv_weight.shape[0]
    length = rows * ctx_count
    core_word = core[None].astype(jnp.int32)

    def line(values, pairs):
        return lax.ppermute(values, "dp", [(2 * p + low, 2 * q + low) for p, q in pairs for low in range(2)])

    def both(values):
        return neighbor(values, "dp", 1), neighbor(values, "y", 1)

    close = lax.optimization_barrier
    swapped = [(0, 1), (1, 0), (2, 3), (3, 2)]
    middle, outward = [(1, 2), (2, 1)], [(1, 0), (2, 3)]
    far_index = data // 2
    is_middle = (far_index == 1) | (far_index == 2)
    hops = [0, 1, jnp.where(is_middle, 3, 2), jnp.where(is_middle, 2, 3)]
    owners = [
        ((far_index ^ hops[i + j]) * 2 + ((data % 2) ^ along)) * column_count + (column ^ down)
        for i in (0, 2)
        for along, down in ((0, 0), (1, 0), (0, 1), (1, 1))
        for j in range(2)
    ]
    table = jnp.stack(owners + [core]).astype(jnp.int32)
    gain = lax.dynamic_index_in_dim(
        norm_gain.reshape(-1, 2, block), core, axis=1, keepdims=False
    ).reshape(1, width // 2)
    query_width = queries.shape[2] // 2
    chip_tokens = 2 * tokens

    beside0, below0 = both(kv_weight)
    far1, across = line(kv_weight, swapped), line(kv_weight, middle)
    vectors = []
    for j in range(patches.shape[1] // vit_gain.shape[0]):
        piece = lax.slice_in_dim(patches, j * vit_gain.shape[0], (j + 1) * vit_gain.shape[0], axis=1)
        center = piece.astype(f32)
        center = center - jnp.mean(center, axis=-1, keepdims=True)
        spread = jnp.mean(center * center, axis=-1, keepdims=True)
        vectors.append((center * lax.rsqrt(spread + epsilon) * vit_gain).astype(bf16))
    normed = jnp.concatenate(vectors, axis=1)
    inner_hidden = jax.nn.gelu(
        jnp.dot(normed, merge_up, preferred_element_type=f32), approximate=False
    ).astype(bf16)
    rows_in = text[0]
    beside0, below0, far1, across, inner_hidden, rows_in, core_word, table, gain = close(
        (beside0, below0, far1, across, inner_hidden, rows_in, core_word, table, gain)
    )

    beside1, below1 = both(far1)
    across2, ends1 = line(far1, middle), line(across, outward)
    merged, merged_other = down_halves(inner_hidden, merge_down, core_word, block)
    beside1, below1, across2, ends1, merged, merged_other, rows_in, core_word = close(
        (beside1, below1, across2, ends1, merged, merged_other, rows_in, core_word)
    )

    corner0, corner1 = neighbor(beside0, "y", 1), neighbor(below1, "dp", 1)
    ends2 = line(across2, outward)
    arriving = swap(merged_other)
    own_rows, other_part = split_halves(rows_in, core_word, block)
    sibling_rows = swap(other_part)
    far2 = jnp.where(is_middle, across, ends1)
    merged = (merged.astype(f32) + arriving.astype(f32)).astype(bf16)
    visual32 = lax.dynamic_slice_in_dim(merged, column * chip_tokens, chip_tokens, 0)
    leaving = lax.dynamic_slice_in_dim(merged, (column ^ 1) * chip_tokens, chip_tokens, 0)
    summing = neighbor(leaving, "y", 1)
    query_in, upstream_in = queries[0], out_grad[0]
    corner0, corner1, ends2, own_rows, sibling_rows, far2, visual32, summing = close(
        (corner0, corner1, ends2, own_rows, sibling_rows, far2, visual32, summing)
    )
    query_in, upstream_in, dest, assign, docs, ends2 = close((query_in, upstream_in, dest, assign, docs, ends2))

    def heads_of(values):
        mine = lax.dynamic_slice_in_dim(values, core * query_width, query_width, 1)
        theirs = lax.dynamic_slice_in_dim(values, (1 - core) * query_width, query_width, 1)
        return mine, theirs

    beside2, below2 = both(far2)
    far3 = jnp.where(is_middle, across2, ends2)
    query_parts, upstream_parts = heads_of(query_in), heads_of(upstream_in)
    query_parts = (query_parts[0], swap(query_parts[1]))
    upstream_parts = (upstream_parts[0], swap(upstream_parts[1]))

    def squares(values):
        values = values.astype(f32)
        return jnp.sum(values * values, axis=1)

    own_squares, sibling_squares = squares(own_rows), squares(sibling_rows)

    dest_other = swap(dest)
    chip_dest = jnp.where(
        core == 0, jnp.concatenate([dest, dest_other]), jnp.concatenate([dest_other, dest])
    )
    token_core = jnp.arange(chip_tokens, dtype=jnp.int32) // tokens
    sequence, row_of = chip_dest // length, chip_dest % length
    slot = token_core * ctx_count + row_of // rows
    slot_total = data_count * column_count * 2 * ctx_count
    slot_index = jnp.arange(slot_total, dtype=jnp.int32)[:, None]
    picking = (slot_index // (column_count * 2 * ctx_count) == sequence[None, :]) & (
        slot_index % (2 * ctx_count) == slot[None, :]
    )
    picking = picking.astype(bf16)
    lane = jnp.arange(128, dtype=jnp.int32)[None, :]
    code = row_of[:, None] + 1
    codes = jnp.where(lane == 0, code // 16, jnp.where(lane == 1, code % 16, 0)).astype(bf16)

    def between_chips(values):
        shaped = values.reshape(data_count * column_count, 2 * ctx_count, -1)
        moved = lax.all_to_all(shaped, ("dp", "y"), split_axis=0, concat_axis=0, tiled=True)
        return moved.reshape(values.shape)

    halves = rows // 2
    positions = (assign[:, None] * halves + jnp.arange(halves, dtype=jnp.int32)[None, :]).reshape(length)
    labels = docs[0].reshape(-1, halves)[assign].reshape(length)
    order = jnp.stack(
        [2 * (column ^ down) + (core ^ side) for down in range(column_count) for side in range(2)]
    )
    key_row = (order[:, None] * rows + jnp.arange(rows, dtype=jnp.int32)[None, :]).reshape(length)
    key_pos = positions.reshape(ctx_count, rows)[order].reshape(length)
    key_doc = labels.reshape(ctx_count, rows)[order].reshape(length)
    key_row = key_row.astype(f32) + 1.0
    keyed = (key_row[:, None], key_row[None, :], key_pos[:, None], key_doc[:, None])
    keyed += (key_pos[None, : 2 * rows], key_doc[None, : 2 * rows])

    def of_core(values, which):
        return lax.dynamic_slice_in_dim(values, which * tokens, tokens, 0)

    beside2, below2, far3, summing, query_parts, upstream_parts, keyed, picking, codes, own_squares, sibling_squares = close(
        (beside2, below2, far3, summing, query_parts, upstream_parts, keyed, picking, codes, own_squares, sibling_squares)
    )

    beside3, below3 = both(far3)
    visual = (visual32.astype(f32) + summing.astype(f32)).astype(bf16)
    blocks = [kv_weight, far1, beside0, beside1, below0, below1, corner0, corner1]
    part0, sums = project(table, own_rows, sibling_rows, visual, gain, blocks, 0, 16, ())
    beside3, below3, part0, sums, visual = close((beside3, below3, part0, sums, visual))

    corner2, corner3 = neighbor(beside2, "y", 1), neighbor(below3, "dp", 1)
    other0 = swap(part0)
    blocks = [far2, far3, beside2, beside3, below2, below3]
    part1, sums = project(table, own_rows, sibling_rows, visual, gain, blocks, 8, 16, (sums,))
    visual_squares = squares(visual)
    arrived = swap(jnp.concatenate([sibling_squares, own_squares, visual_squares]))
    square = jnp.concatenate([own_squares, sibling_squares, visual_squares]) + arrived
    scale = lax.rsqrt(square / width + epsilon)[:, None]
    wide_scale = jnp.broadcast_to(scale, (scale.shape[0], 128))
    own_visual, other_visual = of_core(visual, core), swap(of_core(visual, 1 - core))
    own_scale = jnp.concatenate([scale[:rows], of_core(scale[2 * rows :], core)], axis=0)
    corner2, corner3, part1, sums, other0, wide_scale, own_visual, other_visual, own_scale = close(
        (corner2, corner3, part1, sums, other0, wide_scale, own_visual, other_visual, own_scale)
    )
    part2, *sums = project(table, own_rows, sibling_rows, visual, gain, [corner2, corner3], 14, 16, (sums,))
    turned, turned_other = [part0, part1, part2], [other0]
    mine, theirs = sums
    received = swap(theirs)
    pair_chip, pair_tokens, leaving = finish_pairs(mine, received, wide_scale, codes, picking, rows)
    pair_text = [pair_chip] + [neighbor(pair_chip, "y", down) for down in range(1, column_count)]
    pair_visual = between_chips(leaving)
    turned_other += [swap(after(part, (received,))) for part in turned[1:]]

    own_pairs = jnp.concatenate([pair_chip[:rows], of_core(pair_tokens, core)], axis=0)
    other_pairs = swap(jnp.concatenate([pair_chip[rows:], of_core(pair_tokens, 1 - core)], axis=0))

    pair_text[0] = after(pair_text[0], (own_pairs, other_pairs, turned_other))
    out_a, out_b, grad_a, grad_b, pair_grad, *far_grads, visual_pair_grad, keep = attend_pair(
        query_parts, upstream_parts, pair_text, pair_visual, keyed
    )

    def heads_back(held, leaving):
        arrived = swap(leaving)
        return jnp.where(
            core == 0, jnp.concatenate([held, arrived], axis=1), jnp.concatenate([arrived, held], axis=1)
        )

    received = [neighbor(part, "y", down) for down, part in enumerate(far_grads, 1)]
    returned = between_chips(visual_pair_grad)
    attention, query_grad = heads_back(out_a, out_b), heads_back(grad_a, grad_b)
    pair_grad, attention, query_grad = close((pair_grad, attention, query_grad))
    held, leaving = sum_grads(core_word, pair_grad, received, returned, picking, rows)
    hidden_grad, visual_grad = project_back(
        table, (held, swap(leaving)), (own_pairs, other_pairs), (turned, turned_other), text[0],
        (own_visual, other_visual), norm_gain[None, :], own_scale, keep,
    )
    return (attention[None], query_grad[None], hidden_grad[None], visual_grad)


def solution(mesh):
    data_count, ctx_count = mesh.shape["dp"], mesh.shape["ctx"]
    split = Mesh(mesh.devices.reshape(data_count, -1, 2), ("dp", "y", "core"))

    def call(*arrays):
        text, kv_weight, dest = arrays[5], arrays[7], arrays[4]
        devices = data_count * ctx_count
        rows = text.shape[1] // ctx_count
        fits = (
            ctx_count == 4
            and data_count == 8
            and (kv_weight.shape[0] // devices) % 128 == 0
            and dest.shape[0] // devices <= devices
            and rows % 128 == 0
        )
        if fits:
            whole, ctx, body, used = ("dp", "y", "core"), ("y", "core"), local_fast, split
        else:
            whole, ctx, body, used = ("dp", "ctx"), "ctx", local, mesh
        placed = (
            P("dp", None),
            P(),
            P(None, ctx),
            P(ctx, None),
            P(whole),
            P("dp", ctx, None),
            P(),
            P(whole, None),
            P("dp", ctx, None),
            P("dp", ctx, None),
            P(),
            P("dp", None),
        )
        return jax.shard_map(
            body,
            mesh=used,
            in_specs=placed,
            out_specs=(P("dp", ctx, None), P("dp", ctx, None), P("dp", ctx, None), P(whole, None)),
            check_vma=False,
        )(*arrays)

    return call
```

```python
import math

import jax
import jax.numpy as jnp
from jax import lax
from jax.experimental import pallas as pl
from jax.experimental.pallas import tpu as pltpu
from jax.sharding import Mesh
from jax.sharding import PartitionSpec as P

HEADS = 32
KVH = 4
HD = 128


epsilon = 1e-06


def merger_norm(patches, vit_gain):
    pieces = patches.astype(jnp.float32).reshape(patches.shape[0], 4, vit_gain.shape[0])
    center = pieces - jnp.mean(pieces, axis=-1, keepdims=True)
    spread = jnp.mean(center * center, axis=-1, keepdims=True)
    scaled = center * lax.rsqrt(spread + epsilon) * vit_gain
    return scaled.reshape(patches.shape[0], -1).astype(jnp.bfloat16)


def rms_scale(hidden32, norm_gain):
    square = jnp.mean(hidden32 * hidden32, axis=-1, keepdims=True)
    return hidden32 * lax.rsqrt(square + epsilon) * norm_gain


def attend(query_rows, pair_rows, upstream_rows, query_pos, query_doc, key_pos, key_doc):
    row_count = query_rows.shape[0]
    key_count = pair_rows.shape[0]
    group_size = HEADS // KVH
    score_scale = HD ** (-0.5)
    query_heads = query_rows.reshape(row_count, KVH, group_size, HD)
    key_heads = pair_rows[:, : KVH * HD].reshape(key_count, KVH, HD)
    value_heads = pair_rows[:, KVH * HD :].reshape(key_count, KVH, HD)
    scores = (
        jnp.einsum("qhgd,khd->hgqk", query_heads, key_heads, preferred_element_type=jnp.float32)
        * score_scale
    )
    allowed = (key_pos[None, :] <= query_pos[:, None]) & (key_doc[None, :] == query_doc[:, None])
    scores = jnp.where(allowed, scores, -jnp.inf)
    weights = jnp.exp(scores - jnp.max(scores, axis=-1, keepdims=True))
    weights = weights / jnp.sum(weights, axis=-1, keepdims=True)
    light_weights = weights.astype(jnp.bfloat16)
    output = jnp.einsum(
        "hgqk,khd->qhgd", light_weights, value_heads, preferred_element_type=jnp.float32
    )
    upstream = upstream_rows.reshape(row_count, KVH, group_size, HD)
    value_grad = jnp.einsum(
        "hgqk,qhgd->khd", light_weights, upstream, preferred_element_type=jnp.float32
    )
    weight_grad = jnp.einsum(
        "qhgd,khd->hgqk", upstream, value_heads, preferred_element_type=jnp.float32
    )
    inner_sum = jnp.sum(weights * weight_grad, axis=-1, keepdims=True)
    score_grad = (weights * (weight_grad - inner_sum) * score_scale).astype(jnp.bfloat16)
    query_grad = jnp.einsum(
        "hgqk,khd->qhgd", score_grad, key_heads, preferred_element_type=jnp.float32
    )
    key_grad = jnp.einsum(
        "hgqk,qhgd->khd", score_grad, query_heads, preferred_element_type=jnp.float32
    )
    output = output.reshape(row_count, HEADS * HD).astype(jnp.bfloat16)
    query_grad = query_grad.reshape(row_count, HEADS * HD).astype(jnp.bfloat16)
    return (
        output,
        query_grad,
        key_grad.reshape(key_count, KVH * HD),
        value_grad.reshape(key_count, KVH * HD),
    )


def local(
    patches,
    vit_gain,
    merge_up,
    merge_down,
    dest,
    text,
    norm_gain,
    kv_weight,
    queries,
    out_grad,
    assign,
    docs,
):
    ctx_count = lax.axis_size("ctx")
    data_count = lax.axis_size("dp")
    device_count = ctx_count * data_count
    token_rows = text.shape[1]
    visual_rows = dest.shape[0]
    capacity = max(1, visual_rows // device_count)
    slot_total = device_count * capacity
    normed = merger_norm(patches, vit_gain)
    inner_hidden = jax.nn.gelu(
        jnp.dot(normed, merge_up, preferred_element_type=jnp.float32), approximate=False
    ).astype(jnp.bfloat16)
    visual = lax.psum_scatter(
        jnp.dot(inner_hidden, merge_down, preferred_element_type=jnp.float32).astype(jnp.bfloat16),
        "ctx",
        scatter_dimension=0,
        tiled=True,
    )
    target = dest // token_rows
    local_row = dest % token_rows
    token_order = jnp.arange(visual_rows, dtype=jnp.int32)
    before = (target[:, None] == target[None, :]) & (token_order[None, :] < token_order[:, None])
    slot_index = target * capacity + jnp.sum(before.astype(jnp.int32), axis=1)
    picking = jnp.arange(slot_total, dtype=jnp.int32)[:, None] == slot_index[None, :]
    outgoing = jnp.dot(
        picking.astype(jnp.bfloat16), visual, preferred_element_type=jnp.float32
    ).astype(jnp.bfloat16)
    outgoing_rows = jnp.sum(jnp.where(picking, local_row[None, :] + 1, 0), axis=1) - 1
    arrived, arrived_rows = (
        lax.all_to_all(outgoing, ("dp", "ctx"), split_axis=0, concat_axis=0, tiled=True),
        lax.all_to_all(outgoing_rows, ("dp", "ctx"), split_axis=0, concat_axis=0, tiled=True),
    )
    placing = jnp.arange(token_rows, dtype=jnp.int32)[:, None] == arrived_rows[None, :]
    placed = jnp.dot(
        placing.astype(jnp.bfloat16), arrived, preferred_element_type=jnp.float32
    ).astype(jnp.bfloat16)
    marked = jnp.any(placing, axis=1)
    hidden = jnp.where(marked[:, None], placed, text[0])
    hidden32 = hidden.astype(jnp.float32)
    normed_hidden = rms_scale(hidden32, norm_gain).astype(jnp.bfloat16)
    projected = jnp.dot(
        normed_hidden,
        lax.all_gather(kv_weight, ("dp", "ctx"), axis=0, tiled=True),
        preferred_element_type=jnp.float32,
    )
    pairs_local = projected.astype(jnp.bfloat16)
    pairs_all = lax.all_gather(pairs_local, "ctx", axis=0, tiled=True)
    halves = token_rows // 2
    length = token_rows * ctx_count
    positions = (assign[:, None] * halves + jnp.arange(halves, dtype=jnp.int32)[None, :]).reshape(
        length
    )
    labels = docs[0].reshape(-1, halves)[assign].reshape(length)
    own_start = lax.axis_index("ctx") * token_rows
    query_pos = lax.dynamic_slice_in_dim(positions, own_start, token_rows, 0)
    query_doc = lax.dynamic_slice_in_dim(labels, own_start, token_rows, 0)
    attention, query_grad, key_grad, value_grad = attend(
        queries[0], pairs_all, out_grad[0], query_pos, query_doc, positions, labels
    )
    key_grad, value_grad = (
        lax.psum_scatter(
            key_grad.astype(jnp.bfloat16), "ctx", scatter_dimension=0, tiled=True
        ).astype(jnp.float32),
        lax.psum_scatter(
            value_grad.astype(jnp.bfloat16), "ctx", scatter_dimension=0, tiled=True
        ).astype(jnp.float32),
    )
    pair_grad = jnp.concatenate([key_grad, value_grad], axis=1).astype(jnp.bfloat16)
    contract = (((1,), (1,)), ((), ()))
    normed_grad = lax.dot_general(
        pair_grad,
        lax.all_gather(kv_weight, ("dp", "ctx"), axis=0, tiled=True),
        contract,
        preferred_element_type=jnp.float32,
    )
    forward_value, pullback = jax.vjp(lambda values: rms_scale(values, norm_gain), hidden32)
    full_grad = pullback(normed_grad)[0]
    hidden_grad = jnp.where(marked[:, None], jnp.float32(0.0), full_grad).astype(jnp.bfloat16)
    returning = jnp.dot(
        placing.T.astype(jnp.bfloat16),
        full_grad.astype(jnp.bfloat16),
        preferred_element_type=jnp.float32,
    ).astype(jnp.bfloat16)
    returned = lax.all_to_all(returning, ("dp", "ctx"), split_axis=0, concat_axis=0, tiled=True)
    visual_grad = jnp.dot(
        picking.T.astype(jnp.bfloat16), returned, preferred_element_type=jnp.float32
    ).astype(jnp.bfloat16)
    return (attention[None], query_grad[None], hidden_grad[None], visual_grad)


def neighbor(values, axis, offset):
    count = lax.axis_size(axis)
    return lax.ppermute(values, axis, [(d, d ^ offset) for d in range(count)])


def after(values, earlier):
    return lax.optimization_barrier((values, *earlier))[0]


def swap(values):
    return neighbor(values, "core", 1)


def vmem_params(size=16):
    return pltpu.CompilerParams(vmem_limit_bytes=size * 1024 * 1024)


def brief():
    return pl.CostEstimate(flops=1, bytes_accessed=1, transcendentals=0)


def smem():
    return pl.BlockSpec(memory_space=pltpu.SMEM)


def store_halves(core, values, own_ref, other_ref, block):
    def put(own_parity):
        for j in range(values.shape[1] // (2 * block)):
            even = values[:, 2 * j * block : (2 * j + 1) * block]
            odd = values[:, (2 * j + 1) * block : (2 * j + 2) * block]
            own_ref[:, j * block : (j + 1) * block] = odd if own_parity else even
            other_ref[:, j * block : (j + 1) * block] = even if own_parity else odd

    @pl.when(core == 0)
    def _():
        put(0)

    @pl.when(core != 0)
    def _():
        put(1)


def split_halves(values, core, block):
    rows, width = values.shape
    step = 8 * block

    def kernel(core_ref, value_ref, own_ref, other_ref):
        store_halves(core_ref[0], value_ref[...], own_ref, other_ref, block)

    half = jax.ShapeDtypeStruct((rows, width // 2), values.dtype)
    out = pl.BlockSpec((rows, step // 2), lambda j: (0, j))
    return pl.pallas_call(
        kernel,
        grid=(width // step,),
        in_specs=[smem(), pl.BlockSpec((rows, step), lambda j: (0, j))],
        out_specs=[out, out],
        out_shape=[half, half],
        compiler_params=vmem_params(56),
        cost_estimate=brief(),
        name="split_halves",
    )(core, values)


def up_projection(patches, gain, weight):
    rows, depth = patches.shape
    vector = gain.shape[1]
    width = weight.shape[1]
    count = depth // vector

    def kernel(patch_ref, gain_ref, weight_ref, out_ref, buffers, sems):
        copies = [
            pltpu.make_async_copy(weight_ref.at[j * vector : (j + 1) * vector], buffers.at[j], sems.at[j])
            for j in range(count)
        ]
        for copy in copies:
            copy.start()
        total = jnp.zeros((rows, width), jnp.float32)
        for j in range(count):
            center = patch_ref[:, j * vector : (j + 1) * vector].astype(jnp.float32)
            center = center - jnp.mean(center, axis=1, keepdims=True)
            spread = jnp.mean(center * center, axis=1, keepdims=True)
            normed = (center * lax.rsqrt(spread + epsilon) * gain_ref[...]).astype(jnp.bfloat16)
            copies[j].wait()
            total = total + jnp.dot(normed, buffers[j], preferred_element_type=jnp.float32)
        out_ref[...] = (0.5 * total * (1.0 + lax.erf(total * math.sqrt(0.5)))).astype(jnp.bfloat16)

    vmem = pl.BlockSpec(memory_space=pltpu.VMEM)
    return pl.pallas_call(
        kernel,
        in_specs=[vmem, vmem, pl.BlockSpec(memory_space=pl.ANY)],
        out_specs=vmem,
        out_shape=jax.ShapeDtypeStruct((rows, width), jnp.bfloat16),
        scratch_shapes=[
            pltpu.VMEM((count, vector, width), jnp.bfloat16),
            pltpu.SemaphoreType.DMA((count,)),
        ],
        compiler_params=vmem_params(56),
        cost_estimate=brief(),
        name="merge_up",
    )(patches, gain, weight)


def down_halves(inner_hidden, merge_down, core, block):
    rows, depth = inner_hidden.shape
    width = merge_down.shape[1]
    step = 4 * block
    count = width // step

    def kernel(core_ref, hidden_ref, weight_ref, own_ref, other_ref, buffers, sems):
        copies = [
            pltpu.make_async_copy(weight_ref.at[:, j * step : (j + 1) * step], buffers.at[j], sems.at[j])
            for j in range(count)
        ]
        for copy in copies:
            copy.start()
        for j in range(count):
            copies[j].wait()
            product = jnp.dot(hidden_ref[...], buffers[j], preferred_element_type=jnp.float32)
            place = slice(j * step // 2, (j + 1) * step // 2)
            store_halves(
                core_ref[0], product.astype(jnp.bfloat16), own_ref.at[:, place], other_ref.at[:, place], block
            )

    vmem = pl.BlockSpec(memory_space=pltpu.VMEM)
    half = jax.ShapeDtypeStruct((rows, width // 2), jnp.bfloat16)
    return pl.pallas_call(
        kernel,
        in_specs=[smem(), vmem, pl.BlockSpec(memory_space=pl.ANY)],
        out_specs=[vmem, vmem],
        out_shape=[half, half],
        scratch_shapes=[
            pltpu.VMEM((count, depth, step), jnp.bfloat16),
            pltpu.SemaphoreType.DMA((count,)),
        ],
        compiler_params=vmem_params(56),
        cost_estimate=brief(),
        name="merge_down",
    )(core, inner_hidden, merge_down)


def project(table, own_rows, sibling_rows, visual, gain, blocks, first, count, earlier):
    rows = own_rows.shape[0]
    total = 2 * rows + visual.shape[0]
    block, width = blocks[0].shape
    quarter = width // 4
    size = len(blocks)
    last = first + size == count
    flag = table.shape[0] - 1

    def kernel(table_ref, own_ref, sibling_ref, visual_ref, gain_ref, *rest):
        block_refs = rest[:size]
        before_refs = rest[size : size + len(earlier)]
        turned_ref, *outs, turning, sems = rest[size + len(earlier) :]
        total_ref = outs[-1]
        turns = []
        for r in range(size):
            columns = pl.ds(pl.multiple_of(table_ref[first + r] * block, block), block)
            gains = gain_ref[:, columns]
            part = jnp.concatenate(
                [
                    (ref[:, columns].astype(jnp.float32) * gains).astype(jnp.bfloat16)
                    for ref in (own_ref, sibling_ref, visual_ref)
                ],
                axis=0,
            )
            values = block_refs[r][...]
            product = jnp.dot(part, values, preferred_element_type=jnp.float32)
            if r > 0:
                total_ref[...] += product
            elif earlier:
                total_ref[...] = before_refs[0][...] + product
            else:
                total_ref[...] = product
            turning[r] = values.T
            turn = pltpu.make_async_copy(turning.at[r], turned_ref.at[r], sems.at[r])
            turn.start()
            turns.append(turn)
        if last:
            mine_ref, theirs_ref = outs[:2]

            def put(parity):
                for piece in range(2):
                    start = 2 * piece * quarter
                    mine = slice(start + parity * quarter, start + (parity + 1) * quarter)
                    theirs = slice(start + (1 - parity) * quarter, start + (2 - parity) * quarter)
                    place = slice(piece * quarter, (piece + 1) * quarter)
                    mine_ref[:, place] = total_ref[:, mine]
                    theirs_ref[:rows, place] = total_ref[rows : 2 * rows, theirs].astype(jnp.bfloat16)
                    theirs_ref[rows : 2 * rows, place] = total_ref[:rows, theirs].astype(jnp.bfloat16)
                    theirs_ref[2 * rows :, place] = total_ref[2 * rows :, theirs].astype(jnp.bfloat16)

            @pl.when(table_ref[flag] == 0)
            def _():
                put(0)

            @pl.when(table_ref[flag] != 0)
            def _():
                put(1)

        for turn in turns:
            turn.wait()

    vmem = pl.BlockSpec(memory_space=pltpu.VMEM)
    shape = jax.ShapeDtypeStruct
    sums, scratch = [shape((total, width), jnp.float32)], []
    if last:
        sums = [shape((total, width // 2), jnp.float32), shape((total, width // 2), jnp.bfloat16)]
        scratch = [pltpu.VMEM((total, width), jnp.float32)]
    return pl.pallas_call(
        kernel,
        in_specs=[smem()] + [vmem] * (4 + size + len(earlier)),
        out_specs=[pl.BlockSpec(memory_space=pl.ANY)] + [vmem] * len(sums),
        out_shape=[shape((size, width, block), jnp.bfloat16)] + sums,
        scratch_shapes=scratch + [pltpu.VMEM((size, width, block), jnp.bfloat16), pltpu.SemaphoreType.DMA((size,))],
        compiler_params=vmem_params(24 if last else 56),
        cost_estimate=brief(),
        name="project_pairs",
    )(table, own_rows, sibling_rows, visual, gain, *blocks, *earlier)


def finish_pairs(mine, received, scale, codes, picking, rows):
    total, width = mine.shape
    slots, tokens = picking.shape

    def kernel(mine_ref, received_ref, scale_ref, codes_ref, picking_ref, chip_ref, token_ref, slot_ref):
        pairs = (mine_ref[...] + received_ref[...].astype(jnp.float32)) * jnp.broadcast_to(scale_ref[...], (128, total)).T[:, :1]
        pairs = pairs.astype(jnp.bfloat16)
        chip_ref[...] = pairs[: 2 * rows]
        token_ref[...] = pairs[2 * rows :]
        placing = picking_ref[...]
        slot_ref[:, :width] = jnp.dot(
            placing, pairs[2 * rows :], preferred_element_type=jnp.float32
        ).astype(jnp.bfloat16)
        slot_ref[:, width:] = jnp.dot(
            placing, codes_ref[...], preferred_element_type=jnp.float32
        ).astype(jnp.bfloat16)

    shape = jax.ShapeDtypeStruct
    return pl.pallas_call(
        kernel,
        out_shape=[
            shape((2 * rows, width), jnp.bfloat16),
            shape((tokens, width), jnp.bfloat16),
            shape((slots, width + codes.shape[1]), jnp.bfloat16),
        ],
        compiler_params=vmem_params(56),
        cost_estimate=brief(),
        name="finish_pairs",
    )(mine, received, scale, codes, picking)


def sum_grads(core, pair_grad, received, returned, picking, rows):
    width = pair_grad.shape[1]
    tokens = picking.shape[1] // 2

    def kernel(core_ref, grad_ref, returned_ref, picking_ref, *rest):
        held_ref, sent_ref = rest[-2:]
        text = grad_ref[...].astype(jnp.float32)
        for ref in rest[:-2]:
            text = text + ref[...].astype(jnp.float32)
        text = text.astype(jnp.bfloat16)
        held_ref[:rows] = text[:rows]
        sent_ref[:rows] = text[rows:]
        token = lax.dot_general(
            picking_ref[...], returned_ref[...], (((0,), (0,)), ((), ())), preferred_element_type=jnp.float32
        ).astype(jnp.bfloat16)

        @pl.when(core_ref[0] == 0)
        def _():
            held_ref[rows:] = token[:tokens]
            sent_ref[rows:] = token[tokens:]

        @pl.when(core_ref[0] != 0)
        def _():
            held_ref[rows:] = token[tokens:]
            sent_ref[rows:] = token[:tokens]

    def whole(values):
        return pl.BlockSpec(values.shape, lambda j: (0, 0))

    half = jax.ShapeDtypeStruct((rows + tokens, width), jnp.bfloat16)
    return pl.pallas_call(
        kernel,
        grid=(1,),
        in_specs=[smem(), pl.BlockSpec((2 * rows, width), lambda j: (0, 0)), whole(returned), whole(picking)]
        + [whole(part) for part in received],
        out_specs=[whole(jax.ShapeDtypeStruct((rows + tokens, width), jnp.bfloat16))] * 2,
        out_shape=[half, half],
        compiler_params=vmem_params(56),
        cost_estimate=brief(),
        name="sum_grads",
    )(core, pair_grad, returned, picking, *received)


def project_back(table, grads, pairs, turned, text, visual, gain, scale, keep):
    rows, width = text.shape
    tokens = visual[0].shape[0]
    total = rows + tokens
    pair_width, block = turned[0][0].shape[1:]
    quarter = pair_width // 4
    flag = table.shape[0] - 1
    pieces = len(turned[0])
    count = sum(part.shape[0] for part in turned[0])
    groups, first = [], 0
    for piece in range(pieces):
        size = turned[0][piece].shape[0]
        for low in range(0, size, 4):
            high = min(size, low + 4)
            groups.append((piece, low, high, first + low))
        first += size
    groups = groups[-1:] + groups[:-1]

    def kernel(
        table_ref, grad_ref, grad_other_ref, pair_ref, pair_other_ref, text_ref, visual_ref, visual_other_ref,
        gain_ref, scale_ref, keep_ref, *rest,
    ):
        turned_refs, (hidden_ref, token_ref, joined, buffers, sems) = rest[: 2 * pieces], rest[2 * pieces :]
        core = table_ref[flag]
        copies = []
        for at, (piece, low, high, place) in enumerate(groups):
            copies.append(
                [
                    pltpu.make_async_copy(
                        turned_refs[side * pieces + piece].at[low:high],
                        buffers.at[side, place : place + high - low],
                        sems.at[at, side],
                    )
                    for side in range(2)
                ]
            )
        for pair in copies[:2]:
            for copy in pair:
                copy.start()

        def join(parity):
            for piece in range(2):
                place = slice(piece * quarter, (piece + 1) * quarter)
                start = (2 * piece + parity) * quarter
                joined[:, start : start + quarter] = grad_ref[:, place]
                start = (2 * piece + 1 - parity) * quarter
                joined[:, start : start + quarter] = grad_other_ref[:, place]

        @pl.when(core == 0)
        def _():
            join(0)

        @pl.when(core != 0)
        def _():
            join(1)

        inner = jnp.zeros((total, 1), jnp.float32)
        for left, right in ((grad_ref, pair_ref), (grad_other_ref, pair_other_ref)):
            inner = inner + jnp.sum(
                left[...].astype(jnp.float32) * right[...].astype(jnp.float32), axis=1, keepdims=True
            )
        scales = scale_ref[...]
        backs = inner * scales * scales * (1.0 / width)
        keeps = keep_ref[:rows] > 0
        for at, (piece, low, high, first) in enumerate(groups):
            for copy in copies[at]:
                copy.wait()
            if at + 2 < len(groups):
                for copy in copies[at + 2]:
                    copy.start()
            for r in range(first, first + high - low):
                spot = table_ref[r]
                inside = pl.ds(pl.multiple_of(spot * block, block), block)
                for half, (side, token_in) in enumerate(((core, visual_ref), (1 - core, visual_other_ref))):
                    place = pl.ds(pl.multiple_of((2 * spot + side) * block, block), block)
                    normed_grad = jnp.dot(joined[...], buffers[half, r], preferred_element_type=jnp.float32)
                    full = normed_grad * scales * gain_ref[:, place]
                    hidden = full[:rows] - text_ref[:, place].astype(jnp.float32) * backs[:rows]
                    hidden_ref[:, place] = jnp.where(keeps, hidden, 0.0).astype(jnp.bfloat16)
                    token = full[rows:] - token_in[:, inside].astype(jnp.float32) * backs[rows:]
                    token_ref[:, place] = token.astype(jnp.bfloat16)

    vmem = pl.BlockSpec(memory_space=pltpu.VMEM)
    shape = jax.ShapeDtypeStruct
    return pl.pallas_call(
        kernel,
        in_specs=[smem()] + [vmem] * 10 + [pl.BlockSpec(memory_space=pl.ANY)] * (2 * pieces),
        out_specs=[vmem, vmem],
        out_shape=[shape((rows, width), jnp.bfloat16), shape((tokens, width), jnp.bfloat16)],
        scratch_shapes=[
            pltpu.VMEM((total, pair_width), jnp.bfloat16),
            pltpu.VMEM((2, count, pair_width, block), jnp.bfloat16),
            pltpu.SemaphoreType.DMA((len(groups), 2)),
        ],
        compiler_params=vmem_params(56),
        cost_estimate=brief(),
        name="project_back",
    )(table, *grads, *pairs, text, *visual, gain, scale, keep, *turned[0], *turned[1])


def attend_pair(queries, upstream, pair_text, pair_visual, keyed):
    rows, width = queries[0].shape
    length, pair_width = pair_text[0].shape[0] * len(pair_text), pair_text[0].shape[1]
    slots = pair_visual.shape[0]
    own_kv = pair_width // (2 * HD)
    heads = width // HD
    group = heads // own_kv
    step_heads = group
    steps = heads // step_heads
    score_scale = HD ** (-0.5)
    f32, bf16 = jnp.float32, jnp.bfloat16

    def kernel(
        qa, qb, ua, ub, visual_ref, row_s, row_l, pos_ref, doc_ref, qpos_ref, qdoc_ref, *rest,
    ):
        text_refs = rest[: len(pair_text)]
        oa, ob, ga, gb, *grad_refs, grad_visual_ref, keep_ref, heads_ref, turned_ref, bias_ref, total_ref = rest[
            len(pair_text) :
        ]
        step = pl.program_id(0)

        @pl.when(step == 0)
        def _():
            codes = visual_ref[:, pair_width:].astype(f32).T
            placing = jnp.where(row_s[...] == codes[0:1] * 16.0 + codes[1:2], 1.0, 0.0).astype(f32)
            placed = jnp.dot(placing.astype(bf16), visual_ref[:, :pair_width], preferred_element_type=f32)
            marked = jnp.max(placing, axis=1, keepdims=True)
            keep_ref[...] = 1.0 - marked
            texts = jnp.concatenate([ref[...].astype(f32) for ref in text_refs], axis=0)
            pairs = jnp.where(marked > 0, placed, texts)
            for j in range(2 * own_kv):
                piece = pairs[:, j * HD : (j + 1) * HD]
                heads_ref[j] = piece.astype(bf16)
                turned_ref[j] = piece.T.astype(bf16)
            allowed = (pos_ref[...] <= qpos_ref[...]) & (doc_ref[...] == qdoc_ref[...])
            bias_ref[...] = jnp.where(allowed, 0.0, -jnp.inf).astype(f32).T
            total_ref[...] = jnp.zeros_like(total_ref)

        head = (step * step_heads) // group
        keys, values = heads_ref[head], heads_ref[own_kv + head]
        keys_turned, values_turned = turned_ref[head], turned_ref[own_kv + head]
        lights, score_grads, query_list, ups = [], [], [], []
        for h in range(step_heads):
            lanes = slice(h * HD, (h + 1) * HD)
            query = jnp.concatenate([qa[:, lanes], qb[:, lanes]], axis=0)
            up = jnp.concatenate([ua[:, lanes], ub[:, lanes]], axis=0)
            scores = jnp.dot(query, keys_turned, preferred_element_type=f32)
            weight_grad = jnp.dot(up, values_turned, preferred_element_type=f32)
            scores = scores * (score_scale * math.log2(math.e)) + bias_ref[...]
            weights = jnp.exp2(scores - jnp.max(scores, axis=1, keepdims=True))
            weights = weights * (1.0 / jnp.sum(weights, axis=1, keepdims=True))
            light = weights.astype(bf16)
            inner = jnp.sum(weights * weight_grad, axis=1, keepdims=True)
            score_grad = (weights * (weight_grad - inner)).astype(bf16)
            output = jnp.dot(light, values, preferred_element_type=f32).astype(bf16)
            oa[:, lanes] = output[:rows]
            ob[:, lanes] = output[rows:]
            query_grad = (jnp.dot(score_grad, keys, preferred_element_type=f32) * score_scale).astype(bf16)
            ga[:, lanes] = query_grad[:rows]
            gb[:, lanes] = query_grad[rows:]
            lights.append(light)
            score_grads.append(score_grad)
            query_list.append(query)
            ups.append(up)
        up, light = jnp.concatenate(ups, axis=0).T, jnp.concatenate(lights, axis=0)
        total_ref[own_kv + head] += jnp.dot(up, light, preferred_element_type=f32)
        query, score_grad = jnp.concatenate(query_list, axis=0).T, jnp.concatenate(score_grads, axis=0)
        total_ref[head] += jnp.dot(query, score_grad, preferred_element_type=f32) * score_scale

        @pl.when(step == steps - 1)
        def _():
            codes = visual_ref[:, pair_width : pair_width + 2].astype(f32)
            lifting = jnp.where(codes[:, 0:1] * 16.0 + codes[:, 1:2] == row_l[...], 1.0, 0.0).astype(bf16)
            for j in range(2 * own_kv):
                piece = total_ref[j].T.astype(bf16)
                place = slice(j * HD, (j + 1) * HD)
                for i, ref in enumerate(grad_refs):
                    ref[:, place] = piece[i * ref.shape[0] : (i + 1) * ref.shape[0]]
                grad_visual_ref[:, place] = jnp.dot(lifting, piece, preferred_element_type=f32).astype(bf16)

    part = pl.BlockSpec((rows, step_heads * HD), lambda j: (0, j))
    vmem = pl.BlockSpec(memory_space=pltpu.VMEM)
    shape = jax.ShapeDtypeStruct
    return pl.pallas_call(
        kernel,
        grid=(steps,),
        in_specs=[part] * 4 + [vmem] * (7 + len(pair_text)),
        out_specs=[part] * 4 + [vmem] * (2 + len(pair_text)),
        out_shape=[shape((rows, width), bf16)] * 4
        + [shape(x.shape, bf16) for x in pair_text]
        + [shape((slots, pair_width), bf16), shape((length, 1), f32)],
        scratch_shapes=[
            pltpu.VMEM((2 * own_kv, length, HD), bf16),
            pltpu.VMEM((2 * own_kv, HD, length), bf16),
            pltpu.VMEM((2 * rows, length), f32),
            pltpu.VMEM((2 * own_kv, HD, length), f32),
        ],
        compiler_params=vmem_params(56),
        cost_estimate=brief(),
        name="attend",
    )(
        *queries,
        *upstream,
        pair_visual,
        *keyed,
        *pair_text,
    )


def local_fast(
    patches, vit_gain, merge_up, merge_down, dest, text, norm_gain, kv_weight, queries, out_grad, assign, docs
):
    f32, bf16 = jnp.float32, jnp.bfloat16
    data_count, column_count = lax.axis_size("dp"), lax.axis_size("y")
    ctx_count = 2 * column_count
    data, column, core = lax.axis_index("dp"), lax.axis_index("y"), lax.axis_index("core")
    rows, width = text.shape[1], text.shape[2]
    tokens = dest.shape[0]
    block = kv_weight.shape[0]
    length = rows * ctx_count
    core_word = core[None].astype(jnp.int32)

    def line(values, pairs):
        return lax.ppermute(values, "dp", [(2 * p + low, 2 * q + low) for p, q in pairs for low in range(2)])

    def both(values):
        return neighbor(values, "dp", 1), neighbor(values, "y", 1)

    close = lax.optimization_barrier
    swapped = [(0, 1), (1, 0), (2, 3), (3, 2)]
    middle, outward = [(1, 2), (2, 1)], [(1, 0), (2, 3)]
    far_index = data // 2
    is_middle = (far_index == 1) | (far_index == 2)
    hops = [0, 1, jnp.where(is_middle, 3, 2), jnp.where(is_middle, 2, 3)]
    owners = [
        ((far_index ^ hops[i + j]) * 2 + ((data % 2) ^ along)) * column_count + (column ^ down)
        for i in (0, 2)
        for along, down in ((0, 0), (1, 0), (0, 1), (1, 1))
        for j in range(2)
    ]
    table = jnp.stack(owners + [core]).astype(jnp.int32)
    gain = lax.dynamic_index_in_dim(
        norm_gain.reshape(-1, 2, block), core, axis=1, keepdims=False
    ).reshape(1, width // 2)
    query_width = queries.shape[2] // 2
    chip_tokens = 2 * tokens

    beside0, below0 = both(kv_weight)
    far1, across = line(kv_weight, swapped), line(kv_weight, middle)
    inner_hidden = up_projection(patches, vit_gain[None, :], merge_up)
    rows_in = text[0]
    beside0, below0, far1, across, inner_hidden, rows_in, core_word, table, gain = close(
        (beside0, below0, far1, across, inner_hidden, rows_in, core_word, table, gain)
    )

    beside1, below1 = both(far1)
    across2, ends1 = line(far1, middle), line(across, outward)
    merged, merged_other = down_halves(inner_hidden, merge_down, core_word, block)
    beside1, below1, across2, ends1, merged, merged_other, rows_in, core_word = close(
        (beside1, below1, across2, ends1, merged, merged_other, rows_in, core_word)
    )

    corner0, corner1 = neighbor(beside0, "y", 1), neighbor(below1, "dp", 1)
    ends2 = line(across2, outward)
    arriving = swap(merged_other)
    own_rows, other_part = split_halves(rows_in, core_word, block)
    sibling_rows = swap(other_part)
    far2 = jnp.where(is_middle, across, ends1)
    merged = (merged.astype(f32) + arriving.astype(f32)).astype(bf16)
    visual32 = lax.dynamic_slice_in_dim(merged, column * chip_tokens, chip_tokens, 0)
    leaving = lax.dynamic_slice_in_dim(merged, (column ^ 1) * chip_tokens, chip_tokens, 0)
    summing = neighbor(leaving, "y", 1)
    query_in, upstream_in = queries[0], out_grad[0]
    corner0, corner1, ends2, own_rows, sibling_rows, far2, visual32, summing = close(
        (corner0, corner1, ends2, own_rows, sibling_rows, far2, visual32, summing)
    )
    query_in, upstream_in, dest, assign, docs, ends2 = close((query_in, upstream_in, dest, assign, docs, ends2))

    def heads_of(values):
        mine = lax.dynamic_slice_in_dim(values, core * query_width, query_width, 1)
        theirs = lax.dynamic_slice_in_dim(values, (1 - core) * query_width, query_width, 1)
        return mine, theirs

    beside2, below2 = both(far2)
    far3 = jnp.where(is_middle, across2, ends2)
    query_parts, upstream_parts = heads_of(query_in), heads_of(upstream_in)
    query_parts = (query_parts[0], swap(query_parts[1]))
    upstream_parts = (upstream_parts[0], swap(upstream_parts[1]))

    def squares(values):
        values = values.astype(f32)
        return jnp.sum(values * values, axis=1)

    own_squares, sibling_squares = squares(own_rows), squares(sibling_rows)

    dest_other = swap(dest)
    chip_dest = jnp.where(
        core == 0, jnp.concatenate([dest, dest_other]), jnp.concatenate([dest_other, dest])
    )
    token_core = jnp.arange(chip_tokens, dtype=jnp.int32) // tokens
    sequence, row_of = chip_dest // length, chip_dest % length
    slot = token_core * ctx_count + row_of // rows
    slot_total = data_count * column_count * 2 * ctx_count
    slot_index = jnp.arange(slot_total, dtype=jnp.int32)[:, None]
    picking = (slot_index // (column_count * 2 * ctx_count) == sequence[None, :]) & (
        slot_index % (2 * ctx_count) == slot[None, :]
    )
    picking = picking.astype(bf16)
    lane = jnp.arange(128, dtype=jnp.int32)[None, :]
    code = row_of[:, None] + 1
    codes = jnp.where(lane == 0, code // 16, jnp.where(lane == 1, code % 16, 0)).astype(bf16)

    def between_chips(values):
        shaped = values.reshape(data_count * column_count, 2 * ctx_count, -1)
        moved = lax.all_to_all(shaped, ("dp", "y"), split_axis=0, concat_axis=0, tiled=True)
        return moved.reshape(values.shape)

    halves = rows // 2
    positions = (assign[:, None] * halves + jnp.arange(halves, dtype=jnp.int32)[None, :]).reshape(length)
    labels = docs[0].reshape(-1, halves)[assign].reshape(length)
    order = jnp.stack(
        [2 * (column ^ down) + (core ^ side) for down in range(column_count) for side in range(2)]
    )
    key_row = (order[:, None] * rows + jnp.arange(rows, dtype=jnp.int32)[None, :]).reshape(length)
    key_pos = positions.reshape(ctx_count, rows)[order].reshape(length)
    key_doc = labels.reshape(ctx_count, rows)[order].reshape(length)
    key_row = key_row.astype(f32) + 1.0
    keyed = (key_row[:, None], key_row[None, :], key_pos[:, None], key_doc[:, None])
    keyed += (key_pos[None, : 2 * rows], key_doc[None, : 2 * rows])

    def of_core(values, which):
        return lax.dynamic_slice_in_dim(values, which * tokens, tokens, 0)

    beside2, below2, far3, summing, query_parts, upstream_parts, keyed, picking, codes, own_squares, sibling_squares = close(
        (beside2, below2, far3, summing, query_parts, upstream_parts, keyed, picking, codes, own_squares, sibling_squares)
    )

    beside3, below3 = both(far3)
    visual = (visual32.astype(f32) + summing.astype(f32)).astype(bf16)
    blocks = [kv_weight, far1, beside0, beside1, below0, below1, corner0, corner1]
    part0, sums = project(table, own_rows, sibling_rows, visual, gain, blocks, 0, 16, ())
    beside3, below3, part0, sums, visual = close((beside3, below3, part0, sums, visual))

    corner2, corner3 = neighbor(beside2, "y", 1), neighbor(below3, "dp", 1)
    other0 = swap(part0)
    blocks = [far2, far3, beside2, beside3, below2, below3]
    part1, sums = project(table, own_rows, sibling_rows, visual, gain, blocks, 8, 16, (sums,))
    visual_squares = squares(visual)
    arrived = swap(jnp.concatenate([sibling_squares, own_squares, visual_squares]))
    square = jnp.concatenate([own_squares, sibling_squares, visual_squares]) + arrived
    scale = lax.rsqrt(square / width + epsilon)[:, None]
    wide_scale = scale.reshape(1, -1)
    own_visual, other_visual = of_core(visual, core), swap(of_core(visual, 1 - core))
    own_scale = jnp.concatenate([scale[:rows], of_core(scale[2 * rows :], core)], axis=0)
    corner2, corner3, part1, sums, other0, wide_scale, own_visual, other_visual, own_scale = close(
        (corner2, corner3, part1, sums, other0, wide_scale, own_visual, other_visual, own_scale)
    )
    part2, *sums = project(table, own_rows, sibling_rows, visual, gain, [corner2, corner3], 14, 16, (sums,))
    turned, turned_other = [part0, part1, part2], [other0]
    mine, theirs = sums
    received = swap(theirs)
    pair_chip, pair_tokens, leaving = finish_pairs(mine, received, wide_scale, codes, picking, rows)
    pair_text = [pair_chip] + [neighbor(pair_chip, "y", down) for down in range(1, column_count)]
    pair_visual = between_chips(leaving)
    turned_other += [swap(after(part, (received,))) for part in turned[1:]]

    own_pairs = jnp.concatenate([pair_chip[:rows], of_core(pair_tokens, core)], axis=0)
    other_pairs = swap(jnp.concatenate([pair_chip[rows:], of_core(pair_tokens, 1 - core)], axis=0))

    pair_text[0] = after(pair_text[0], (own_pairs, other_pairs, turned_other))
    out_a, out_b, grad_a, grad_b, pair_grad, *far_grads, visual_pair_grad, keep = attend_pair(
        query_parts, upstream_parts, pair_text, pair_visual, keyed
    )

    def heads_back(held, leaving):
        arrived = swap(leaving)
        return jnp.where(
            core == 0, jnp.concatenate([held, arrived], axis=1), jnp.concatenate([arrived, held], axis=1)
        )

    received = [neighbor(part, "y", down) for down, part in enumerate(far_grads, 1)]
    returned = between_chips(visual_pair_grad)
    attention, query_grad = heads_back(out_a, out_b), heads_back(grad_a, grad_b)
    pair_grad, attention, query_grad = close((pair_grad, attention, query_grad))
    held, leaving = sum_grads(core_word, pair_grad, received, returned, picking, rows)
    hidden_grad, visual_grad = project_back(
        table, (held, swap(leaving)), (own_pairs, other_pairs), (turned, turned_other), text[0],
        (own_visual, other_visual), norm_gain[None, :], own_scale, keep,
    )
    return (attention[None], query_grad[None], hidden_grad[None], visual_grad)


def solution(mesh):
    data_count, ctx_count = mesh.shape["dp"], mesh.shape["ctx"]
    split = Mesh(mesh.devices.reshape(data_count, -1, 2), ("dp", "y", "core"))

    def call(*arrays):
        text, kv_weight, dest = arrays[5], arrays[7], arrays[4]
        devices = data_count * ctx_count
        rows = text.shape[1] // ctx_count
        fits = (
            ctx_count == 4
            and data_count == 8
            and (kv_weight.shape[0] // devices) % 128 == 0
            and dest.shape[0] // devices <= devices
            and rows % 128 == 0
        )
        if fits:
            whole, ctx, body, used = ("dp", "y", "core"), ("y", "core"), local_fast, split
        else:
            whole, ctx, body, used = ("dp", "ctx"), "ctx", local, mesh
        placed = (
            P("dp", None),
            P(),
            P(None, ctx),
            P(ctx, None),
            P(whole),
            P("dp", ctx, None),
            P(),
            P(whole, None),
            P("dp", ctx, None),
            P("dp", ctx, None),
            P(),
            P("dp", None),
        )
        return jax.shard_map(
            body,
            mesh=used,
            in_specs=placed,
            out_specs=(P("dp", ctx, None), P("dp", ctx, None), P("dp", ctx, None), P(whole, None)),
            check_vma=False,
        )(*arrays)

    return call
```

```python
import math

import jax
import jax.numpy as jnp
from jax import lax
from jax.experimental import pallas as pl
from jax.experimental.pallas import tpu as pltpu
from jax.sharding import Mesh
from jax.sharding import PartitionSpec as P

HEADS = 32
KVH = 4
HD = 128


epsilon = 1e-06


def merger_norm(patches, vit_gain):
    pieces = patches.astype(jnp.float32).reshape(patches.shape[0], 4, vit_gain.shape[0])
    center = pieces - jnp.mean(pieces, axis=-1, keepdims=True)
    spread = jnp.mean(center * center, axis=-1, keepdims=True)
    scaled = center * lax.rsqrt(spread + epsilon) * vit_gain
    return scaled.reshape(patches.shape[0], -1).astype(jnp.bfloat16)


def rms_scale(hidden32, norm_gain):
    square = jnp.mean(hidden32 * hidden32, axis=-1, keepdims=True)
    return hidden32 * lax.rsqrt(square + epsilon) * norm_gain


def attend(query_rows, pair_rows, upstream_rows, query_pos, query_doc, key_pos, key_doc):
    row_count = query_rows.shape[0]
    key_count = pair_rows.shape[0]
    group_size = HEADS // KVH
    score_scale = HD ** (-0.5)
    query_heads = query_rows.reshape(row_count, KVH, group_size, HD)
    key_heads = pair_rows[:, : KVH * HD].reshape(key_count, KVH, HD)
    value_heads = pair_rows[:, KVH * HD :].reshape(key_count, KVH, HD)
    scores = (
        jnp.einsum("qhgd,khd->hgqk", query_heads, key_heads, preferred_element_type=jnp.float32)
        * score_scale
    )
    allowed = (key_pos[None, :] <= query_pos[:, None]) & (key_doc[None, :] == query_doc[:, None])
    scores = jnp.where(allowed, scores, -jnp.inf)
    weights = jnp.exp(scores - jnp.max(scores, axis=-1, keepdims=True))
    weights = weights / jnp.sum(weights, axis=-1, keepdims=True)
    light_weights = weights.astype(jnp.bfloat16)
    output = jnp.einsum(
        "hgqk,khd->qhgd", light_weights, value_heads, preferred_element_type=jnp.float32
    )
    upstream = upstream_rows.reshape(row_count, KVH, group_size, HD)
    value_grad = jnp.einsum(
        "hgqk,qhgd->khd", light_weights, upstream, preferred_element_type=jnp.float32
    )
    weight_grad = jnp.einsum(
        "qhgd,khd->hgqk", upstream, value_heads, preferred_element_type=jnp.float32
    )
    inner_sum = jnp.sum(weights * weight_grad, axis=-1, keepdims=True)
    score_grad = (weights * (weight_grad - inner_sum) * score_scale).astype(jnp.bfloat16)
    query_grad = jnp.einsum(
        "hgqk,khd->qhgd", score_grad, key_heads, preferred_element_type=jnp.float32
    )
    key_grad = jnp.einsum(
        "hgqk,qhgd->khd", score_grad, query_heads, preferred_element_type=jnp.float32
    )
    output = output.reshape(row_count, HEADS * HD).astype(jnp.bfloat16)
    query_grad = query_grad.reshape(row_count, HEADS * HD).astype(jnp.bfloat16)
    return (
        output,
        query_grad,
        key_grad.reshape(key_count, KVH * HD),
        value_grad.reshape(key_count, KVH * HD),
    )


def local(
    patches,
    vit_gain,
    merge_up,
    merge_down,
    dest,
    text,
    norm_gain,
    kv_weight,
    queries,
    out_grad,
    assign,
    docs,
):
    ctx_count = lax.axis_size("ctx")
    data_count = lax.axis_size("dp")
    device_count = ctx_count * data_count
    token_rows = text.shape[1]
    visual_rows = dest.shape[0]
    capacity = max(1, visual_rows // device_count)
    slot_total = device_count * capacity
    normed = merger_norm(patches, vit_gain)
    inner_hidden = jax.nn.gelu(
        jnp.dot(normed, merge_up, preferred_element_type=jnp.float32), approximate=False
    ).astype(jnp.bfloat16)
    visual = lax.psum_scatter(
        jnp.dot(inner_hidden, merge_down, preferred_element_type=jnp.float32).astype(jnp.bfloat16),
        "ctx",
        scatter_dimension=0,
        tiled=True,
    )
    target = dest // token_rows
    local_row = dest % token_rows
    token_order = jnp.arange(visual_rows, dtype=jnp.int32)
    before = (target[:, None] == target[None, :]) & (token_order[None, :] < token_order[:, None])
    slot_index = target * capacity + jnp.sum(before.astype(jnp.int32), axis=1)
    picking = jnp.arange(slot_total, dtype=jnp.int32)[:, None] == slot_index[None, :]
    outgoing = jnp.dot(
        picking.astype(jnp.bfloat16), visual, preferred_element_type=jnp.float32
    ).astype(jnp.bfloat16)
    outgoing_rows = jnp.sum(jnp.where(picking, local_row[None, :] + 1, 0), axis=1) - 1
    arrived, arrived_rows = (
        lax.all_to_all(outgoing, ("dp", "ctx"), split_axis=0, concat_axis=0, tiled=True),
        lax.all_to_all(outgoing_rows, ("dp", "ctx"), split_axis=0, concat_axis=0, tiled=True),
    )
    placing = jnp.arange(token_rows, dtype=jnp.int32)[:, None] == arrived_rows[None, :]
    placed = jnp.dot(
        placing.astype(jnp.bfloat16), arrived, preferred_element_type=jnp.float32
    ).astype(jnp.bfloat16)
    marked = jnp.any(placing, axis=1)
    hidden = jnp.where(marked[:, None], placed, text[0])
    hidden32 = hidden.astype(jnp.float32)
    normed_hidden = rms_scale(hidden32, norm_gain).astype(jnp.bfloat16)
    projected = jnp.dot(
        normed_hidden,
        lax.all_gather(kv_weight, ("dp", "ctx"), axis=0, tiled=True),
        preferred_element_type=jnp.float32,
    )
    pairs_local = projected.astype(jnp.bfloat16)
    pairs_all = lax.all_gather(pairs_local, "ctx", axis=0, tiled=True)
    halves = token_rows // 2
    length = token_rows * ctx_count
    positions = (assign[:, None] * halves + jnp.arange(halves, dtype=jnp.int32)[None, :]).reshape(
        length
    )
    labels = docs[0].reshape(-1, halves)[assign].reshape(length)
    own_start = lax.axis_index("ctx") * token_rows
    query_pos = lax.dynamic_slice_in_dim(positions, own_start, token_rows, 0)
    query_doc = lax.dynamic_slice_in_dim(labels, own_start, token_rows, 0)
    attention, query_grad, key_grad, value_grad = attend(
        queries[0], pairs_all, out_grad[0], query_pos, query_doc, positions, labels
    )
    key_grad, value_grad = (
        lax.psum_scatter(
            key_grad.astype(jnp.bfloat16), "ctx", scatter_dimension=0, tiled=True
        ).astype(jnp.float32),
        lax.psum_scatter(
            value_grad.astype(jnp.bfloat16), "ctx", scatter_dimension=0, tiled=True
        ).astype(jnp.float32),
    )
    pair_grad = jnp.concatenate([key_grad, value_grad], axis=1).astype(jnp.bfloat16)
    contract = (((1,), (1,)), ((), ()))
    normed_grad = lax.dot_general(
        pair_grad,
        lax.all_gather(kv_weight, ("dp", "ctx"), axis=0, tiled=True),
        contract,
        preferred_element_type=jnp.float32,
    )
    forward_value, pullback = jax.vjp(lambda values: rms_scale(values, norm_gain), hidden32)
    full_grad = pullback(normed_grad)[0]
    hidden_grad = jnp.where(marked[:, None], jnp.float32(0.0), full_grad).astype(jnp.bfloat16)
    returning = jnp.dot(
        placing.T.astype(jnp.bfloat16),
        full_grad.astype(jnp.bfloat16),
        preferred_element_type=jnp.float32,
    ).astype(jnp.bfloat16)
    returned = lax.all_to_all(returning, ("dp", "ctx"), split_axis=0, concat_axis=0, tiled=True)
    visual_grad = jnp.dot(
        picking.T.astype(jnp.bfloat16), returned, preferred_element_type=jnp.float32
    ).astype(jnp.bfloat16)
    return (attention[None], query_grad[None], hidden_grad[None], visual_grad)


def neighbor(values, axis, offset):
    count = lax.axis_size(axis)
    return lax.ppermute(values, axis, [(d, d ^ offset) for d in range(count)])


def after(values, earlier):
    return lax.optimization_barrier((values, *earlier))[0]


def swap(values):
    return neighbor(values, "core", 1)


def vmem_params(size=16):
    return pltpu.CompilerParams(vmem_limit_bytes=size * 1024 * 1024)


def brief():
    return pl.CostEstimate(flops=1, bytes_accessed=1, transcendentals=0)


def smem():
    return pl.BlockSpec(memory_space=pltpu.SMEM)


def store_halves(core, values, own_ref, other_ref, block):
    def put(own_parity):
        for j in range(values.shape[1] // (2 * block)):
            even = values[:, 2 * j * block : (2 * j + 1) * block]
            odd = values[:, (2 * j + 1) * block : (2 * j + 2) * block]
            own_ref[:, j * block : (j + 1) * block] = odd if own_parity else even
            other_ref[:, j * block : (j + 1) * block] = even if own_parity else odd

    @pl.when(core == 0)
    def _():
        put(0)

    @pl.when(core != 0)
    def _():
        put(1)


def split_halves(values, core, block):
    rows, width = values.shape
    step = 8 * block

    def kernel(core_ref, value_ref, own_ref, other_ref):
        store_halves(core_ref[0], value_ref[...], own_ref, other_ref, block)

    half = jax.ShapeDtypeStruct((rows, width // 2), values.dtype)
    out = pl.BlockSpec((rows, step // 2), lambda j: (0, j))
    return pl.pallas_call(
        kernel,
        grid=(width // step,),
        in_specs=[smem(), pl.BlockSpec((rows, step), lambda j: (0, j))],
        out_specs=[out, out],
        out_shape=[half, half],
        compiler_params=vmem_params(56),
        cost_estimate=brief(),
        name="split_halves",
    )(core, values)


def up_projection(patches, gain, weight):
    rows, depth = patches.shape
    vector = gain.shape[1]
    width = weight.shape[1]
    count = depth // vector

    def kernel(patch_ref, gain_ref, weight_ref, out_ref, buffers, sems):
        copies = [
            pltpu.make_async_copy(weight_ref.at[j * vector : (j + 1) * vector], buffers.at[j], sems.at[j])
            for j in range(count)
        ]
        for copy in copies:
            copy.start()
        total = jnp.zeros((rows, width), jnp.float32)
        for j in range(count):
            center = patch_ref[:, j * vector : (j + 1) * vector].astype(jnp.float32)
            center = center - jnp.mean(center, axis=1, keepdims=True)
            spread = jnp.mean(center * center, axis=1, keepdims=True)
            normed = (center * lax.rsqrt(spread + epsilon) * gain_ref[...]).astype(jnp.bfloat16)
            copies[j].wait()
            total = total + jnp.dot(normed, buffers[j], preferred_element_type=jnp.float32)
        out_ref[...] = (0.5 * total * (1.0 + lax.erf(total * math.sqrt(0.5)))).astype(jnp.bfloat16)

    vmem = pl.BlockSpec(memory_space=pltpu.VMEM)
    return pl.pallas_call(
        kernel,
        in_specs=[vmem, vmem, pl.BlockSpec(memory_space=pl.ANY)],
        out_specs=vmem,
        out_shape=jax.ShapeDtypeStruct((rows, width), jnp.bfloat16),
        scratch_shapes=[
            pltpu.VMEM((count, vector, width), jnp.bfloat16),
            pltpu.SemaphoreType.DMA((count,)),
        ],
        compiler_params=vmem_params(56),
        cost_estimate=brief(),
        name="merge_up",
    )(patches, gain, weight)


def down_halves(inner_hidden, merge_down, core, block):
    rows, depth = inner_hidden.shape
    width = merge_down.shape[1]
    step = 4 * block
    count = width // step

    def kernel(core_ref, hidden_ref, weight_ref, own_ref, other_ref, buffers, sems):
        copies = [
            pltpu.make_async_copy(weight_ref.at[:, j * step : (j + 1) * step], buffers.at[j], sems.at[j])
            for j in range(count)
        ]
        for copy in copies:
            copy.start()
        for j in range(count):
            copies[j].wait()
            product = jnp.dot(hidden_ref[...], buffers[j], preferred_element_type=jnp.float32)
            place = slice(j * step // 2, (j + 1) * step // 2)
            store_halves(
                core_ref[0], product.astype(jnp.bfloat16), own_ref.at[:, place], other_ref.at[:, place], block
            )

    vmem = pl.BlockSpec(memory_space=pltpu.VMEM)
    half = jax.ShapeDtypeStruct((rows, width // 2), jnp.bfloat16)
    return pl.pallas_call(
        kernel,
        in_specs=[smem(), vmem, pl.BlockSpec(memory_space=pl.ANY)],
        out_specs=[vmem, vmem],
        out_shape=[half, half],
        scratch_shapes=[
            pltpu.VMEM((count, depth, step), jnp.bfloat16),
            pltpu.SemaphoreType.DMA((count,)),
        ],
        compiler_params=vmem_params(56),
        cost_estimate=brief(),
        name="merge_down",
    )(core, inner_hidden, merge_down)


def project(table, own_rows, sibling_rows, visual, gain, blocks, first, count, earlier):
    rows = own_rows.shape[0]
    total = 2 * rows + visual.shape[0]
    block, width = blocks[0].shape
    quarter = width // 4
    size = len(blocks)
    last = first + size == count
    flag = table.shape[0] - 1

    def kernel(table_ref, own_ref, sibling_ref, visual_ref, gain_ref, *rest):
        block_refs = rest[:size]
        before_refs = rest[size : size + len(earlier)]
        turned_ref, *outs, turning, sems = rest[size + len(earlier) :]
        total_ref = outs[-1]
        turns = []
        for r in range(size):
            columns = pl.ds(pl.multiple_of(table_ref[first + r] * block, block), block)
            gains = gain_ref[:, columns]
            part = jnp.concatenate(
                [
                    (ref[:, columns].astype(jnp.float32) * gains).astype(jnp.bfloat16)
                    for ref in (own_ref, sibling_ref, visual_ref)
                ],
                axis=0,
            )
            values = block_refs[r][...]
            product = jnp.dot(part, values, preferred_element_type=jnp.float32)
            if r > 0:
                total_ref[...] += product
            elif earlier:
                total_ref[...] = before_refs[0][...] + product
            else:
                total_ref[...] = product
            turning[r] = values.T
            turn = pltpu.make_async_copy(turning.at[r], turned_ref.at[r], sems.at[r])
            turn.start()
            turns.append(turn)
        if last:
            mine_ref, theirs_ref = outs[:2]

            def put(parity):
                for piece in range(2):
                    start = 2 * piece * quarter
                    mine = slice(start + parity * quarter, start + (parity + 1) * quarter)
                    theirs = slice(start + (1 - parity) * quarter, start + (2 - parity) * quarter)
                    place = slice(piece * quarter, (piece + 1) * quarter)
                    mine_ref[:, place] = total_ref[:, mine]
                    theirs_ref[:rows, place] = total_ref[rows : 2 * rows, theirs].astype(jnp.bfloat16)
                    theirs_ref[rows : 2 * rows, place] = total_ref[:rows, theirs].astype(jnp.bfloat16)
                    theirs_ref[2 * rows :, place] = total_ref[2 * rows :, theirs].astype(jnp.bfloat16)

            @pl.when(table_ref[flag] == 0)
            def _():
                put(0)

            @pl.when(table_ref[flag] != 0)
            def _():
                put(1)

        for turn in turns:
            turn.wait()

    vmem = pl.BlockSpec(memory_space=pltpu.VMEM)
    shape = jax.ShapeDtypeStruct
    sums, scratch = [shape((total, width), jnp.float32)], []
    if last:
        sums = [shape((total, width // 2), jnp.float32), shape((total, width // 2), jnp.bfloat16)]
        scratch = [pltpu.VMEM((total, width), jnp.float32)]
    return pl.pallas_call(
        kernel,
        in_specs=[smem()] + [vmem] * (4 + size + len(earlier)),
        out_specs=[pl.BlockSpec(memory_space=pl.ANY)] + [vmem] * len(sums),
        out_shape=[shape((size, width, block), jnp.bfloat16)] + sums,
        scratch_shapes=scratch + [pltpu.VMEM((size, width, block), jnp.bfloat16), pltpu.SemaphoreType.DMA((size,))],
        compiler_params=vmem_params(24 if last else 56),
        cost_estimate=brief(),
        name="project_pairs",
    )(table, own_rows, sibling_rows, visual, gain, *blocks, *earlier)


def finish_pairs(mine, received, scale, codes, picking, rows):
    total, width = mine.shape
    slots, tokens = picking.shape

    def kernel(mine_ref, received_ref, scale_ref, codes_ref, picking_ref, chip_ref, token_ref, slot_ref):
        pairs = (mine_ref[...] + received_ref[...].astype(jnp.float32)) * jnp.broadcast_to(scale_ref[...], (128, total)).T[:, :1]
        pairs = pairs.astype(jnp.bfloat16)
        chip_ref[...] = pairs[: 2 * rows]
        token_ref[...] = pairs[2 * rows :]
        placing = picking_ref[...]
        slot_ref[:, :width] = jnp.dot(
            placing, pairs[2 * rows :], preferred_element_type=jnp.float32
        ).astype(jnp.bfloat16)
        slot_ref[:, width:] = jnp.dot(
            placing, codes_ref[...], preferred_element_type=jnp.float32
        ).astype(jnp.bfloat16)

    shape = jax.ShapeDtypeStruct
    return pl.pallas_call(
        kernel,
        out_shape=[
            shape((2 * rows, width), jnp.bfloat16),
            shape((tokens, width), jnp.bfloat16),
            shape((slots, width + codes.shape[1]), jnp.bfloat16),
        ],
        compiler_params=vmem_params(56),
        cost_estimate=brief(),
        name="finish_pairs",
    )(mine, received, scale, codes, picking)


def sum_grads(core, pair_grad, received, returned, picking, rows):
    width = pair_grad.shape[1]
    tokens = picking.shape[1] // 2

    def kernel(core_ref, grad_ref, returned_ref, picking_ref, *rest):
        held_ref, sent_ref = rest[-2:]
        text = grad_ref[...].astype(jnp.float32)
        for ref in rest[:-2]:
            text = text + ref[...].astype(jnp.float32)
        text = text.astype(jnp.bfloat16)
        held_ref[:rows] = text[:rows]
        sent_ref[:rows] = text[rows:]
        token = lax.dot_general(
            picking_ref[...], returned_ref[...], (((0,), (0,)), ((), ())), preferred_element_type=jnp.float32
        ).astype(jnp.bfloat16)

        @pl.when(core_ref[0] == 0)
        def _():
            held_ref[rows:] = token[:tokens]
            sent_ref[rows:] = token[tokens:]

        @pl.when(core_ref[0] != 0)
        def _():
            held_ref[rows:] = token[tokens:]
            sent_ref[rows:] = token[:tokens]

    def whole(values):
        return pl.BlockSpec(values.shape, lambda j: (0, 0))

    half = jax.ShapeDtypeStruct((rows + tokens, width), jnp.bfloat16)
    return pl.pallas_call(
        kernel,
        grid=(1,),
        in_specs=[smem(), pl.BlockSpec((2 * rows, width), lambda j: (0, 0)), whole(returned), whole(picking)]
        + [whole(part) for part in received],
        out_specs=[whole(jax.ShapeDtypeStruct((rows + tokens, width), jnp.bfloat16))] * 2,
        out_shape=[half, half],
        compiler_params=vmem_params(56),
        cost_estimate=brief(),
        name="sum_grads",
    )(core, pair_grad, returned, picking, *received)


def project_back(table, grads, pairs, turned, text, visual, gain, scale, keep):
    rows, width = text.shape
    tokens = visual[0].shape[0]
    total = rows + tokens
    pair_width, block = turned[0][0].shape[1:]
    quarter = pair_width // 4
    flag = table.shape[0] - 1
    pieces = len(turned[0])
    count = sum(part.shape[0] for part in turned[0])
    groups, first = [], 0
    for piece in range(pieces):
        size = turned[0][piece].shape[0]
        for low in range(0, size, 4):
            high = min(size, low + 4)
            groups.append((piece, low, high, first + low))
        first += size
    groups = groups[-1:] + groups[:-1]

    def kernel(
        table_ref, grad_ref, grad_other_ref, pair_ref, pair_other_ref, text_ref, visual_ref, visual_other_ref,
        gain_ref, scale_ref, keep_ref, *rest,
    ):
        turned_refs, (hidden_ref, token_ref, joined, buffers, sems) = rest[: 2 * pieces], rest[2 * pieces :]
        core = table_ref[flag]
        copies = []
        for at, (piece, low, high, place) in enumerate(groups):
            copies.append(
                [
                    pltpu.make_async_copy(
                        turned_refs[side * pieces + piece].at[low:high],
                        buffers.at[side, place : place + high - low],
                        sems.at[at, side],
                    )
                    for side in range(2)
                ]
            )
        for pair in copies[:2]:
            for copy in pair:
                copy.start()

        def join(parity):
            for piece in range(2):
                place = slice(piece * quarter, (piece + 1) * quarter)
                start = (2 * piece + parity) * quarter
                joined[:, start : start + quarter] = grad_ref[:, place]
                start = (2 * piece + 1 - parity) * quarter
                joined[:, start : start + quarter] = grad_other_ref[:, place]

        @pl.when(core == 0)
        def _():
            join(0)

        @pl.when(core != 0)
        def _():
            join(1)

        inner = jnp.zeros((total, 1), jnp.float32)
        for left, right in ((grad_ref, pair_ref), (grad_other_ref, pair_other_ref)):
            inner = inner + jnp.sum(
                left[...].astype(jnp.float32) * right[...].astype(jnp.float32), axis=1, keepdims=True
            )
        scales = scale_ref[...]
        backs = inner * scales * scales * (1.0 / width)
        keeps = keep_ref[:rows] > 0
        for at, (piece, low, high, first) in enumerate(groups):
            for copy in copies[at]:
                copy.wait()
            if at + 2 < len(groups):
                for copy in copies[at + 2]:
                    copy.start()
            for r in range(first, first + high - low):
                spot = table_ref[r]
                inside = pl.ds(pl.multiple_of(spot * block, block), block)
                for half, (side, token_in) in enumerate(((core, visual_ref), (1 - core, visual_other_ref))):
                    place = pl.ds(pl.multiple_of((2 * spot + side) * block, block), block)
                    normed_grad = jnp.dot(joined[...], buffers[half, r], preferred_element_type=jnp.float32)
                    full = normed_grad * scales * gain_ref[:, place]
                    hidden = full[:rows] - text_ref[:, place].astype(jnp.float32) * backs[:rows]
                    hidden_ref[:, place] = jnp.where(keeps, hidden, 0.0).astype(jnp.bfloat16)
                    token = full[rows:] - token_in[:, inside].astype(jnp.float32) * backs[rows:]
                    token_ref[:, place] = token.astype(jnp.bfloat16)

    vmem = pl.BlockSpec(memory_space=pltpu.VMEM)
    shape = jax.ShapeDtypeStruct
    return pl.pallas_call(
        kernel,
        in_specs=[smem()] + [vmem] * 10 + [pl.BlockSpec(memory_space=pl.ANY)] * (2 * pieces),
        out_specs=[vmem, vmem],
        out_shape=[shape((rows, width), jnp.bfloat16), shape((tokens, width), jnp.bfloat16)],
        scratch_shapes=[
            pltpu.VMEM((total, pair_width), jnp.bfloat16),
            pltpu.VMEM((2, count, pair_width, block), jnp.bfloat16),
            pltpu.SemaphoreType.DMA((len(groups), 2)),
        ],
        compiler_params=vmem_params(56),
        cost_estimate=brief(),
        name="project_back",
    )(table, *grads, *pairs, text, *visual, gain, scale, keep, *turned[0], *turned[1])


def attend_pair(queries, upstream, pair_text, pair_visual, keyed):
    rows, width = queries[0].shape
    length, pair_width = pair_text[0].shape[0] * len(pair_text), pair_text[0].shape[1]
    slots = pair_visual.shape[0]
    own_kv = pair_width // (2 * HD)
    heads = width // HD
    group = heads // own_kv
    step_heads = group
    steps = heads // step_heads
    score_scale = HD ** (-0.5)
    f32, bf16 = jnp.float32, jnp.bfloat16

    def kernel(
        qa, qb, ua, ub, visual_ref, row_s, row_l, pos_ref, doc_ref, qpos_ref, qdoc_ref, *rest,
    ):
        text_refs = rest[: len(pair_text)]
        oa, ob, ga, gb, *grad_refs, grad_visual_ref, keep_ref, heads_ref, turned_ref, bias_ref, total_ref = rest[
            len(pair_text) :
        ]
        step = pl.program_id(0)

        @pl.when(step == 0)
        def _():
            codes = visual_ref[:, pair_width:].astype(f32).T
            placing = jnp.where(row_s[...] == codes[0:1] * 16.0 + codes[1:2], 1.0, 0.0).astype(f32)
            placed = jnp.dot(placing.astype(bf16), visual_ref[:, :pair_width], preferred_element_type=f32)
            marked = jnp.max(placing, axis=1, keepdims=True)
            keep_ref[...] = 1.0 - marked
            texts = jnp.concatenate([ref[...].astype(f32) for ref in text_refs], axis=0)
            pairs = jnp.where(marked > 0, placed, texts)
            for j in range(2 * own_kv):
                piece = pairs[:, j * HD : (j + 1) * HD]
                heads_ref[j] = piece.astype(bf16)
                turned_ref[j] = piece.T.astype(bf16)
            allowed = (pos_ref[...] <= qpos_ref[...]) & (doc_ref[...] == qdoc_ref[...])
            bias_ref[...] = jnp.where(allowed, 0.0, -jnp.inf).astype(f32).T
            total_ref[...] = jnp.zeros_like(total_ref)

        head = (step * step_heads) // group
        keys, values = heads_ref[head], heads_ref[own_kv + head]
        keys_turned, values_turned = turned_ref[head], turned_ref[own_kv + head]
        lights, score_grads, query_list, ups = [], [], [], []
        for h in range(step_heads):
            lanes = slice(h * HD, (h + 1) * HD)
            query = jnp.concatenate([qa[:, lanes], qb[:, lanes]], axis=0)
            up = jnp.concatenate([ua[:, lanes], ub[:, lanes]], axis=0)
            scores = jnp.dot(query, keys_turned, preferred_element_type=f32)
            weight_grad = jnp.dot(up, values_turned, preferred_element_type=f32)
            scores = scores * (score_scale * math.log2(math.e)) + bias_ref[...]
            weights = jnp.exp2(scores - jnp.max(scores, axis=1, keepdims=True))
            weights = weights * (1.0 / jnp.sum(weights, axis=1, keepdims=True))
            light = weights.astype(bf16)
            inner = jnp.sum(weights * weight_grad, axis=1, keepdims=True)
            score_grad = (weights * (weight_grad - inner)).astype(bf16)
            output = jnp.dot(light, values, preferred_element_type=f32).astype(bf16)
            oa[:, lanes] = output[:rows]
            ob[:, lanes] = output[rows:]
            query_grad = (jnp.dot(score_grad, keys, preferred_element_type=f32) * score_scale).astype(bf16)
            ga[:, lanes] = query_grad[:rows]
            gb[:, lanes] = query_grad[rows:]
            lights.append(light)
            score_grads.append(score_grad)
            query_list.append(query)
            ups.append(up)
        up, light = jnp.concatenate(ups, axis=0).T, jnp.concatenate(lights, axis=0)
        total_ref[own_kv + head] += jnp.dot(up, light, preferred_element_type=f32)
        query, score_grad = jnp.concatenate(query_list, axis=0).T, jnp.concatenate(score_grads, axis=0)
        total_ref[head] += jnp.dot(query, score_grad, preferred_element_type=f32) * score_scale

        @pl.when(step == steps - 1)
        def _():
            codes = visual_ref[:, pair_width : pair_width + 2].astype(f32)
            lifting = jnp.where(codes[:, 0:1] * 16.0 + codes[:, 1:2] == row_l[...], 1.0, 0.0).astype(bf16)
            for j in range(2 * own_kv):
                piece = total_ref[j].T.astype(bf16)
                place = slice(j * HD, (j + 1) * HD)
                for i, ref in enumerate(grad_refs):
                    ref[:, place] = piece[i * ref.shape[0] : (i + 1) * ref.shape[0]]
                grad_visual_ref[:, place] = jnp.dot(lifting, piece, preferred_element_type=f32).astype(bf16)

    part = pl.BlockSpec((rows, step_heads * HD), lambda j: (0, j))
    vmem = pl.BlockSpec(memory_space=pltpu.VMEM)
    shape = jax.ShapeDtypeStruct
    return pl.pallas_call(
        kernel,
        grid=(steps,),
        in_specs=[part] * 4 + [vmem] * (7 + len(pair_text)),
        out_specs=[part] * 4 + [vmem] * (2 + len(pair_text)),
        out_shape=[shape((rows, width), bf16)] * 4
        + [shape(x.shape, bf16) for x in pair_text]
        + [shape((slots, pair_width), bf16), shape((length, 1), f32)],
        scratch_shapes=[
            pltpu.VMEM((2 * own_kv, length, HD), bf16),
            pltpu.VMEM((2 * own_kv, HD, length), bf16),
            pltpu.VMEM((2 * rows, length), f32),
            pltpu.VMEM((2 * own_kv, HD, length), f32),
        ],
        compiler_params=vmem_params(56),
        cost_estimate=brief(),
        name="attend",
    )(
        *queries,
        *upstream,
        pair_visual,
        *keyed,
        *pair_text,
    )


def local_fast(
    patches, vit_gain, merge_up, merge_down, dest, text, norm_gain, kv_weight, queries, out_grad, assign, docs
):
    f32, bf16 = jnp.float32, jnp.bfloat16
    data_count, column_count = lax.axis_size("dp"), lax.axis_size("y")
    ctx_count = 2 * column_count
    data, column, core = lax.axis_index("dp"), lax.axis_index("y"), lax.axis_index("core")
    rows, width = text.shape[1], text.shape[2]
    tokens = dest.shape[0]
    block = kv_weight.shape[0]
    length = rows * ctx_count
    core_word = core[None].astype(jnp.int32)

    def line(values, pairs):
        return lax.ppermute(values, "dp", [(2 * p + low, 2 * q + low) for p, q in pairs for low in range(2)])

    def both(values):
        return neighbor(values, "dp", 1), neighbor(values, "y", 1)

    close = lax.optimization_barrier
    swapped = [(0, 1), (1, 0), (2, 3), (3, 2)]
    middle, outward = [(1, 2), (2, 1)], [(1, 0), (2, 3)]
    far_index = data // 2
    is_middle = (far_index == 1) | (far_index == 2)
    hops = [0, 1, jnp.where(is_middle, 3, 2), jnp.where(is_middle, 2, 3)]
    owners = [
        ((far_index ^ hops[i + j]) * 2 + ((data % 2) ^ along)) * column_count + (column ^ down)
        for i in (0, 2)
        for along, down in ((0, 0), (1, 0), (0, 1), (1, 1))
        for j in range(2)
    ]
    table = jnp.stack(owners + [core]).astype(jnp.int32)
    gain = lax.dynamic_index_in_dim(
        norm_gain.reshape(-1, 2, block), core, axis=1, keepdims=False
    ).reshape(1, width // 2)
    query_width = queries.shape[2] // 2
    chip_tokens = 2 * tokens

    beside0, below0 = both(kv_weight)
    far1, across = line(kv_weight, swapped), line(kv_weight, middle)
    inner_hidden = up_projection(patches, vit_gain[None, :], merge_up)
    rows_in = text[0]
    inner_hidden, rows_in, core_word, table, gain, far1, across, beside0, below0 = close(
        (inner_hidden, rows_in, core_word, table, gain, far1, across, beside0, below0)
    )

    beside1, below1 = both(far1)
    across2, ends1 = line(far1, middle), line(across, outward)
    merged, merged_other = down_halves(inner_hidden, merge_down, core_word, block)
    merged, merged_other, rows_in, core_word, ends1, across2, below1, beside1 = close(
        (merged, merged_other, rows_in, core_word, ends1, across2, below1, beside1)
    )

    corner0, corner1 = neighbor(beside0, "y", 1), neighbor(below1, "dp", 1)
    ends2 = line(across2, outward)
    arriving = swap(merged_other)
    own_rows, other_part = split_halves(rows_in, core_word, block)
    sibling_rows = swap(other_part)
    far2 = jnp.where(is_middle, across, ends1)
    merged = (merged.astype(f32) + arriving.astype(f32)).astype(bf16)
    visual32 = lax.dynamic_slice_in_dim(merged, column * chip_tokens, chip_tokens, 0)
    leaving = lax.dynamic_slice_in_dim(merged, (column ^ 1) * chip_tokens, chip_tokens, 0)
    summing = neighbor(leaving, "y", 1)
    query_in, upstream_in = queries[0], out_grad[0]
    corner0, corner1, ends2, own_rows, sibling_rows, far2, visual32, summing = close(
        (corner0, corner1, ends2, own_rows, sibling_rows, far2, visual32, summing)
    )
    query_in, upstream_in, dest, assign, docs, ends2 = close((query_in, upstream_in, dest, assign, docs, ends2))

    def heads_of(values):
        mine = lax.dynamic_slice_in_dim(values, core * query_width, query_width, 1)
        theirs = lax.dynamic_slice_in_dim(values, (1 - core) * query_width, query_width, 1)
        return mine, theirs

    beside2, below2 = both(far2)
    far3 = jnp.where(is_middle, across2, ends2)
    query_parts, upstream_parts = heads_of(query_in), heads_of(upstream_in)
    query_parts = (query_parts[0], swap(query_parts[1]))
    upstream_parts = (upstream_parts[0], swap(upstream_parts[1]))

    def squares(values):
        values = values.astype(f32)
        return jnp.sum(values * values, axis=1)

    own_squares, sibling_squares = squares(own_rows), squares(sibling_rows)

    dest_other = swap(dest)
    chip_dest = jnp.where(
        core == 0, jnp.concatenate([dest, dest_other]), jnp.concatenate([dest_other, dest])
    )
    token_core = jnp.arange(chip_tokens, dtype=jnp.int32) // tokens
    sequence, row_of = chip_dest // length, chip_dest % length
    slot = token_core * ctx_count + row_of // rows
    slot_total = data_count * column_count * 2 * ctx_count
    slot_index = jnp.arange(slot_total, dtype=jnp.int32)[:, None]
    picking = (slot_index // (column_count * 2 * ctx_count) == sequence[None, :]) & (
        slot_index % (2 * ctx_count) == slot[None, :]
    )
    picking = picking.astype(bf16)
    lane = jnp.arange(128, dtype=jnp.int32)[None, :]
    code = row_of[:, None] + 1
    codes = jnp.where(lane == 0, code // 16, jnp.where(lane == 1, code % 16, 0)).astype(bf16)

    def between_chips(values):
        shaped = values.reshape(data_count * column_count, 2 * ctx_count, -1)
        moved = lax.all_to_all(shaped, ("dp", "y"), split_axis=0, concat_axis=0, tiled=True)
        return moved.reshape(values.shape)

    halves = rows // 2
    positions = (assign[:, None] * halves + jnp.arange(halves, dtype=jnp.int32)[None, :]).reshape(length)
    labels = docs[0].reshape(-1, halves)[assign].reshape(length)
    order = jnp.stack(
        [2 * (column ^ down) + (core ^ side) for down in range(column_count) for side in range(2)]
    )
    key_row = (order[:, None] * rows + jnp.arange(rows, dtype=jnp.int32)[None, :]).reshape(length)
    key_pos = positions.reshape(ctx_count, rows)[order].reshape(length)
    key_doc = labels.reshape(ctx_count, rows)[order].reshape(length)
    key_row = key_row.astype(f32) + 1.0
    keyed = (key_row[:, None], key_row[None, :], key_pos[:, None], key_doc[:, None])
    keyed += (key_pos[None, : 2 * rows], key_doc[None, : 2 * rows])

    def of_core(values, which):
        return lax.dynamic_slice_in_dim(values, which * tokens, tokens, 0)

    beside2, below2, far3, summing, query_parts, upstream_parts, keyed, picking, codes, own_squares, sibling_squares = close(
        (beside2, below2, far3, summing, query_parts, upstream_parts, keyed, picking, codes, own_squares, sibling_squares)
    )

    beside3, below3 = both(far3)
    visual = (visual32.astype(f32) + summing.astype(f32)).astype(bf16)
    blocks = [kv_weight, far1, beside0, beside1, below0, below1, corner0, corner1]
    part0, sums = project(table, own_rows, sibling_rows, visual, gain, blocks, 0, 16, ())
    beside3, below3, part0, sums, visual = close((beside3, below3, part0, sums, visual))

    corner2, corner3 = neighbor(beside2, "y", 1), neighbor(below3, "dp", 1)
    other0 = swap(part0)
    blocks = [far2, far3, beside2, beside3, below2, below3]
    part1, sums = project(table, own_rows, sibling_rows, visual, gain, blocks, 8, 16, (sums,))
    visual_squares = squares(visual)
    arrived = swap(jnp.concatenate([sibling_squares, own_squares, visual_squares]))
    square = jnp.concatenate([own_squares, sibling_squares, visual_squares]) + arrived
    scale = lax.rsqrt(square / width + epsilon)[:, None]
    wide_scale = scale.reshape(1, -1)
    own_visual, other_visual = of_core(visual, core), swap(of_core(visual, 1 - core))
    own_scale = jnp.concatenate([scale[:rows], of_core(scale[2 * rows :], core)], axis=0)
    corner2, corner3, part1, sums, other0, wide_scale, own_visual, other_visual, own_scale = close(
        (corner2, corner3, part1, sums, other0, wide_scale, own_visual, other_visual, own_scale)
    )
    part2, *sums = project(table, own_rows, sibling_rows, visual, gain, [corner2, corner3], 14, 16, (sums,))
    turned, turned_other = [part0, part1, part2], [other0]
    mine, theirs = sums
    received = swap(theirs)
    pair_chip, pair_tokens, leaving = finish_pairs(mine, received, wide_scale, codes, picking, rows)
    pair_text = [pair_chip] + [neighbor(pair_chip, "y", down) for down in range(1, column_count)]
    pair_visual = between_chips(leaving)
    turned_other += [swap(after(part, (received,))) for part in turned[1:]]

    own_pairs = jnp.concatenate([pair_chip[:rows], of_core(pair_tokens, core)], axis=0)
    other_pairs = swap(jnp.concatenate([pair_chip[rows:], of_core(pair_tokens, 1 - core)], axis=0))

    pair_text[0] = after(pair_text[0], (own_pairs, other_pairs, turned_other))
    out_a, out_b, grad_a, grad_b, pair_grad, *far_grads, visual_pair_grad, keep = attend_pair(
        query_parts, upstream_parts, pair_text, pair_visual, keyed
    )

    def heads_back(held, leaving):
        arrived = swap(leaving)
        return jnp.where(
            core == 0, jnp.concatenate([held, arrived], axis=1), jnp.concatenate([arrived, held], axis=1)
        )

    received = [neighbor(part, "y", down) for down, part in enumerate(far_grads, 1)]
    returned = between_chips(visual_pair_grad)
    attention, query_grad = heads_back(out_a, out_b), heads_back(grad_a, grad_b)
    pair_grad, attention, query_grad = close((pair_grad, attention, query_grad))
    held, leaving = sum_grads(core_word, pair_grad, received, returned, picking, rows)
    hidden_grad, visual_grad = project_back(
        table, (held, swap(leaving)), (own_pairs, other_pairs), (turned, turned_other), text[0],
        (own_visual, other_visual), norm_gain[None, :], own_scale, keep,
    )
    return (attention[None], query_grad[None], hidden_grad[None], visual_grad)


def solution(mesh):
    data_count, ctx_count = mesh.shape["dp"], mesh.shape["ctx"]
    split = Mesh(mesh.devices.reshape(data_count, -1, 2), ("dp", "y", "core"))

    def call(*arrays):
        text, kv_weight, dest = arrays[5], arrays[7], arrays[4]
        devices = data_count * ctx_count
        rows = text.shape[1] // ctx_count
        fits = (
            ctx_count == 4
            and data_count == 8
            and (kv_weight.shape[0] // devices) % 128 == 0
            and dest.shape[0] // devices <= devices
            and rows % 128 == 0
        )
        if fits:
            whole, ctx, body, used = ("dp", "y", "core"), ("y", "core"), local_fast, split
        else:
            whole, ctx, body, used = ("dp", "ctx"), "ctx", local, mesh
        placed = (
            P("dp", None),
            P(),
            P(None, ctx),
            P(ctx, None),
            P(whole),
            P("dp", ctx, None),
            P(),
            P(whole, None),
            P("dp", ctx, None),
            P("dp", ctx, None),
            P(),
            P("dp", None),
        )
        return jax.shard_map(
            body,
            mesh=used,
            in_specs=placed,
            out_specs=(P("dp", ctx, None), P("dp", ctx, None), P("dp", ctx, None), P(whole, None)),
            check_vma=False,
        )(*arrays)

    return call
```
